128 devices in a mesh: pool: 4 (over y), fft: 32 (over z, x, core).
Axes of the slice: x: 4, y: 4, z: 4, core: 2. Of those that a mesh axis runs over, the one named last changes fastest.
Arguments:
- wave_coeff: float32 [4, 2, 2, 128, 128, 128], P('pool', None, None, None, 'fft'), may hold values from -16384 to 16384, as said below
- band_energy: float32 [4, 2], P('pool'), may hold values from -1 to -0.25
- local_potential: float32 [128, 128, 128], P('fft'), may hold values from 0 to 1
- perturbation: float32 [128, 128, 128], P('fft'), may hold values from -6 to 6
- xc_kernel: float32 [128, 128, 128], P('fft'), may hold values from -2 to -0.5
Outputs:
- response_coeff: float32 [4, 2, 2, 128, 128, 128], P('pool', None, None, None, 'fft')
- response_density: float32 [128, 128, 128], P('fft')
- hxc_potential: float32 [128, 128, 128], P('fft')
The draws below stay inside these ranges and needn't reach their ends.
Inputs may be any that keep to these rules, and one draw needn't show every extreme that they name: `wave_coeff`: each band has <psi|psi> = 1.
All inputs are finite; a program needn't handle non-finite values.
Results may differ from the reference program's by a relative error of at most 0.0003.
Values sent between devices are 32-bit elements; how exact they have to be, the bound alone decides.
A program may use at most 128 MiB of HBM per device.

```python
import math
import jax
import jax.numpy as jnp
from jax import lax

NX = 128
NY = 128
NZ = 128
NB = 2
CG_STEPS = 3
KPTS = 4


cell_length = 51.3


def squared_wavenumbers(length):
    position = jnp.arange(length, dtype=jnp.int32)
    signed = jnp.where(2 * position >= length, position - length, position).astype(jnp.float32)
    return (signed * (2.0 * math.pi / cell_length)) ** 2


def draw_wave_coeff(key, part):
    key = jax.random.fold_in(key, 11)
    noise = jax.random.normal(key, (KPTS, NB, 2, NX, NY, NZ), jnp.float32)
    noise = jnp.clip(noise, -6.0, 6.0)
    kinetic = 0.5 * (squared_wavenumbers(NX)[:, None, None] + squared_wavenumbers(NY)[None, :, None] + squared_wavenumbers(NZ)[None, None, :])
    envelope = 1.0 / (1.0 + kinetic) ** 2
    shaped = noise * envelope
    squares = jnp.sum(shaped * shaped, axis=(2, 3, 4, 5), keepdims=True)
    return shaped * jnp.sqrt(float(NX * NY * NZ) / squares)


def steps_of(key, dims, split, smallest, largest):
    def one(dim, blocks):
        heights = jax.random.uniform(jax.random.fold_in(jax.random.fold_in(key, 6), dim), (blocks,), jnp.float32, smallest / len(split), largest / len(split))
        return jnp.repeat(jnp.exp(heights), dims[dim] // blocks).reshape((-1,) + (1,) * (len(dims) - dim - 1))

    level = one(*split[0])
    for cut in split[1:]:
        level = level * one(*cut)
    return level


def normal_values(rng, extent, scale, limit, cuts=(), kind=jnp.bfloat16):
    result = jax.random.normal(rng, extent, jnp.float32) * scale
    if len(cuts) > 0:
        result = steps_of(rng, extent, cuts, -0.22, 0.18) * result
    return jnp.clip(result, min=-limit, max=limit).astype(kind)


def setup_inputs(seed: int = 0) -> dict:
    keys = jax.random.split(jax.random.key(seed), 6)
    wave_coeff = draw_wave_coeff(jax.random.fold_in(keys[5], 71), 0)
    band_energy = jnp.clip(-1.0 + 0.75 * jax.random.uniform(keys[1], (KPTS, NB), jnp.float32) ** steps_of(keys[1], (KPTS, NB), ((0, 4),), -0.2, 0.2), -1.0, -0.25)
    local_potential = jnp.clip(1.0 * jax.random.uniform(keys[2], (NX, NY, NZ), jnp.float32) ** steps_of(keys[2], (NX, NY, NZ), ((0, 32),), -0.2, 0.2), 0.0, 1.0)
    perturbation = normal_values(keys[3], (NX, NY, NZ), 1.0, 6.0, ((0, 32),), jnp.float32)
    xc_kernel = jnp.clip(-2.0 + 1.5 * jax.random.uniform(keys[4], (NX, NY, NZ), jnp.float32) ** steps_of(keys[4], (NX, NY, NZ), ((0, 32),), -0.2, 0.2), -2.0, -0.5)
    return dict(wave_coeff=wave_coeff, band_energy=band_energy, local_potential=local_potential, perturbation=perturbation, xc_kernel=xc_kernel)


cell_length = 51.3
projector_shift = 2.0
precondition_shift = 1.0
highest = lax.Precision.HIGHEST


def wavenumbers(length):
    position = jnp.arange(length, dtype=jnp.int32)
    signed = jnp.where(2 * position >= length, position - length, position)
    return signed.astype(jnp.float32) * (2.0 * math.pi / cell_length)


def point_offset(point, axis_number):
    bit_value = (point // (2 ** axis_number)) % 2
    return (0.5 * bit_value.astype(jnp.float32) - 0.25) * (2.0 * math.pi / cell_length)


def kinetic_grid():
    along_x = wavenumbers(NX) ** 2
    along_y = wavenumbers(NY) ** 2
    along_z = wavenumbers(NZ) ** 2
    return 0.5 * (along_x[:, None, None] + along_y[None, :, None] + along_z[None, None, :])


def kinetic_point(point):
    along_x = (wavenumbers(NX) + point_offset(point, 0)) ** 2
    along_y = (wavenumbers(NY) + point_offset(point, 1)) ** 2
    along_z = (wavenumbers(NZ) + point_offset(point, 2)) ** 2
    return 0.5 * (along_x[:, None, None] + along_y[None, :, None] + along_z[None, None, :])


def forward_fft(real_part, imag_part):
    spectrum = jnp.fft.fftn(lax.complex(real_part, imag_part), axes=(-3, -2, -1))
    return jnp.real(spectrum), jnp.imag(spectrum)


def inverse_fft(real_part, imag_part):
    spectrum = jnp.fft.ifftn(lax.complex(real_part, imag_part), axes=(-3, -2, -1))
    return jnp.real(spectrum), jnp.imag(spectrum)


def band_products(wave_real, wave_imag, field_real, field_imag):
    length = wave_real.shape[0]
    factor = 1.0 / (NX * NY * NZ)
    left_real = wave_real.reshape(length, -1)
    left_imag = wave_imag.reshape(length, -1)
    right_real = field_real.reshape(length, -1)
    right_imag = field_imag.reshape(length, -1)
    prod_real = jnp.dot(left_real, right_real.T, precision=highest, preferred_element_type=jnp.float32)
    prod_real = prod_real + jnp.dot(left_imag, right_imag.T, precision=highest, preferred_element_type=jnp.float32)
    prod_imag = jnp.dot(left_real, right_imag.T, precision=highest, preferred_element_type=jnp.float32)
    prod_imag = prod_imag - jnp.dot(left_imag, right_real.T, precision=highest, preferred_element_type=jnp.float32)
    return prod_real * factor, prod_imag * factor


def project(wave_real, wave_imag, prod_real, prod_imag):
    shape_full = wave_real.shape
    flat_real = wave_real.reshape(shape_full[0], -1)
    flat_imag = wave_imag.reshape(shape_full[0], -1)
    out_real = jnp.dot(prod_real.T, flat_real, precision=highest, preferred_element_type=jnp.float32)
    out_real = out_real - jnp.dot(prod_imag.T, flat_imag, precision=highest, preferred_element_type=jnp.float32)
    out_imag = jnp.dot(prod_imag.T, flat_real, precision=highest, preferred_element_type=jnp.float32)
    out_imag = out_imag + jnp.dot(prod_real.T, flat_imag, precision=highest, preferred_element_type=jnp.float32)
    return out_real.reshape(shape_full), out_imag.reshape(shape_full)


def real_inner(left_real, left_imag, right_real, right_imag):
    return jnp.sum(left_real * right_real + left_imag * right_imag, axis=(1, 2, 3)) / (NX * NY * NZ)


def spread(values):
    return values[:, None, None, None]


def solve_point(wave, energy, point, local_potential, perturbation):
    kinetic = kinetic_point(point)
    wave_real = wave[:, 0]
    wave_imag = wave[:, 1]
    space_real, space_imag = inverse_fft(wave_real, wave_imag)
    mixed_real, mixed_imag = forward_fft(perturbation * space_real, perturbation * space_imag)
    prod_real, prod_imag = band_products(wave_real, wave_imag, mixed_real, mixed_imag)
    proj_real, proj_imag = project(wave_real, wave_imag, prod_real, prod_imag)
    resid_real = proj_real - mixed_real
    resid_imag = proj_imag - mixed_imag
    shifted = kinetic[None] - spread(energy)
    precond = 1.0 / (kinetic + precondition_shift)

    def operate(search_real, search_imag):
        field_real, field_imag = inverse_fft(search_real, search_imag)
        pot_real, pot_imag = forward_fft(local_potential * field_real, local_potential * field_imag)
        inner_real, inner_imag = band_products(wave_real, wave_imag, search_real, search_imag)
        back_real, back_imag = project(wave_real, wave_imag, inner_real, inner_imag)
        image_real = shifted * search_real + pot_real + projector_shift * back_real
        image_imag = shifted * search_imag + pot_imag + projector_shift * back_imag
        return image_real, image_imag

    solution_real = jnp.zeros_like(resid_real)
    solution_imag = jnp.zeros_like(resid_imag)
    step_real = precond * resid_real
    step_imag = precond * resid_imag
    search_real, search_imag = step_real, step_imag
    residual_dot = real_inner(resid_real, resid_imag, step_real, step_imag)
    for iteration in range(CG_STEPS):
        image_real, image_imag = operate(search_real, search_imag)
        step_size = residual_dot / real_inner(search_real, search_imag, image_real, image_imag)
        solution_real = solution_real + spread(step_size) * search_real
        solution_imag = solution_imag + spread(step_size) * search_imag
        resid_real = resid_real - spread(step_size) * image_real
        resid_imag = resid_imag - spread(step_size) * image_imag
        if iteration + 1 < CG_STEPS:
            step_real = precond * resid_real
            step_imag = precond * resid_imag
            dot_new = real_inner(resid_real, resid_imag, step_real, step_imag)
            ratio = dot_new / residual_dot
            search_real = step_real + spread(ratio) * search_real
            search_imag = step_imag + spread(ratio) * search_imag
            residual_dot = dot_new
    response_real, response_imag = inverse_fft(solution_real, solution_imag)
    density_term = 2.0 * (NX * NY * NZ) * jnp.sum(space_real * response_real + space_imag * response_imag, axis=0)
    return jnp.stack([solution_real, solution_imag], axis=1), density_term


def reference(wave_coeff, band_energy, local_potential, perturbation, xc_kernel):
    kinetic = kinetic_grid()
    points = jnp.arange(wave_coeff.shape[0], dtype=jnp.int32)

    def per_point(inputs):
        return solve_point(inputs[0], inputs[1], inputs[2], local_potential, perturbation)

    response_coeff, density_terms = lax.map(per_point, (wave_coeff, band_energy, points))
    response_density = jnp.sum(density_terms, axis=0)
    squared = 2.0 * kinetic
    nonzero = (squared > 0).astype(squared.dtype)
    coulomb = 4.0 * math.pi * nonzero / (squared + (1.0 - nonzero))
    hart_real, hart_imag = forward_fft(response_density, jnp.zeros_like(response_density))
    back_real, back_imag = inverse_fft(coulomb * hart_real, coulomb * hart_imag)
    hxc_potential = back_real + xc_kernel * response_density
    return response_coeff, response_density, hxc_potential
```

```python
import functools
import math

import jax
import jax.numpy as jnp
import ml_dtypes
import numpy as np
from jax import lax
from jax.experimental import pallas as pl
from jax.experimental.pallas import tpu as pltpu
from jax.sharding import PartitionSpec as P

CG_STEPS = 3
BANDS = 2
cell_length = 51.3
unit = 2.0 * math.pi / cell_length
MESH = pl.DeviceIdType.MESH
f32 = jnp.float32
bf16 = jnp.bfloat16


def left_table(rows, cols, n, sign, scale=1.0):
    rows, cols = np.array(rows), np.array(cols)
    phase = 2.0 * np.pi * ((rows[:, None, 1] * cols[None, :, 1]) % n) / n
    out_part, in_part = rows[:, None, 0], cols[None, :, 0]
    value = np.where(
        out_part == in_part,
        np.cos(phase),
        np.where(out_part == 1, sign, -sign) * np.sin(phase),
    )
    return value * scale


def split_table(table, axis):
    high = table.astype(ml_dtypes.bfloat16)
    low = (table - high.astype(np.float64)).astype(ml_dtypes.bfloat16)
    return np.concatenate([high, high, low], axis=axis)


def real_basis(n, order):
    k = np.array([f for f, _ in order])
    phase = 2.0 * np.pi * ((k[:, None] * np.arange(n)[None, :]) % n) / n
    is_sin = np.array([s for _, s in order])[:, None]
    rows = np.where(is_sin == 1, np.sin(phase), np.cos(phase))
    weight = np.where((k == 0) | (2 * k == n), 1.0, 2.0)[:, None] / n
    return rows, rows * weight


def make_tables(n, parts):
    local = n // parts
    natural = [(c, j) for c in range(2) for j in range(n)]
    by_owner = [(c, q * local + m) for q in range(parts) for c in range(2) for m in range(local)]
    by_local = [(c, q * local + m) for c in range(2) for m in range(local) for q in range(parts)]
    scale = 1.0 / n**3
    left = np.stack(
        [
            split_table(left_table(by_owner, natural, n, 1.0), 1),
            split_table(left_table(natural, by_local, n, 1.0, scale), 1),
            split_table(left_table(by_owner, natural, n, -1.0), 1),
            split_table(left_table(natural, by_local, n, -1.0), 1),
        ]
    )
    right = np.stack(
        [
            split_table(left_table(natural, natural, n, 1.0).T, 0),
            split_table(left_table(natural, natural, n, -1.0).T, 0),
        ]
    )
    half = n // 2
    plain = [(k, 0) for k in range(half + 1)] + [(k, 1) for k in range(1, half)]
    columns = [
        [(2 * p, 0) for p in range(parts)],
        [(half, 0)] + [(2 * p, 1) for p in range(1, parts)],
        [(2 * p + 1, 0) for p in range(parts)],
        [(2 * p + 1, 1) for p in range(parts)],
    ]
    y_rows, y_back = real_basis(n, sum(columns, []))
    rows, back = real_basis(n, plain)
    by_local_x = [q * local + m for m in range(local) for q in range(parts)]
    x_rows = rows[:, by_local_x]
    x_back = np.zeros((parts, 2 * local, n))
    x_back[:, :local] = back.T.reshape(parts, local, n)
    real = [y_rows, y_back.T, x_rows, x_back.reshape(2 * n, n), rows.T, back]
    return left, right, [np.asarray(t, np.float32) for t in real]


def exact_dot(a, b):
    return jnp.dot(a, b, precision=lax.Precision.HIGHEST, preferred_element_type=f32)


def halves(value):
    high = value.astype(bf16)
    low = (value - high.astype(f32)).astype(bf16)
    return high, low


def left_dot(table, data):
    high, low = halves(data)
    return jnp.dot(table, jnp.concatenate([high, low, high], axis=0), preferred_element_type=f32)


def right_dot(data, table):
    high, low = halves(data)
    return jnp.dot(jnp.concatenate([high, low, high], axis=1), table, preferred_element_type=f32)


def kernel(
    n,
    parts,
    pools,
    wave,
    energy,
    potential,
    perturbation,
    xc,
    left,
    right,
    y_rows,
    y_back,
    x_rows,
    x_back,
    z_rows,
    z_back,
    coeff,
    density,
    hxc,
    kin,
    pre,
    resid,
    search,
    space_wave,
    space_search,
    overlap,
    total,
    send,
    recv,
    small_send,
    small_recv,
    pool_send,
    pool_recv,
    pool_dens,
    pool_hart,
    own_dens,
    own_hart,
    go_send,
    go_recv,
    back_send,
    back_recv,
    bulk_out,
    bulk_in,
    small_out,
    small_in,
    pool_out,
    pool_in,
    turn_out,
    turn_in,
):
    local = n // parts
    block = 2 * local * local
    grid_total = n**3
    inverse_total = 1.0 / grid_total
    me = lax.axis_index("fft")
    pool = lax.axis_index("pool")

    def lanes(value, index):
        return value[:, index * n : (index + 1) * n]

    def peer(index):
        return lax.rem(me + index, parts)

    def pool_peer(index):
        return lax.rem(pool + index, pools)

    barrier = pltpu.get_barrier_semaphore()

    def greet(index, _):
        pl.semaphore_signal(barrier, inc=1, device_id={"fft": peer(index)}, device_id_type=MESH)
        return 0

    def greet_pool(index, _):
        pl.semaphore_signal(
            barrier, inc=1, device_id={"pool": pool_peer(index)}, device_id_type=MESH
        )
        return 0

    lax.fori_loop(1, parts, greet, 0)
    lax.fori_loop(1, pools, greet_pool, 0)
    pl.semaphore_wait(barrier, parts + pools - 2)


    def send_bulk(phase, band, value):
        for m in range(local):
            send[phase, band, :, 2 * local * m : 2 * local * (m + 1), :] = lanes(value, m).reshape(
                parts, 2 * local, n
            )
        here = pl.multiple_of(me * block, block)
        recv[phase, band, pl.ds(here, block), :] = send[phase, band, me]

        def start(index, _):
            target = peer(index)
            pltpu.make_async_remote_copy(
                src_ref=send.at[phase, band, target],
                dst_ref=recv.at[phase, band, pl.ds(here, block)],
                send_sem=bulk_out.at[phase, band],
                recv_sem=bulk_in.at[phase, band],
                device_id={"fft": target},
                device_id_type=MESH,
            ).start()
            return 0

        lax.fori_loop(1, parts, start, 0)

    def wait_bytes(ref, sem):
        pltpu.make_async_copy(ref, ref, sem).wait()

    def receive_bulk(phase, band):
        wait_bytes(recv.at[phase, band, pl.ds(0, block * (parts - 1))], bulk_in.at[phase, band])
        rows = []
        for c in range(2):
            for m in range(local):
                pieces = []
                for other in range(local):
                    first = 2 * local * m + local * c + other
                    pieces.append(recv[phase, band, pl.ds(first, parts, stride=block), :])
                rows.append(jnp.concatenate(pieces, axis=1))
        return jnp.concatenate(rows, axis=0)

    row_id = lax.broadcasted_iota(jnp.int32, (8, n), 0)
    lane_id = lax.broadcasted_iota(jnp.int32, (8, n), 1)

    def lane_sums(value):
        column = jnp.sum(value, axis=0, keepdims=True)
        result = lanes(column, 0)
        for m in range(1, local):
            result = result + lanes(column, m)
        return result

    def send_small(slot, values):
        stacked = jnp.zeros((8, n), f32)
        for i, value in enumerate(values):
            stacked = jnp.where(row_id == i, value, stacked)
        sums = jnp.sum(stacked, axis=1, keepdims=True)
        row = jnp.sum(jnp.where(row_id == lane_id, sums, 0.0), axis=0, keepdims=True)
        small_send[slot] = row
        small_recv[slot, me] = row

        def start(index, _):
            target = peer(index)
            pltpu.make_async_remote_copy(
                src_ref=small_send.at[slot],
                dst_ref=small_recv.at[slot, me],
                send_sem=small_out.at[slot],
                recv_sem=small_in.at[slot],
                device_id={"fft": target},
                device_id_type=MESH,
            ).start()
            return 0

        lax.fori_loop(1, parts, start, 0)

    def receive_small(slot, count):
        wait_bytes(small_recv.at[slot, pl.ds(0, parts - 1)], small_in.at[slot])
        row = jnp.sum(small_recv[slot], axis=0)
        return [
            jnp.sum(jnp.where(lane_id[:1] == i, row, 0.0), axis=1, keepdims=True)
            for i in range(count)
        ]


    def along_z(real, imag, table):
        rows = jnp.concatenate(
            [jnp.concatenate([lanes(real, m), lanes(imag, m)], axis=1) for m in range(local)],
            axis=0,
        )
        out = right_dot(rows, table)
        picked = [out[m * n : (m + 1) * n] for m in range(local)]
        return (
            jnp.concatenate([lanes(v, 0) for v in picked], axis=1),
            jnp.concatenate([lanes(v, 1) for v in picked], axis=1),
        )

    def send_real(phase, band, real, imag):
        real, imag = along_z(real, imag, right[0])
        send_bulk(phase, band, left_dot(left[0], jnp.concatenate([real, imag], axis=0)))

    def receive_real(phase, band):
        out = left_dot(left[1], receive_bulk(phase, band))
        return out[:n], out[n:]

    def send_reciprocal(phase, band, real, imag):
        send_bulk(phase, band, left_dot(left[2], jnp.concatenate([real, imag], axis=0)))

    def receive_reciprocal(phase, band):
        out = left_dot(left[3], receive_bulk(phase, band))
        return along_z(out[:n], out[n:], right[1])


    for band in range(BANDS):
        send_real(0, band, wave[band, 0], wave[band, 1])

    def wavenumber(index):
        signed = jnp.where(2 * index >= n, index - n, index)
        return signed.astype(f32) * unit

    def offset(axis_number):
        bit = lax.rem(pool // 2**axis_number, 2)
        return (0.5 * bit.astype(f32) - 0.25) * unit

    index_x = lax.broadcasted_iota(jnp.int32, (n, n), 0)
    index_z = lax.broadcasted_iota(jnp.int32, (n, n), 1)
    square_x = (wavenumber(index_x) + offset(0)) ** 2
    square_z = (wavenumber(index_z) + offset(2)) ** 2
    for m in range(local):
        square_y = (wavenumber(me * local + m) + offset(1)) ** 2
        value = 0.5 * (square_x + square_y + square_z)
        kin[:, m * n : (m + 1) * n] = value
        pre[:, m * n : (m + 1) * n] = 1.0 / (value + 1.0)

    def wide(ref):
        return jnp.concatenate([ref[m] for m in range(local)], axis=1)


    overlaps = []
    for band in range(BANDS):
        real, imag = receive_real(0, band)
        space_wave[band, 0] = real
        space_wave[band, 1] = imag
        change = wide(perturbation)
        changed_real = change * real
        changed_imag = change * imag
        overlaps.append(lane_sums(changed_real * real + changed_imag * imag))
        if band == BANDS - 1:
            first_real = space_wave[0, 0]
            first_imag = space_wave[0, 1]
            overlaps.append(lane_sums(first_real * changed_real + first_imag * changed_imag))
            overlaps.append(lane_sums(first_real * changed_imag - first_imag * changed_real))
            send_small(0, overlaps)
        send_reciprocal(1, band, changed_real, changed_imag)

    def slot_a(step, band):
        return 1 + BANDS * step + band

    def slot_b(step, band):
        return 1 + BANDS * (CG_STEPS + step) + band

    def search_sums(band, real, imag):
        shifted = kin[...] - energy[0, band]
        sums = [lane_sums(shifted * (real * real + imag * imag))]
        for m in range(BANDS):
            sums.append(lane_sums(wave[m, 0] * real + wave[m, 1] * imag))
            sums.append(lane_sums(wave[m, 0] * imag - wave[m, 1] * real))
        return [value * inverse_total for value in sums]


    partial = [None] * BANDS
    rho = [None] * BANDS
    for band in range(BANDS):
        real, imag = receive_reciprocal(1, band)
        if band == 0:
            same0, same1, cross_real, cross_imag = receive_small(0, 4)
        if band == 0:
            m0_real, m0_imag, m1_real, m1_imag = same0, 0.0 * same0, cross_real, -cross_imag
        else:
            m0_real, m0_imag, m1_real, m1_imag = cross_real, cross_imag, same1, 0.0 * same1
        resid_real = (
            wave[0, 0] * m0_real
            - wave[0, 1] * m0_imag
            + wave[1, 0] * m1_real
            - wave[1, 1] * m1_imag
            - real
        )
        resid_imag = (
            wave[0, 0] * m0_imag
            + wave[0, 1] * m0_real
            + wave[1, 0] * m1_imag
            + wave[1, 1] * m1_real
            - imag
        )
        step_real = pre[...] * resid_real
        step_imag = pre[...] * resid_imag
        send_small(
            slot_a(0, band),
            [lane_sums(resid_real * step_real + resid_imag * step_imag) * inverse_total],
        )
        resid[band, 0] = resid_real
        resid[band, 1] = resid_imag
        search[band, 0] = step_real
        search[band, 1] = step_imag
        send_real(2, band, step_real, step_imag)
    for band in range(BANDS):
        partial[band] = search_sums(band, search[band, 0], search[band, 1])


    step_size = [None] * BANDS
    beta = [None] * BANDS

    def finish_curvature(step, band):
        curvature, c0_real, c0_imag, c1_real, c1_imag = receive_small(slot_b(step, band), 5)
        curvature = curvature + 2.0 * (
            c0_real * c0_real + c0_imag * c0_imag + c1_real * c1_real + c1_imag * c1_imag
        )
        return rho[band] / curvature, c0_real, c0_imag, c1_real, c1_imag

    for step in range(CG_STEPS):
        last = step + 1 == CG_STEPS
        for band in range(BANDS):
            real, imag = receive_real(2 + 2 * step, band)
            if step > 0:
                real = real + beta[band] * space_search[band, 0]
                imag = imag + beta[band] * space_search[band, 1]
            if not last:
                space_search[band, 0] = real
                space_search[band, 1] = imag
            level = wide(potential)
            image_real = level * real
            image_imag = level * imag
            sums = list(partial[band])
            sums[0] = sums[0] + lane_sums(image_real * real + image_imag * imag)
            send_small(slot_b(step, band), sums)
            overlap[band] = space_wave[band, 0] * real + space_wave[band, 1] * imag
            if not last:
                send_reciprocal(3 + 2 * step, band, image_real, image_imag)
        if step == 0:
            for band in range(BANDS):
                (rho[band],) = receive_small(slot_a(0, band), 1)
        if last:
            break
        for band in range(BANDS):
            size, c0_real, c0_imag, c1_real, c1_imag = finish_curvature(step, band)
            added = size * overlap[band]
            if step == 0 and band == 0:
                total[...] = added
            else:
                total[...] = total[...] + added
            pot_real, pot_imag = receive_reciprocal(3 + 2 * step, band)
            shifted = kin[...] - energy[0, band]
            real = search[band, 0]
            imag = search[band, 1]
            image_real = (
                shifted * real
                + pot_real
                + 2.0
                * (
                    wave[0, 0] * c0_real
                    - wave[0, 1] * c0_imag
                    + wave[1, 0] * c1_real
                    - wave[1, 1] * c1_imag
                )
            )
            image_imag = (
                shifted * imag
                + pot_imag
                + 2.0
                * (
                    wave[0, 0] * c0_imag
                    + wave[0, 1] * c0_real
                    + wave[1, 0] * c1_imag
                    + wave[1, 1] * c1_real
                )
            )
            resid_real = resid[band, 0] - size * image_real
            resid_imag = resid[band, 1] - size * image_imag
            step_real = pre[...] * resid_real
            step_imag = pre[...] * resid_imag
            send_small(
                slot_a(step + 1, band),
                [lane_sums(resid_real * step_real + resid_imag * step_imag) * inverse_total],
            )
            resid[band, 0] = resid_real
            resid[band, 1] = resid_imag
            send_real(4 + 2 * step, band, step_real, step_imag)
            step_size[band] = size
        for band in range(BANDS):
            size = step_size[band]
            (rho_new,) = receive_small(slot_a(step + 1, band), 1)
            beta[band] = rho_new / rho[band]
            rho[band] = rho_new
            for c in range(2):
                value = search[band, c]
                moved = size * value
                coeff[band, c] = moved if step == 0 else coeff[band, c] + moved
                search[band, c] = pre[...] * resid[band, c] + beta[band] * value
            partial[band] = search_sums(band, search[band, 0], search[band, 1])


    sums = total[...]
    for band in range(BANDS):
        step_size[band] = finish_curvature(CG_STEPS - 1, band)[0]
        sums = sums + step_size[band] * overlap[band]
    pool_send[...] = exact_dot(y_rows[...], (2.0 * grid_total) * sums).reshape(
        pools, parts, local * n
    )

    def exchange(source, target, which):
        def start(index, _):
            other = pool_peer(index)
            pltpu.make_async_remote_copy(
                src_ref=source.at[other] if which == 0 else source,
                dst_ref=target.at[pool],
                send_sem=pool_out.at[which],
                recv_sem=pool_in.at[which],
                device_id={"pool": other},
                device_id_type=MESH,
            ).start()
            return 0

        lax.fori_loop(1, pools, start, 0)

    def turn(source, target, which):
        here = pl.multiple_of(me * 2 * local, 2 * local)
        target[pl.ds(here, 2 * local), :] = source[pl.ds(here, 2 * local), :]

        def start(index, _):
            other = peer(index)
            there = pl.multiple_of(other * 2 * local, 2 * local)
            pltpu.make_async_remote_copy(
                src_ref=source.at[pl.ds(there, 2 * local)],
                dst_ref=target.at[pl.ds(here, 2 * local)],
                send_sem=turn_out.at[which],
                recv_sem=turn_in.at[which],
                device_id={"fft": other},
                device_id_type=MESH,
            ).start()
            return 0

        lax.fori_loop(1, parts, start, 0)

    def wait_turn(target, which):
        wait_bytes(target.at[pl.ds(0, 2 * local * (parts - 1))], turn_in.at[which])
        return [target[pl.ds(m, parts, stride=2 * local), :] for m in range(local)]

    exchange(pool_send, pool_recv, 0)
    pool_recv[pool] = pool_send[pool]
    go_send[...] = jnp.zeros_like(go_send)
    for band in range(BANDS):
        for c in range(2):
            coeff[band, c] = coeff[band, c] + step_size[band] * search[band, c]
    wait_bytes(pool_recv.at[pl.ds(0, pools - 1)], pool_in.at[0])
    column = jnp.sum(pool_recv[...], axis=0)
    for m in range(local):
        go_send[pl.ds(m, parts, stride=2 * local), :] = lanes(column, m)
    turn(go_send, go_recv, 0)
    own_dens[...] = column
    pool_dens[pool] = column
    exchange(own_dens, pool_dens, 1)


    even = 2 * me
    frequency = jnp.where(
        pool == 0, even, jnp.where(pool == 1, jnp.where(me == 0, n // 2, even), even + 1)
    )

    def plain_square(index):
        k = jnp.where(index > n // 2, index - n // 2, index)
        return (k.astype(f32) * unit) ** 2

    squared = (
        plain_square(index_x) + (frequency.astype(f32) * unit) ** 2 + plain_square(index_z)
    )
    nonzero = (squared > 0).astype(f32)
    coulomb = 4.0 * math.pi * nonzero / (squared + (1.0 - nonzero))

    field = jnp.concatenate(wait_turn(go_recv, 0), axis=0)
    field = exact_dot(exact_dot(x_rows[...], field), z_rows[...])
    field = exact_dot(coulomb * field, z_back[...])
    back_send[...] = exact_dot(x_back[...], field)
    turn(back_send, back_recv, 1)
    wait_bytes(pool_dens.at[pl.ds(0, pools - 1)], pool_in.at[1])
    whole = exact_dot(y_back[...], pool_dens[...].reshape(n, local * n))
    for m in range(local):
        density[m] = lanes(whole, m)
    column = jnp.concatenate(wait_turn(back_recv, 1), axis=1)
    own_hart[...] = column
    pool_hart[pool] = column
    exchange(own_hart, pool_hart, 2)
    wait_bytes(pool_hart.at[pl.ds(0, pools - 1)], pool_in.at[2])
    hartree = exact_dot(y_back[...], pool_hart[...].reshape(n, local * n))
    for m in range(local):
        hxc[m] = lanes(hartree, m) + xc[m] * density[m]


    for phase in range(2 * CG_STEPS + 1):
        for band in range(BANDS):
            wait_bytes(send.at[phase, band, pl.ds(0, parts - 1)], bulk_out.at[phase, band])
    for slot in range(1 + 2 * BANDS * CG_STEPS):
        wait_bytes(small_recv.at[slot, pl.ds(0, parts - 1)], small_out.at[slot])
    for which in range(3):
        wait_bytes(pool_recv.at[pl.ds(0, pools - 1)], pool_out.at[which])
    for which in range(2):
        wait_bytes(go_send.at[pl.ds(0, 2 * local * (parts - 1))], turn_out.at[which])


def body(wave_coeff, band_energy, local_potential, perturbation, xc_kernel, parts, pools):
    n = wave_coeff.shape[-1]
    local = n // parts
    block = 2 * local * local
    wide = local * n
    phases = 2 * CG_STEPS + 1
    slots = 1 + 2 * BANDS * CG_STEPS
    left, right, real = make_tables(n, parts)
    vmem = pl.BlockSpec(memory_space=pltpu.VMEM)
    field = (BANDS, 2, n, wide)
    dma = pltpu.SemaphoreType.DMA
    coeff, density, hxc = pl.pallas_call(
        functools.partial(kernel, n, parts, pools),
        out_shape=(
            jax.ShapeDtypeStruct(field, f32),
            jax.ShapeDtypeStruct((local, n, n), f32),
            jax.ShapeDtypeStruct((local, n, n), f32),
        ),
        in_specs=[vmem, pl.BlockSpec(memory_space=pltpu.SMEM)] + [vmem] * 11,
        out_specs=(vmem, vmem, vmem),
        scratch_shapes=[
            pltpu.VMEM((n, wide), f32),
            pltpu.VMEM((n, wide), f32),
            pltpu.VMEM(field, f32),
            pltpu.VMEM(field, f32),
            pltpu.VMEM(field, f32),
            pltpu.VMEM(field, f32),
            pltpu.VMEM((BANDS, n, wide), f32),
            pltpu.VMEM((n, wide), f32),
            pltpu.VMEM((phases, BANDS, parts, block, n), f32),
            pltpu.VMEM((phases, BANDS, parts * block, n), f32),
            pltpu.VMEM((slots, 1, n), f32),
            pltpu.VMEM((slots, parts, 1, n), f32),
            pltpu.VMEM((pools, parts, wide), f32),
            pltpu.VMEM((pools, parts, wide), f32),
            pltpu.VMEM((pools, parts, wide), f32),
            pltpu.VMEM((pools, parts, wide), f32),
            pltpu.VMEM((parts, wide), f32),
            pltpu.VMEM((parts, wide), f32),
            pltpu.VMEM((2 * n, n), f32),
            pltpu.VMEM((2 * n, n), f32),
            pltpu.VMEM((2 * n, n), f32),
            pltpu.VMEM((2 * n, n), f32),
            dma((phases, BANDS)),
            dma((phases, BANDS)),
            dma((slots,)),
            dma((slots,)),
            dma((3,)),
            dma((3,)),
            dma((2,)),
            dma((2,)),
        ],
        compiler_params=pltpu.CompilerParams(
            collective_id=0, has_side_effects=True, vmem_limit_bytes=56 * 1024 * 1024
        ),
    )(
        wave_coeff.reshape(field),
        band_energy,
        local_potential,
        perturbation,
        xc_kernel,
        jnp.asarray(left),
        jnp.asarray(right),
        *[jnp.asarray(t) for t in real],
    )
    return coeff.reshape(wave_coeff.shape), density, hxc


def solution(mesh):
    return jax.shard_map(
        functools.partial(body, parts=mesh.shape["fft"], pools=mesh.shape["pool"]),
        mesh=mesh,
        in_specs=(
            P("pool", None, None, None, "fft", None),
            P("pool", None),
            P("fft", None, None),
            P("fft", None, None),
            P("fft", None, None),
        ),
        out_specs=(
            P("pool", None, None, None, "fft", None),
            P("fft", None, None),
            P("fft", None, None),
        ),
        check_vma=False,
    )
```

```python
import functools
import math

import jax
import jax.numpy as jnp
import ml_dtypes
import numpy as np
from jax import lax
from jax.experimental import pallas as pl
from jax.experimental.pallas import tpu as pltpu
from jax.sharding import PartitionSpec as P

CG_STEPS = 3
BANDS = 2
cell_length = 51.3
unit = 2.0 * math.pi / cell_length
MESH = pl.DeviceIdType.MESH
f32 = jnp.float32
bf16 = jnp.bfloat16


def left_table(rows, cols, n, sign, scale=1.0):
    rows, cols = np.array(rows), np.array(cols)
    phase = 2.0 * np.pi * ((rows[:, None, 1] * cols[None, :, 1]) % n) / n
    out_part, in_part = rows[:, None, 0], cols[None, :, 0]
    value = np.where(
        out_part == in_part,
        np.cos(phase),
        np.where(out_part == 1, sign, -sign) * np.sin(phase),
    )
    return value * scale


def split_table(table, axis):
    high = table.astype(ml_dtypes.bfloat16)
    low = (table - high.astype(np.float64)).astype(ml_dtypes.bfloat16)
    return np.concatenate([high, high, low], axis=axis)


def real_basis(n, order):
    k = np.array([f for f, _ in order])
    phase = 2.0 * np.pi * ((k[:, None] * np.arange(n)[None, :]) % n) / n
    is_sin = np.array([s for _, s in order])[:, None]
    rows = np.where(is_sin == 1, np.sin(phase), np.cos(phase))
    weight = np.where((k == 0) | (2 * k == n), 1.0, 2.0)[:, None] / n
    return rows, rows * weight


def make_tables(n, parts):
    local = n // parts
    natural = [(c, j) for c in range(2) for j in range(n)]
    by_owner = [(c, q * local + m) for q in range(parts) for c in range(2) for m in range(local)]
    by_local = [(c, q * local + m) for c in range(2) for m in range(local) for q in range(parts)]
    scale = 1.0 / n**3
    left = np.stack(
        [
            split_table(left_table(by_owner, natural, n, 1.0), 1),
            split_table(left_table(natural, by_local, n, 1.0, scale), 1),
            split_table(left_table(by_owner, natural, n, -1.0), 1),
            split_table(left_table(natural, by_local, n, -1.0), 1),
        ]
    )
    right = np.stack(
        [
            split_table(left_table(natural, natural, n, 1.0).T, 0),
            split_table(left_table(natural, natural, n, -1.0).T, 0),
        ]
    )
    half = n // 2
    plain = [(k, 0) for k in range(half + 1)] + [(k, 1) for k in range(1, half)]
    columns = [
        [(2 * p, 0) for p in range(parts)],
        [(half, 0)] + [(2 * p, 1) for p in range(1, parts)],
        [(2 * p + 1, 0) for p in range(parts)],
        [(2 * p + 1, 1) for p in range(parts)],
    ]
    y_rows, y_back = real_basis(n, sum(columns, []))
    rows, back = real_basis(n, plain)
    by_local_x = [q * local + m for m in range(local) for q in range(parts)]
    x_rows = rows[:, by_local_x]
    x_back = np.zeros((parts, 2 * local, n))
    x_back[:, :local] = back.T.reshape(parts, local, n)
    basis_y = np.stack([split_table(y_rows * 2.0 * n**3, 1), split_table(y_back.T, 1)])
    basis_z = np.stack([split_table(rows.T, 0), split_table(back, 0)])
    basis_x = split_table(x_rows, 1)
    spread_x = split_table(x_back.reshape(2 * n, n), 1)
    return [left, right, basis_y, basis_x, spread_x, basis_z]


def halves(value):
    high = value.astype(bf16)
    low = (value - high.astype(f32)).astype(bf16)
    return high, low


def left_dot(table, data):
    high, low = halves(data)
    return jnp.dot(table, jnp.concatenate([high, low, high], axis=0), preferred_element_type=f32)


def right_dot(data, table):
    high, low = halves(data)
    return jnp.dot(jnp.concatenate([high, low, high], axis=1), table, preferred_element_type=f32)


def kernel(
    n,
    parts,
    pools,
    grid,
    raw_hbm,
    energy,
    potential_hbm,
    perturbation_hbm,
    xc_hbm,
    left_hbm,
    right_hbm,
    basis_y_hbm,
    basis_x_hbm,
    spread_x_hbm,
    basis_z_hbm,
    coeff,
    density,
    hxc,
    raw,
    potential,
    perturbation,
    xc,
    left,
    right,
    basis_y,
    basis_x,
    spread_x,
    basis_z,
    wave,
    kin,
    pre,
    resid,
    search,
    answer,
    space_wave,
    space_search,
    overlap,
    total,
    send,
    recv,
    small_send,
    small_recv,
    go_send,
    go_recv,
    back_send,
    back_recv,
    loaded,
    bulk_out,
    bulk_in,
    small_out,
    small_in,
    turn_out,
    turn_in,
):
    local = n // parts
    block = 2 * local * local
    devices = parts * pools
    inverse_total = 1.0 / n**3
    me = lax.axis_index("fft")
    pool = lax.axis_index("pool")
    size_z, size_x, size_c = grid
    my_z, my_x, my_c = me // (size_x * size_c), lax.rem(me // size_c, size_x), lax.rem(me, size_c)
    at_self = (-(size_z // 2) % size_z) * size_x * size_c + (-(size_x // 2) % size_x) * size_c

    def lanes(value, index):
        return value[:, index * n : (index + 1) * n]

    def peer(index):
        z = lax.rem(my_z + size_z // 2 + index // (size_x * size_c), size_z)
        x = lax.rem(my_x + size_x // 2 + lax.rem(index // size_c, size_x), size_x)
        c = lax.rem(my_c + lax.rem(index, size_c), size_c)
        return (z * size_x + x) * size_c + c

    def for_peers(act):
        def step(index, _):
            act(peer(index))
            return 0

        lax.fori_loop(0, at_self, step, 0)
        lax.fori_loop(at_self + 1, parts, step, 0)

    def for_devices(act):
        for shift in (2, 1, 3):
            other_pool = lax.rem(pool + shift, pools)

            def step(index, _, other_pool=other_pool):
                act(peer(index), other_pool)
                return 0

            lax.fori_loop(0, parts, step, 0)
        for_peers(lambda other: act(other, pool))

    barrier = pltpu.get_barrier_semaphore()

    def greet(other, other_pool):
        pl.semaphore_signal(
            barrier, inc=1, device_id={"pool": other_pool, "fft": other}, device_id_type=MESH
        )

    for_devices(greet)
    loads = {}
    order = [
        (raw_hbm, raw),
        (right_hbm, right),
        (left_hbm, left),
        (perturbation_hbm, perturbation),
        (potential_hbm, potential),
        (basis_y_hbm, basis_y),
        (basis_x_hbm, basis_x),
        (basis_z_hbm, basis_z),
        (spread_x_hbm, spread_x),
        (xc_hbm, xc),
    ]
    for i, (source, target) in enumerate(order):
        loads[i] = pltpu.make_async_copy(source, target, loaded.at[i])
        loads[i].start()


    def store_bulk(phase, band, value):
        for m in range(local):
            send[phase, band, :, 2 * local * m : 2 * local * (m + 1), :] = lanes(value, m).reshape(
                parts, 2 * local, n
            )

    def start_bulk(phase, band):
        here = pl.multiple_of(me * block, block)

        def start(other):
            pltpu.make_async_remote_copy(
                src_ref=send.at[phase, band, other],
                dst_ref=recv.at[phase, band, pl.ds(here, block)],
                send_sem=bulk_out.at[phase, band],
                recv_sem=bulk_in.at[phase, band],
                device_id={"fft": other},
                device_id_type=MESH,
            ).start()

        for_peers(start)
        recv[phase, band, pl.ds(here, block), :] = send[phase, band, me]

    def send_bulk(phase, band, value):
        store_bulk(phase, band, value)
        start_bulk(phase, band)

    def wait_bytes(ref, sem):
        pltpu.make_async_copy(ref, ref, sem).wait()

    def receive_bulk(phase, band):
        wait_bytes(recv.at[phase, band, pl.ds(0, block * (parts - 1))], bulk_in.at[phase, band])
        rows = []
        for c in range(2):
            for m in range(local):
                pieces = []
                for other in range(local):
                    first = 2 * local * m + local * c + other
                    pieces.append(recv[phase, band, pl.ds(first, parts, stride=block), :])
                rows.append(jnp.concatenate(pieces, axis=1))
        return jnp.concatenate(rows, axis=0)

    row_id = lax.broadcasted_iota(jnp.int32, (8, n), 0)
    lane_id = lax.broadcasted_iota(jnp.int32, (8, n), 1)

    def lane_sums(value):
        column = jnp.sum(value, axis=0, keepdims=True)
        result = lanes(column, 0)
        for m in range(1, local):
            result = result + lanes(column, m)
        return result

    def send_small(slot, values):
        stacked = jnp.zeros((8, n), f32)
        for i, value in enumerate(values):
            stacked = jnp.where(row_id == i, value, stacked)
        sums = jnp.sum(stacked, axis=1, keepdims=True)
        row = jnp.sum(jnp.where(row_id == lane_id, sums, 0.0), axis=0, keepdims=True)
        small_send[slot] = row
        small_recv[slot, me] = row

        def start(other):
            pltpu.make_async_remote_copy(
                src_ref=small_send.at[slot],
                dst_ref=small_recv.at[slot, me],
                send_sem=small_out.at[slot],
                recv_sem=small_in.at[slot],
                device_id={"fft": other},
                device_id_type=MESH,
            ).start()

        for_peers(start)

    def receive_small(slot, count):
        wait_bytes(small_recv.at[slot, pl.ds(0, parts - 1)], small_in.at[slot])
        row = jnp.sum(small_recv[slot], axis=0)
        return [
            jnp.sum(jnp.where(lane_id[:1] == i, row, 0.0), axis=1, keepdims=True)
            for i in range(count)
        ]


    def along_z(real, imag, table):
        rows = jnp.concatenate(
            [jnp.concatenate([lanes(real, m), lanes(imag, m)], axis=1) for m in range(local)],
            axis=0,
        )
        out = right_dot(rows, table)
        picked = [out[m * n : (m + 1) * n] for m in range(local)]
        return (
            jnp.concatenate([lanes(v, 0) for v in picked], axis=1),
            jnp.concatenate([lanes(v, 1) for v in picked], axis=1),
        )

    def send_real(phase, band, real, imag):
        real, imag = along_z(real, imag, right[0])
        send_bulk(phase, band, left_dot(left[0], jnp.concatenate([real, imag], axis=0)))

    def receive_real(phase, band):
        out = left_dot(left[1], receive_bulk(phase, band))
        return out[:n], out[n:]

    def send_reciprocal(phase, band, real, imag):
        send_bulk(phase, band, left_dot(left[2], jnp.concatenate([real, imag], axis=0)))

    def receive_reciprocal(phase, band):
        out = left_dot(left[3], receive_bulk(phase, band))
        return along_z(out[:n], out[n:], right[1])


    loads[0].wait()
    for band in range(BANDS):
        for c in range(2):
            for m in range(local):
                wave[band, c, :, m * n : (m + 1) * n] = raw[
                    band, c, pl.ds(m, n, stride=local), :
                ]
        if band == 0:
            loads[1].wait()
            loads[2].wait()
        real, imag = along_z(wave[band, 0], wave[band, 1], right[0])
        store_bulk(0, band, left_dot(left[0], jnp.concatenate([real, imag], axis=0)))
        if band == 0:
            pl.semaphore_wait(barrier, devices - 1)
        start_bulk(0, band)

    def wavenumber(index):
        signed = jnp.where(2 * index >= n, index - n, index)
        return signed.astype(f32) * unit

    def offset(axis_number):
        bit = lax.rem(pool // 2**axis_number, 2)
        return (0.5 * bit.astype(f32) - 0.25) * unit

    index_x = lax.broadcasted_iota(jnp.int32, (n, n), 0)
    index_z = lax.broadcasted_iota(jnp.int32, (n, n), 1)
    square_x = (wavenumber(index_x) + offset(0)) ** 2
    square_z = (wavenumber(index_z) + offset(2)) ** 2
    for m in range(local):
        square_y = (wavenumber(me * local + m) + offset(1)) ** 2
        value = 0.5 * (square_x + square_y + square_z)
        kin[:, m * n : (m + 1) * n] = value
        pre[:, m * n : (m + 1) * n] = 1.0 / (value + 1.0)

    def wide(ref):
        return jnp.concatenate([ref[m] for m in range(local)], axis=1)


    overlaps = []
    for i in range(3, len(order)):
        loads[i].wait()
    for band in range(BANDS):
        real, imag = receive_real(0, band)
        space_wave[band, 0] = real
        space_wave[band, 1] = imag
        change = wide(perturbation)
        changed_real = change * real
        changed_imag = change * imag
        overlaps.append(lane_sums(changed_real * real + changed_imag * imag))
        if band == BANDS - 1:
            first_real = space_wave[0, 0]
            first_imag = space_wave[0, 1]
            overlaps.append(lane_sums(first_real * changed_real + first_imag * changed_imag))
            overlaps.append(lane_sums(first_real * changed_imag - first_imag * changed_real))
            send_small(0, overlaps)
        send_reciprocal(1, band, changed_real, changed_imag)

    def slot_a(step, band):
        return 1 + BANDS * step + band

    def slot_b(step, band):
        return 1 + BANDS * (CG_STEPS + step) + band

    def search_sums(band, real, imag):
        shifted = kin[...] - energy[0, band]
        sums = [lane_sums(shifted * (real * real + imag * imag))]
        for m in range(BANDS):
            sums.append(lane_sums(wave[m, 0] * real + wave[m, 1] * imag))
            sums.append(lane_sums(wave[m, 0] * imag - wave[m, 1] * real))
        return [value * inverse_total for value in sums]


    partial = [None] * BANDS
    rho = [None] * BANDS
    for band in range(BANDS):
        real, imag = receive_reciprocal(1, band)
        if band == 0:
            same0, same1, cross_real, cross_imag = receive_small(0, 4)
        if band == 0:
            m0_real, m0_imag, m1_real, m1_imag = same0, 0.0 * same0, cross_real, -cross_imag
        else:
            m0_real, m0_imag, m1_real, m1_imag = cross_real, cross_imag, same1, 0.0 * same1
        resid_real = (
            wave[0, 0] * m0_real
            - wave[0, 1] * m0_imag
            + wave[1, 0] * m1_real
            - wave[1, 1] * m1_imag
            - real
        )
        resid_imag = (
            wave[0, 0] * m0_imag
            + wave[0, 1] * m0_real
            + wave[1, 0] * m1_imag
            + wave[1, 1] * m1_real
            - imag
        )
        step_real = pre[...] * resid_real
        step_imag = pre[...] * resid_imag
        send_small(
            slot_a(0, band),
            [lane_sums(resid_real * step_real + resid_imag * step_imag) * inverse_total],
        )
        resid[band, 0] = resid_real
        resid[band, 1] = resid_imag
        search[band, 0] = step_real
        search[band, 1] = step_imag
        send_real(2, band, step_real, step_imag)


    step_size = [None] * BANDS
    beta = [None] * BANDS

    def finish_curvature(step, band):
        curvature, c0_real, c0_imag, c1_real, c1_imag = receive_small(slot_b(step, band), 5)
        curvature = curvature + 2.0 * (
            c0_real * c0_real + c0_imag * c0_imag + c1_real * c1_real + c1_imag * c1_imag
        )
        return rho[band] / curvature, c0_real, c0_imag, c1_real, c1_imag

    def next_search(step, band):
        size = step_size[band]
        (rho_new,) = receive_small(slot_a(step, band), 1)
        beta[band] = rho_new / rho[band]
        rho[band] = rho_new
        for c in range(2):
            value = search[band, c]
            moved = size * value
            answer[band, c] = moved if step == 1 else answer[band, c] + moved
            search[band, c] = pre[...] * resid[band, c] + beta[band] * value

    for step in range(CG_STEPS):
        last = step + 1 == CG_STEPS
        for band in range(BANDS):
            if step > 0:
                next_search(step, band)
            partial[band] = search_sums(band, search[band, 0], search[band, 1])
            real, imag = receive_real(2 + 2 * step, band)
            if step > 0:
                real = real + beta[band] * space_search[band, 0]
                imag = imag + beta[band] * space_search[band, 1]
            if not last:
                space_search[band, 0] = real
                space_search[band, 1] = imag
            level = wide(potential)
            image_real = level * real
            image_imag = level * imag
            sums = list(partial[band])
            sums[0] = sums[0] + lane_sums(image_real * real + image_imag * imag)
            send_small(slot_b(step, band), sums)
            overlap[band] = space_wave[band, 0] * real + space_wave[band, 1] * imag
            if not last:
                send_reciprocal(3 + 2 * step, band, image_real, image_imag)
        if step == 0:
            for band in range(BANDS):
                (rho[band],) = receive_small(slot_a(0, band), 1)
        if last:
            break
        for band in range(BANDS):
            size, c0_real, c0_imag, c1_real, c1_imag = finish_curvature(step, band)
            added = size * overlap[band]
            if step == 0 and band == 0:
                total[...] = added
            else:
                total[...] = total[...] + added
            pot_real, pot_imag = receive_reciprocal(3 + 2 * step, band)
            shifted = kin[...] - energy[0, band]
            real = search[band, 0]
            imag = search[band, 1]
            image_real = (
                shifted * real
                + pot_real
                + 2.0
                * (
                    wave[0, 0] * c0_real
                    - wave[0, 1] * c0_imag
                    + wave[1, 0] * c1_real
                    - wave[1, 1] * c1_imag
                )
            )
            image_imag = (
                shifted * imag
                + pot_imag
                + 2.0
                * (
                    wave[0, 0] * c0_imag
                    + wave[0, 1] * c0_real
                    + wave[1, 0] * c1_imag
                    + wave[1, 1] * c1_real
                )
            )
            resid_real = resid[band, 0] - size * image_real
            resid_imag = resid[band, 1] - size * image_imag
            step_real = pre[...] * resid_real
            step_imag = pre[...] * resid_imag
            send_small(
                slot_a(step + 1, band),
                [lane_sums(resid_real * step_real + resid_imag * step_imag) * inverse_total],
            )
            resid[band, 0] = resid_real
            resid[band, 1] = resid_imag
            send_real(4 + 2 * step, band, step_real, step_imag)
            step_size[band] = size

    columns = left_dot(basis_y[0], total[...])
    moved = [left_dot(basis_y[0], overlap[band]) for band in range(BANDS)]
    for band in range(BANDS):
        step_size[band] = finish_curvature(CG_STEPS - 1, band)[0]
        columns = columns + step_size[band] * moved[band]

    slot = 2 * local

    def turn(which, source, target, all_columns):
        here = pl.multiple_of((pool * parts + me) * slot, slot)
        own = here if all_columns else pl.multiple_of(me * slot, slot)
        target[pl.ds(here, local), :] = source[pl.ds(own, local), :]

        def start(other, other_pool):
            there = other_pool * parts + other if all_columns else other
            there = pl.multiple_of(there * slot, slot)
            pltpu.make_async_remote_copy(
                src_ref=source.at[pl.ds(there, local)],
                dst_ref=target.at[pl.ds(here, local)],
                send_sem=turn_out.at[which],
                recv_sem=turn_in.at[which],
                device_id={"pool": other_pool, "fft": other},
                device_id_type=MESH,
            ).start()

        for_devices(start)

    def wait_turn(which, target):
        wait_bytes(target.at[pl.ds(0, local * (devices - 1))], turn_in.at[which])

    for m in range(local):
        go_send[pl.ds(m, devices, stride=slot), :] = lanes(columns, m)
    turn(0, go_send, go_recv, True)
    for band in range(BANDS):
        for c in range(2):
            value = answer[band, c] + step_size[band] * search[band, c]
            for m in range(local):
                coeff[band, c, pl.ds(m, n, stride=local), :] = lanes(value, m)

    even = 2 * me
    frequency = jnp.where(
        pool == 0, even, jnp.where(pool == 1, jnp.where(me == 0, n // 2, even), even + 1)
    )

    def plain_square(index):
        k = jnp.where(index > n // 2, index - n // 2, index)
        return (k.astype(f32) * unit) ** 2

    squared = (
        plain_square(index_x) + (frequency.astype(f32) * unit) ** 2 + plain_square(index_z)
    )
    nonzero = (squared > 0).astype(f32)
    coulomb = 4.0 * math.pi * nonzero / (squared + (1.0 - nonzero))

    wait_turn(0, go_recv)
    pieces = []
    for m in range(local):
        piece = go_recv[pl.ds(m, parts, stride=slot), :]
        for other in range(1, pools):
            piece = piece + go_recv[pl.ds(other * parts * slot + m, parts, stride=slot), :]
        back_send[0, pl.ds(m, parts, stride=slot), :] = piece
        pieces.append(piece)
    turn(1, back_send.at[0], back_recv.at[0], False)


    field = left_dot(basis_x[...], jnp.concatenate(pieces, axis=0))
    field = coulomb * right_dot(field, basis_z[0])
    field = left_dot(spread_x[...], right_dot(field, basis_z[1]))
    back_send[1] = field
    turn(2, back_send.at[1], back_recv.at[1], False)

    for i, result in enumerate((density, hxc)):
        wait_turn(1 + i, back_recv.at[i])
        columns = [back_recv[i, pl.ds(m, devices, stride=slot), :] for m in range(local)]
        whole = left_dot(basis_y[1], jnp.concatenate(columns, axis=1))
        for m in range(local):
            if i == 0:
                result[m] = lanes(whole, m)
            else:
                result[m] = lanes(whole, m) + xc[m] * density[m]


    for phase in range(2 * CG_STEPS + 1):
        for band in range(BANDS):
            wait_bytes(send.at[phase, band, pl.ds(0, parts - 1)], bulk_out.at[phase, band])
    for slot in range(1 + 2 * BANDS * CG_STEPS):
        wait_bytes(small_recv.at[slot, pl.ds(0, parts - 1)], small_out.at[slot])
    for which in range(3):
        wait_bytes(go_recv.at[pl.ds(0, local * (devices - 1))], turn_out.at[which])


def body(wave_coeff, band_energy, local_potential, perturbation, xc_kernel, parts, pools):
    n = wave_coeff.shape[-1]
    local = n // parts
    block = 2 * local * local
    wide = local * n
    phases = 2 * CG_STEPS + 1
    slots = 1 + 2 * BANDS * CG_STEPS
    slot_rows = 2 * local * parts
    grid = (4, 4, 2) if parts == 32 else (1, parts, 1)
    operands = [
        wave_coeff.reshape(BANDS, 2, n * local, n),
        local_potential,
        perturbation,
        xc_kernel,
    ] + [jnp.asarray(t) for t in make_tables(n, parts)]
    anywhere = pl.BlockSpec(memory_space=pl.ANY)
    vmem = pl.BlockSpec(memory_space=pltpu.VMEM)
    field = pltpu.VMEM((BANDS, 2, n, wide), f32)
    dma = pltpu.SemaphoreType.DMA
    coeff, density, hxc = pl.pallas_call(
        functools.partial(kernel, n, parts, pools, grid),
        out_shape=(
            jax.ShapeDtypeStruct(operands[0].shape, f32),
            jax.ShapeDtypeStruct((local, n, n), f32),
            jax.ShapeDtypeStruct((local, n, n), f32),
        ),
        in_specs=[anywhere, pl.BlockSpec(memory_space=pltpu.SMEM)] + [anywhere] * 9,
        out_specs=(vmem, vmem, vmem),
        scratch_shapes=[pltpu.VMEM(t.shape, t.dtype) for t in operands]
        + [
            field,
            pltpu.VMEM((n, wide), f32),
            pltpu.VMEM((n, wide), f32),
            field,
            field,
            field,
            field,
            field,
            pltpu.VMEM((BANDS, n, wide), f32),
            pltpu.VMEM((n, wide), f32),
            pltpu.VMEM((phases, BANDS, parts, block, n), f32),
            pltpu.VMEM((phases, BANDS, parts * block, n), f32),
            pltpu.VMEM((slots, 1, n), f32),
            pltpu.VMEM((slots, parts, 1, n), f32),
            pltpu.VMEM((pools * slot_rows, n), f32),
            pltpu.VMEM((pools * slot_rows, n), f32),
            pltpu.VMEM((2, slot_rows, n), f32),
            pltpu.VMEM((2, pools * slot_rows, n), f32),
            dma((10,)),
            dma((phases, BANDS)),
            dma((phases, BANDS)),
            dma((slots,)),
            dma((slots,)),
            dma((3,)),
            dma((3,)),
        ],
        compiler_params=pltpu.CompilerParams(
            collective_id=0, has_side_effects=True, vmem_limit_bytes=56 * 1024 * 1024
        ),
    )(operands[0], band_energy, *operands[1:])
    return coeff.reshape(wave_coeff.shape), density, hxc


def solution(mesh):
    return jax.shard_map(
        functools.partial(body, parts=mesh.shape["fft"], pools=mesh.shape["pool"]),
        mesh=mesh,
        in_specs=(
            P("pool", None, None, None, "fft", None),
            P("pool", None),
            P("fft", None, None),
            P("fft", None, None),
            P("fft", None, None),
        ),
        out_specs=(
            P("pool", None, None, None, "fft", None),
            P("fft", None, None),
            P("fft", None, None),
        ),
        check_vma=False,
    )
```

```python
import functools
import math

import jax
import jax.numpy as jnp
import ml_dtypes
import numpy as np
from jax import lax
from jax.experimental import pallas as pl
from jax.experimental.pallas import tpu as pltpu
from jax.sharding import PartitionSpec as P

CG_STEPS = 3
BANDS = 2
cell_length = 51.3
unit = 2.0 * math.pi / cell_length
MESH = pl.DeviceIdType.MESH
f32 = jnp.float32
bf16 = jnp.bfloat16


def left_table(rows, cols, n, sign, scale=1.0):
    rows, cols = np.array(rows), np.array(cols)
    phase = 2.0 * np.pi * ((rows[:, None, 1] * cols[None, :, 1]) % n) / n
    out_part, in_part = rows[:, None, 0], cols[None, :, 0]
    value = np.where(
        out_part == in_part,
        np.cos(phase),
        np.where(out_part == 1, sign, -sign) * np.sin(phase),
    )
    return value * scale


def split_table(table, axis):
    high = table.astype(ml_dtypes.bfloat16)
    low = (table - high.astype(np.float64)).astype(ml_dtypes.bfloat16)
    return np.concatenate([high, high, low], axis=axis)


def real_basis(n, order):
    k = np.array([f for f, _ in order])
    phase = 2.0 * np.pi * ((k[:, None] * np.arange(n)[None, :]) % n) / n
    is_sin = np.array([s for _, s in order])[:, None]
    rows = np.where(is_sin == 1, np.sin(phase), np.cos(phase))
    weight = np.where((k == 0) | (2 * k == n), 1.0, 2.0)[:, None] / n
    return rows, rows * weight


def make_tables(n, parts):
    local = n // parts
    natural = [(c, j) for c in range(2) for j in range(n)]
    by_owner = [(c, q * local + m) for q in range(parts) for c in range(2) for m in range(local)]
    by_local = [(c, q * local + m) for c in range(2) for m in range(local) for q in range(parts)]
    scale = 1.0 / n**3
    left = np.stack(
        [
            split_table(left_table(by_owner, natural, n, 1.0), 1),
            split_table(left_table(natural, by_local, n, 1.0, scale), 1),
            split_table(left_table(by_owner, natural, n, -1.0), 1),
            split_table(left_table(natural, by_local, n, -1.0), 1),
        ]
    )
    right = np.stack(
        [
            split_table(left_table(natural, natural, n, 1.0).T, 0),
            split_table(left_table(natural, natural, n, -1.0).T, 0),
        ]
    )
    half = n // 2
    plain = [(k, 0) for k in range(half + 1)] + [(k, 1) for k in range(1, half)]
    columns = [
        [(2 * p, 0) for p in range(parts)],
        [(half, 0)] + [(2 * p, 1) for p in range(1, parts)],
        [(2 * p + 1, 0) for p in range(parts)],
        [(2 * p + 1, 1) for p in range(parts)],
    ]
    y_rows, y_back = real_basis(n, sum(columns, []))
    rows, back = real_basis(n, plain)
    by_local_x = [q * local + m for m in range(local) for q in range(parts)]
    x_rows = rows[:, by_local_x]
    x_back = np.zeros((parts, 2 * local, n))
    x_back[:, :local] = back.T.reshape(parts, local, n)
    basis_y = np.stack([split_table(y_rows * 2.0 * n**3, 1), split_table(y_back.T, 1)])
    basis_z = np.stack([split_table(rows.T, 0), split_table(back, 0)])
    basis_x = split_table(x_rows, 1)
    spread_x = split_table(x_back.reshape(2 * n, n), 1)
    return [left, right, basis_y, basis_x, spread_x, basis_z]


def halves(value):
    high = value.astype(bf16)
    low = (value - high.astype(f32)).astype(bf16)
    return high, low


def left_dot(table, data):
    high, low = halves(data)
    return jnp.dot(table, jnp.concatenate([high, low, high], axis=0), preferred_element_type=f32)


def right_dot(data, table):
    high, low = halves(data)
    return jnp.dot(jnp.concatenate([high, low, high], axis=1), table, preferred_element_type=f32)


def kernel(
    n,
    parts,
    pools,
    grid,
    raw_hbm,
    energy,
    potential_hbm,
    perturbation_hbm,
    xc_hbm,
    left_hbm,
    right_hbm,
    basis_y_hbm,
    basis_x_hbm,
    spread_x_hbm,
    basis_z_hbm,
    coeff,
    density,
    hxc,
    raw,
    potential,
    perturbation,
    xc,
    left,
    right,
    basis_y,
    basis_x,
    spread_x,
    basis_z,
    wave,
    kin,
    pre,
    resid,
    search,
    answer,
    ahead,
    space_wave,
    space_search,
    overlap,
    total,
    send,
    recv,
    small_send,
    small_recv,
    go_send,
    go_recv,
    back_send,
    back_recv,
    loaded,
    bulk_out,
    bulk_in,
    small_out,
    small_in,
    turn_out,
    turn_in,
):
    local = n // parts
    block = 2 * local * local
    room = block + 8
    devices = parts * pools
    inverse_total = 1.0 / n**3
    me = lax.axis_index("fft")
    pool = lax.axis_index("pool")
    size_z, size_x, size_c = grid
    my_z, my_x, my_c = me // (size_x * size_c), lax.rem(me // size_c, size_x), lax.rem(me, size_c)
    at_self = (-(size_z // 2) % size_z) * size_x * size_c + (-(size_x // 2) % size_x) * size_c

    def lanes(value, index):
        return value[:, index * n : (index + 1) * n]

    def peer(index):
        z = lax.rem(my_z + size_z // 2 + index // (size_x * size_c), size_z)
        x = lax.rem(my_x + size_x // 2 + lax.rem(index // size_c, size_x), size_x)
        c = lax.rem(my_c + lax.rem(index, size_c), size_c)
        return (z * size_x + x) * size_c + c

    def for_peers(act):
        def step(index, _):
            act(peer(index))
            return 0

        lax.fori_loop(0, at_self, step, 0)
        lax.fori_loop(at_self + 1, parts, step, 0)

    def for_devices(act):
        for shift in (2, 1, 3):
            other_pool = lax.rem(pool + shift, pools)

            def step(index, _, other_pool=other_pool):
                act(peer(index), other_pool)
                return 0

            lax.fori_loop(0, parts, step, 0)
        for_peers(lambda other: act(other, pool))

    barrier = pltpu.get_barrier_semaphore()

    def greet(other, other_pool):
        pl.semaphore_signal(
            barrier, inc=1, device_id={"pool": other_pool, "fft": other}, device_id_type=MESH
        )

    for_devices(greet)
    loads = {}
    order = [
        (raw_hbm, raw),
        (right_hbm, right),
        (left_hbm, left),
        (perturbation_hbm, perturbation),
        (potential_hbm, potential),
        (basis_y_hbm, basis_y),
        (basis_x_hbm, basis_x),
        (basis_z_hbm, basis_z),
        (spread_x_hbm, spread_x),
        (xc_hbm, xc),
    ]
    for i, (source, target) in enumerate(order):
        loads[i] = pltpu.make_async_copy(source, target, loaded.at[i])
        loads[i].start()


    def store_bulk(phase, band, value):
        for m in range(local):
            send[phase, band, :, 2 * local * m : 2 * local * (m + 1), :] = lanes(value, m).reshape(
                parts, 2 * local, n
            )

    def start_bulk(phase, band, row=None):
        here = pl.multiple_of(me * room, room)
        used = block if row is None else block + 1
        if row is not None:
            send[phase, band, :, block : block + 8, :] = jnp.broadcast_to(row, (parts, 8, n))

        def start(other):
            pltpu.make_async_remote_copy(
                src_ref=send.at[phase, band, other, pl.ds(0, used)],
                dst_ref=recv.at[phase, band, pl.ds(here, used)],
                send_sem=bulk_out.at[phase, band],
                recv_sem=bulk_in.at[phase, band],
                device_id={"fft": other},
                device_id_type=MESH,
            ).start()

        for_peers(start)
        recv[phase, band, pl.ds(here, room), :] = send[phase, band, me]

    def send_bulk(phase, band, value, row=None):
        store_bulk(phase, band, value)
        start_bulk(phase, band, row)

    def bulk_rows(phase):
        return (parts - 1) * (block + 1 if phase >= 2 else block)

    def wait_bytes(ref, sem):
        pltpu.make_async_copy(ref, ref, sem).wait()

    def receive_bulk(phase, band):
        wait_bytes(recv.at[phase, band, pl.ds(0, bulk_rows(phase))], bulk_in.at[phase, band])
        rows = []
        for c in range(2):
            for m in range(local):
                pieces = []
                for other in range(local):
                    first = 2 * local * m + local * c + other
                    pieces.append(recv[phase, band, pl.ds(first, parts, stride=room), :])
                rows.append(jnp.concatenate(pieces, axis=1))
        return jnp.concatenate(rows, axis=0)

    row_id = lax.broadcasted_iota(jnp.int32, (8, n), 0)
    lane_id = lax.broadcasted_iota(jnp.int32, (8, n), 1)

    def lane_sums(value):
        column = jnp.sum(value, axis=0, keepdims=True)
        result = lanes(column, 0)
        for m in range(1, local):
            result = result + lanes(column, m)
        return result

    def pack(values):
        stacked = jnp.zeros((8, n), f32)
        for i, value in enumerate(values):
            stacked = jnp.where(row_id == i, value, stacked)
        sums = jnp.sum(stacked, axis=1, keepdims=True)
        return jnp.sum(jnp.where(row_id == lane_id, sums, 0.0), axis=0, keepdims=True)

    def unpack(row, count):
        return [
            jnp.sum(jnp.where(lane_id[:1] == i, row, 0.0), axis=1, keepdims=True)
            for i in range(count)
        ]

    def bulk_row(phase, band, count):
        rows = recv[phase, band, pl.ds(block, parts, stride=room), :]
        return unpack(jnp.sum(rows, axis=0, keepdims=True), count)

    def send_small(slot, values):
        row = pack(values)
        small_send[slot] = row
        small_recv[slot, me] = row

        def start(other):
            pltpu.make_async_remote_copy(
                src_ref=small_send.at[slot],
                dst_ref=small_recv.at[slot, me],
                send_sem=small_out.at[slot],
                recv_sem=small_in.at[slot],
                device_id={"fft": other},
                device_id_type=MESH,
            ).start()

        for_peers(start)

    def receive_small(slot, count):
        wait_bytes(small_recv.at[slot, pl.ds(0, parts - 1)], small_in.at[slot])
        return unpack(jnp.sum(small_recv[slot], axis=0), count)


    def along_z(real, imag, table):
        rows = jnp.concatenate(
            [jnp.concatenate([lanes(real, m), lanes(imag, m)], axis=1) for m in range(local)],
            axis=0,
        )
        out = right_dot(rows, table)
        picked = [out[m * n : (m + 1) * n] for m in range(local)]
        return (
            jnp.concatenate([lanes(v, 0) for v in picked], axis=1),
            jnp.concatenate([lanes(v, 1) for v in picked], axis=1),
        )

    def send_real(phase, band, real, imag, row):
        real, imag = along_z(real, imag, right[0])
        send_bulk(phase, band, left_dot(left[0], jnp.concatenate([real, imag], axis=0)), row)

    def receive_real(phase, band):
        out = left_dot(left[1], receive_bulk(phase, band))
        return out[:n], out[n:]

    def send_reciprocal(phase, band, real, imag, row=None):
        send_bulk(phase, band, left_dot(left[2], jnp.concatenate([real, imag], axis=0)), row)

    def receive_reciprocal(phase, band):
        out = left_dot(left[3], receive_bulk(phase, band))
        return along_z(out[:n], out[n:], right[1])


    loads[0].wait()
    for band in range(BANDS):
        for c in range(2):
            for m in range(local):
                wave[band, c, :, m * n : (m + 1) * n] = raw[
                    band, c, pl.ds(m, n, stride=local), :
                ]
        if band == 0:
            loads[1].wait()
            loads[2].wait()
        real, imag = along_z(wave[band, 0], wave[band, 1], right[0])
        store_bulk(0, band, left_dot(left[0], jnp.concatenate([real, imag], axis=0)))
        if band == 0:
            pl.semaphore_wait(barrier, devices - 1)
        start_bulk(0, band)

    def wavenumber(index):
        signed = jnp.where(2 * index >= n, index - n, index)
        return signed.astype(f32) * unit

    def offset(axis_number):
        bit = lax.rem(pool // 2**axis_number, 2)
        return (0.5 * bit.astype(f32) - 0.25) * unit

    index_x = lax.broadcasted_iota(jnp.int32, (n, n), 0)
    index_z = lax.broadcasted_iota(jnp.int32, (n, n), 1)
    square_x = (wavenumber(index_x) + offset(0)) ** 2
    square_z = (wavenumber(index_z) + offset(2)) ** 2
    for m in range(local):
        square_y = (wavenumber(me * local + m) + offset(1)) ** 2
        value = 0.5 * (square_x + square_y + square_z)
        kin[:, m * n : (m + 1) * n] = value
        pre[:, m * n : (m + 1) * n] = 1.0 / (value + 1.0)

    def wide(ref):
        return jnp.concatenate([ref[m] for m in range(local)], axis=1)


    overlaps = []
    for i in range(3, len(order)):
        loads[i].wait()
    for band in range(BANDS):
        real, imag = receive_real(0, band)
        space_wave[band, 0] = real
        space_wave[band, 1] = imag
        change = wide(perturbation)
        changed_real = change * real
        changed_imag = change * imag
        overlaps.append(lane_sums(changed_real * real + changed_imag * imag))
        if band == BANDS - 1:
            first_real = space_wave[0, 0]
            first_imag = space_wave[0, 1]
            overlaps.append(lane_sums(first_real * changed_real + first_imag * changed_imag))
            overlaps.append(lane_sums(first_real * changed_imag - first_imag * changed_real))
            send_small(0, overlaps)
        send_reciprocal(1, band, changed_real, changed_imag)

    def products(band, real, imag):
        sums = []
        for m in range(BANDS):
            sums.append(lane_sums(wave[m, 0] * real + wave[m, 1] * imag))
            sums.append(lane_sums(wave[m, 0] * imag - wave[m, 1] * real))
        return [value * inverse_total for value in sums]

    def kinetic_sum(band, left_real, left_imag, right_real, right_imag):
        shifted = kin[...] - energy[0, band]
        return lane_sums(shifted * (left_real * right_real + left_imag * right_imag)) * inverse_total

    def send_step(phase, band, resid_real, resid_imag):
        real = pre[...] * resid_real
        imag = pre[...] * resid_imag
        row = pack([lane_sums(resid_real * real + resid_imag * imag) * inverse_total])
        resid[band, 0] = resid_real
        resid[band, 1] = resid_imag
        ahead[band, 0] = real
        ahead[band, 1] = imag
        send_real(phase, band, real, imag, row)


    partial = [None] * BANDS
    rho = [None] * BANDS
    for band in range(BANDS):
        real, imag = receive_reciprocal(1, band)
        if band == 0:
            same0, same1, cross_real, cross_imag = receive_small(0, 4)
        if band == 0:
            m0_real, m0_imag, m1_real, m1_imag = same0, 0.0 * same0, cross_real, -cross_imag
        else:
            m0_real, m0_imag, m1_real, m1_imag = cross_real, cross_imag, same1, 0.0 * same1
        resid_real = (
            wave[0, 0] * m0_real
            - wave[0, 1] * m0_imag
            + wave[1, 0] * m1_real
            - wave[1, 1] * m1_imag
            - real
        )
        resid_imag = (
            wave[0, 0] * m0_imag
            + wave[0, 1] * m0_real
            + wave[1, 0] * m1_imag
            + wave[1, 1] * m1_real
            - imag
        )
        send_step(2, band, resid_real, resid_imag)


    step_size = [None] * BANDS

    def finish_curvature(band, values):
        curvature, c0_real, c0_imag, c1_real, c1_imag = values
        curvature = curvature + 2.0 * (
            c0_real * c0_real + c0_imag * c0_imag + c1_real * c1_real + c1_imag * c1_imag
        )
        return rho[band] / curvature

    for step in range(CG_STEPS):
        last = step + 1 == CG_STEPS
        for band in range(BANDS):
            real, imag = ahead[band, 0], ahead[band, 1]
            sums = [kinetic_sum(band, real, imag, real, imag)] + products(band, real, imag)
            if step > 0:
                cross = kinetic_sum(band, real, imag, search[band, 0], search[band, 1])
            real, imag = receive_real(2 + 2 * step, band)
            (rho_new,) = bulk_row(2 + 2 * step, band, 1)
            if step > 0:
                beta = rho_new / rho[band]
                before = partial[band]
                sums[0] = sums[0] + beta * (2.0 * cross + beta * before[0])
                for i in range(1, 1 + 2 * BANDS):
                    sums[i] = sums[i] + beta * before[i]
                real = real + beta * space_search[band, 0]
                imag = imag + beta * space_search[band, 1]
            rho[band] = rho_new
            partial[band] = list(sums)
            if not last:
                space_search[band, 0] = real
                space_search[band, 1] = imag
            level = wide(potential)
            image_real = level * real
            image_imag = level * imag
            sums[0] = sums[0] + lane_sums(image_real * real + image_imag * imag)
            if last:
                send_small(1 + band, sums)
            else:
                send_reciprocal(3 + 2 * step, band, image_real, image_imag, pack(sums))
            overlap[band] = space_wave[band, 0] * real + space_wave[band, 1] * imag
            for c in range(2):
                if step == 0:
                    search[band, c] = ahead[band, c]
                else:
                    search[band, c] = ahead[band, c] + beta * search[band, c]
        if last:
            break
        for band in range(BANDS):
            pot_real, pot_imag = receive_reciprocal(3 + 2 * step, band)
            values = bulk_row(3 + 2 * step, band, 5)
            _, c0_real, c0_imag, c1_real, c1_imag = values
            size = finish_curvature(band, values)
            shifted = kin[...] - energy[0, band]
            real = search[band, 0]
            imag = search[band, 1]
            image_real = (
                shifted * real
                + pot_real
                + 2.0
                * (
                    wave[0, 0] * c0_real
                    - wave[0, 1] * c0_imag
                    + wave[1, 0] * c1_real
                    - wave[1, 1] * c1_imag
                )
            )
            image_imag = (
                shifted * imag
                + pot_imag
                + 2.0
                * (
                    wave[0, 0] * c0_imag
                    + wave[0, 1] * c0_real
                    + wave[1, 0] * c1_imag
                    + wave[1, 1] * c1_real
                )
            )
            send_step(
                4 + 2 * step,
                band,
                resid[band, 0] - size * image_real,
                resid[band, 1] - size * image_imag,
            )
            added = size * overlap[band]
            total[...] = added if step == 0 and band == 0 else total[...] + added
            for c in range(2):
                moved = size * search[band, c]
                answer[band, c] = moved if step == 0 else answer[band, c] + moved


    columns = left_dot(basis_y[0], total[...])
    moved = [left_dot(basis_y[0], overlap[band]) for band in range(BANDS)]
    for band in range(BANDS):
        step_size[band] = finish_curvature(band, receive_small(1 + band, 5))
        columns = columns + step_size[band] * moved[band]

    slot = 2 * local

    def turn(which, source, target, all_columns):
        here = pl.multiple_of((pool * parts + me) * slot, slot)
        own = here if all_columns else pl.multiple_of(me * slot, slot)
        target[pl.ds(here, local), :] = source[pl.ds(own, local), :]

        def start(other, other_pool):
            there = other_pool * parts + other if all_columns else other
            there = pl.multiple_of(there * slot, slot)
            pltpu.make_async_remote_copy(
                src_ref=source.at[pl.ds(there, local)],
                dst_ref=target.at[pl.ds(here, local)],
                send_sem=turn_out.at[which],
                recv_sem=turn_in.at[which],
                device_id={"pool": other_pool, "fft": other},
                device_id_type=MESH,
            ).start()

        for_devices(start)

    def wait_turn(which, target):
        wait_bytes(target.at[pl.ds(0, local * (devices - 1))], turn_in.at[which])

    for m in range(local):
        go_send[pl.ds(m, devices, stride=slot), :] = lanes(columns, m)
    turn(0, go_send, go_recv, True)
    for band in range(BANDS):
        for c in range(2):
            value = answer[band, c] + step_size[band] * search[band, c]
            for m in range(local):
                coeff[band, c, pl.ds(m, n, stride=local), :] = lanes(value, m)

    even = 2 * me
    frequency = jnp.where(
        pool == 0, even, jnp.where(pool == 1, jnp.where(me == 0, n // 2, even), even + 1)
    )

    def plain_square(index):
        k = jnp.where(index > n // 2, index - n // 2, index)
        return (k.astype(f32) * unit) ** 2

    squared = (
        plain_square(index_x) + (frequency.astype(f32) * unit) ** 2 + plain_square(index_z)
    )
    nonzero = (squared > 0).astype(f32)
    coulomb = 4.0 * math.pi * nonzero / (squared + (1.0 - nonzero))

    wait_turn(0, go_recv)
    pieces = []
    for m in range(local):
        piece = go_recv[pl.ds(m, parts, stride=slot), :]
        for other in range(1, pools):
            piece = piece + go_recv[pl.ds(other * parts * slot + m, parts, stride=slot), :]
        back_send[0, pl.ds(m, parts, stride=slot), :] = piece
        pieces.append(piece)
    turn(1, back_send.at[0], back_recv.at[0], False)


    field = left_dot(basis_x[...], jnp.concatenate(pieces, axis=0))
    field = coulomb * right_dot(field, basis_z[0])
    field = left_dot(spread_x[...], right_dot(field, basis_z[1]))
    back_send[1] = field
    turn(2, back_send.at[1], back_recv.at[1], False)

    for i, result in enumerate((density, hxc)):
        wait_turn(1 + i, back_recv.at[i])
        columns = [back_recv[i, pl.ds(m, devices, stride=slot), :] for m in range(local)]
        whole = left_dot(basis_y[1], jnp.concatenate(columns, axis=1))
        for m in range(local):
            if i == 0:
                result[m] = lanes(whole, m)
            else:
                result[m] = lanes(whole, m) + xc[m] * density[m]


    for phase in range(2 * CG_STEPS + 1):
        for band in range(BANDS):
            wait_bytes(recv.at[phase, band, pl.ds(0, bulk_rows(phase))], bulk_out.at[phase, band])
    for slot in range(1 + BANDS):
        wait_bytes(small_recv.at[slot, pl.ds(0, parts - 1)], small_out.at[slot])
    for which in range(3):
        wait_bytes(go_recv.at[pl.ds(0, local * (devices - 1))], turn_out.at[which])


def hand_over(coeff, density, hxc, coeff_out, density_out, hxc_out, done):
    pairs = [(density, density_out), (hxc, hxc_out)]
    pairs += [(coeff.at[b, c], coeff_out.at[b, c]) for b in range(BANDS) for c in range(2)]
    copies = [pltpu.make_async_copy(a, b, done.at[i]) for i, (a, b) in enumerate(pairs)]
    for copy in copies:
        copy.start()
    for copy in copies:
        copy.wait()


def body(wave_coeff, band_energy, local_potential, perturbation, xc_kernel, parts, pools):
    n = wave_coeff.shape[-1]
    local = n // parts
    block = 2 * local * local
    wide = local * n
    phases = 2 * CG_STEPS + 1
    room = block + 8
    slots = 1 + BANDS
    slot_rows = 2 * local * parts
    grid = (4, 4, 2) if parts == 32 else (1, parts, 1)
    operands = [
        wave_coeff.reshape(BANDS, 2, n * local, n),
        local_potential,
        perturbation,
        xc_kernel,
    ] + [jnp.asarray(t) for t in make_tables(n, parts)]
    anywhere = pl.BlockSpec(memory_space=pl.ANY)
    vmem = pl.BlockSpec(memory_space=pltpu.VMEM)
    field = pltpu.VMEM((BANDS, 2, n, wide), f32)
    dma = pltpu.SemaphoreType.DMA
    coeff, density, hxc = pl.pallas_call(
        functools.partial(kernel, n, parts, pools, grid),
        out_shape=(
            jax.ShapeDtypeStruct(operands[0].shape, f32),
            jax.ShapeDtypeStruct((local, n, n), f32),
            jax.ShapeDtypeStruct((local, n, n), f32),
        ),
        in_specs=[anywhere, pl.BlockSpec(memory_space=pltpu.SMEM)] + [anywhere] * 9,
        out_specs=(vmem, vmem, vmem),
        scratch_shapes=[pltpu.VMEM(t.shape, t.dtype) for t in operands]
        + [
            field,
            pltpu.VMEM((n, wide), f32),
            pltpu.VMEM((n, wide), f32),
            field,
            field,
            field,
            field,
            field,
            field,
            pltpu.VMEM((BANDS, n, wide), f32),
            pltpu.VMEM((n, wide), f32),
            pltpu.VMEM((phases, BANDS, parts, room, n), f32),
            pltpu.VMEM((phases, BANDS, parts * room, n), f32),
            pltpu.VMEM((slots, 1, n), f32),
            pltpu.VMEM((slots, parts, 1, n), f32),
            pltpu.VMEM((pools * slot_rows, n), f32),
            pltpu.VMEM((pools * slot_rows, n), f32),
            pltpu.VMEM((2, slot_rows, n), f32),
            pltpu.VMEM((2, pools * slot_rows, n), f32),
            dma((10,)),
            dma((phases, BANDS)),
            dma((phases, BANDS)),
            dma((slots,)),
            dma((slots,)),
            dma((3,)),
            dma((3,)),
        ],
        compiler_params=pltpu.CompilerParams(
            collective_id=0, has_side_effects=True, vmem_limit_bytes=56 * 1024 * 1024
        ),
    )(operands[0], band_energy, *operands[1:])
    results = [coeff, density, hxc]
    coeff, density, hxc = pl.pallas_call(
        hand_over,
        out_shape=[jax.ShapeDtypeStruct(t.shape, f32) for t in results],
        in_specs=[anywhere] * 3,
        out_specs=[anywhere] * 3,
        scratch_shapes=[dma((2 * BANDS + 2,))],
    )(*results)
    return coeff.reshape(wave_coeff.shape), density, hxc


def solution(mesh):
    return jax.shard_map(
        functools.partial(body, parts=mesh.shape["fft"], pools=mesh.shape["pool"]),
        mesh=mesh,
        in_specs=(
            P("pool", None, None, None, "fft", None),
            P("pool", None),
            P("fft", None, None),
            P("fft", None, None),
            P("fft", None, None),
        ),
        out_specs=(
            P("pool", None, None, None, "fft", None),
            P("fft", None, None),
            P("fft", None, None),
        ),
        check_vma=False,
    )
```

```python
import functools
import math

import jax
import jax.numpy as jnp
import ml_dtypes
import numpy as np
from jax import lax
from jax.experimental import pallas as pl
from jax.experimental.pallas import tpu as pltpu
from jax.sharding import PartitionSpec as P

CG_STEPS = 3
BANDS = 2
HALVES = 2
cell_length = 51.3
unit = 2.0 * math.pi / cell_length
MESH = pl.DeviceIdType.MESH
f32 = jnp.float32
bf16 = jnp.bfloat16


def left_table(rows, cols, n, sign, scale=1.0):
    rows, cols = np.array(rows), np.array(cols)
    phase = 2.0 * np.pi * ((rows[:, None, 1] * cols[None, :, 1]) % n) / n
    out_part, in_part = rows[:, None, 0], cols[None, :, 0]
    value = np.where(
        out_part == in_part,
        np.cos(phase),
        np.where(out_part == 1, sign, -sign) * np.sin(phase),
    )
    return value * scale


def split_table(table, axis):
    high = table.astype(ml_dtypes.bfloat16)
    low = (table - high.astype(np.float64)).astype(ml_dtypes.bfloat16)
    return np.concatenate([high, high, low], axis=axis)


def real_basis(n, order):
    k = np.array([f for f, _ in order])
    phase = 2.0 * np.pi * ((k[:, None] * np.arange(n)[None, :]) % n) / n
    is_sin = np.array([s for _, s in order])[:, None]
    rows = np.where(is_sin == 1, np.sin(phase), np.cos(phase))
    weight = np.where((k == 0) | (2 * k == n), 1.0, 2.0)[:, None] / n
    return rows, rows * weight


def make_tables(n, parts):
    local = n // parts
    natural = [(c, j) for c in range(2) for j in range(n)]
    by_owner = [(c, q * local + m) for q in range(parts) for c in range(2) for m in range(local)]
    split = np.array_split(np.arange(local), HALVES)
    by_local = [
        [(c, q * local + m) for c in range(2) for m in ms for q in range(parts)] for ms in split
    ]
    outgoing = np.stack(
        [split_table(left_table(by_owner, natural, n, sign), 1) for sign in (1.0, -1.0)]
    )
    incoming = np.stack(
        [
            np.stack([split_table(left_table(natural, cols, n, sign, size), 1) for cols in by_local])
            for sign, size in ((1.0, 1.0 / n**3), (-1.0, 1.0))
        ]
    )
    right = np.stack(
        [
            split_table(left_table(natural, natural, n, 1.0).T, 0),
            split_table(left_table(natural, natural, n, -1.0).T, 0),
        ]
    )
    half = n // 2
    plain = [(k, 0) for k in range(half + 1)] + [(k, 1) for k in range(1, half)]
    columns = [
        [(2 * p, 0) for p in range(parts)],
        [(half, 0)] + [(2 * p, 1) for p in range(1, parts)],
        [(2 * p + 1, 0) for p in range(parts)],
        [(2 * p + 1, 1) for p in range(parts)],
    ]
    y_rows, y_back = real_basis(n, sum(columns, []))
    rows, back = real_basis(n, plain)
    by_local_x = [q * local + m for m in range(local) for q in range(parts)]
    x_rows = rows[:, by_local_x]
    x_back = np.zeros((parts, 2 * local, n))
    x_back[:, :local] = back.T.reshape(parts, local, n)
    basis_y = np.stack([split_table(y_rows * 2.0 * n**3, 1), split_table(y_back.T, 1)])
    basis_z = np.stack([split_table(rows.T, 0), split_table(back, 0)])
    basis_x = split_table(x_rows, 1)
    spread_x = split_table(x_back.reshape(2 * n, n), 1)
    return [outgoing, right, incoming, basis_y, basis_x, spread_x, basis_z]


def halves(value):
    high = value.astype(bf16)
    low = (value - high.astype(f32)).astype(bf16)
    return high, low


def left_dot(table, data):
    high, low = halves(data)
    return jnp.dot(table, jnp.concatenate([high, low, high], axis=0), preferred_element_type=f32)


def right_dot(data, table):
    high, low = halves(data)
    return jnp.dot(jnp.concatenate([high, low, high], axis=1), table, preferred_element_type=f32)


def kernel(
    n,
    parts,
    pools,
    raw_hbm,
    energy,
    potential_hbm,
    perturbation_hbm,
    xc_hbm,
    outgoing_hbm,
    right_hbm,
    incoming_hbm,
    basis_y_hbm,
    basis_x_hbm,
    spread_x_hbm,
    basis_z_hbm,
    coeff,
    density,
    hxc,
    raw,
    potential,
    perturbation,
    xc,
    outgoing,
    right,
    incoming,
    basis_y,
    basis_x,
    spread_x,
    basis_z,
    wave,
    kin,
    pre,
    resid,
    search,
    answer,
    ahead,
    space_wave,
    space_search,
    overlap,
    total,
    send,
    recv,
    small_send,
    small_recv,
    go_send,
    go_recv,
    back_send,
    back_recv,
    loaded,
    bulk_out,
    bulk_in,
    small_out,
    small_in,
    turn_out,
    turn_in,
):
    local = n // parts
    group = local // HALVES
    block = 2 * local * group
    room = block + 8
    devices = parts * pools
    inverse_total = 1.0 / n**3
    me = lax.axis_index("fft")
    pool = lax.axis_index("pool")
    def lanes(value, index):
        return value[:, index * n : (index + 1) * n]

    def turned(start, shift, size):
        index = start + shift
        return jnp.where(index >= size, index - size, index)

    def for_peers(act):
        def step(shift, _):
            act(turned(me, shift, parts))
            return 0

        lax.fori_loop(parts // 2, parts, step, 0)
        lax.fori_loop(1, parts // 2, step, 0)

    def for_devices(act):
        for pool_shift in (2, 1, 3):
            other_pool = turned(pool, pool_shift, pools)

            def step(shift, _, other_pool=other_pool):
                act(turned(me, shift, parts), other_pool)
                return 0

            lax.fori_loop(parts // 2, parts, step, 0)
            lax.fori_loop(0, parts // 2, step, 0)
        for_peers(lambda other: act(other, pool))

    barrier = pltpu.get_barrier_semaphore()

    def greet(other, other_pool):
        pl.semaphore_signal(
            barrier, inc=1, device_id={"pool": other_pool, "fft": other}, device_id_type=MESH
        )

    for_devices(greet)
    loads = {}
    order = [
        (raw_hbm, raw),
        (right_hbm, right),
        (outgoing_hbm, outgoing),
        (incoming_hbm, incoming),
        (perturbation_hbm, perturbation),
        (potential_hbm, potential),
        (basis_y_hbm, basis_y),
        (basis_x_hbm, basis_x),
        (basis_z_hbm, basis_z),
        (spread_x_hbm, spread_x),
        (xc_hbm, xc),
    ]
    for i, (source, target) in enumerate(order):
        loads[i] = pltpu.make_async_copy(source, target, loaded.at[i])
        loads[i].start()


    def row_half(phase):
        return phase % 2 if phase >= 2 else None

    def used_rows(phase, half):
        return block + 1 if half == row_half(phase) else block

    def store_half(phase, band, half, value, row=None):
        for m in range(group):
            send[phase, band, half, :, 2 * local * m : 2 * local * (m + 1), :] = lanes(
                value, m
            ).reshape(parts, 2 * local, n)
        if half == row_half(phase):
            send[phase, band, half, :, block:room, :] = jnp.broadcast_to(row, (parts, 8, n))

    def start_half(phase, band, half):
        here = pl.multiple_of(me * room, room)
        used = used_rows(phase, half)

        def start(other):
            pltpu.make_async_remote_copy(
                src_ref=send.at[phase, band, half, other, pl.ds(0, used)],
                dst_ref=recv.at[phase, band, half, pl.ds(here, used)],
                send_sem=bulk_out.at[phase, band, half],
                recv_sem=bulk_in.at[phase, band, half],
                device_id={"fft": other},
                device_id_type=MESH,
            ).start()

        for_peers(start)
        recv[phase, band, half, pl.ds(here, room), :] = send[phase, band, half, me]

    def half_bytes(phase, band, half):
        return recv.at[phase, band, half, pl.ds(0, (parts - 1) * used_rows(phase, half))]

    def wait_bytes(ref, sem):
        pltpu.make_async_copy(ref, ref, sem).wait()

    def receive_bulk(phase, band, tables):
        out = None
        for half in range(HALVES):
            wait_bytes(half_bytes(phase, band, half), bulk_in.at[phase, band, half])
            rows = []
            for c in range(2):
                for m in range(group):
                    pieces = []
                    for other in range(local):
                        first = 2 * local * m + local * c + other
                        pieces.append(
                            recv[phase, band, half, pl.ds(first, parts, stride=room), :]
                        )
                    rows.append(jnp.concatenate(pieces, axis=1))
            part = left_dot(tables[half], jnp.concatenate(rows, axis=0))
            out = part if out is None else out + part
        return out

    row_id = lax.broadcasted_iota(jnp.int32, (8, n), 0)
    lane_id = lax.broadcasted_iota(jnp.int32, (8, n), 1)

    def lane_sums(value):
        column = jnp.sum(value, axis=0, keepdims=True)
        result = lanes(column, 0)
        for m in range(1, local):
            result = result + lanes(column, m)
        return result

    def pack(values):
        stacked = jnp.zeros((8, n), f32)
        for i, value in enumerate(values):
            stacked = jnp.where(row_id == i, value, stacked)
        sums = jnp.sum(stacked, axis=1, keepdims=True)
        return jnp.sum(jnp.where(row_id == lane_id, sums, 0.0), axis=0, keepdims=True)

    def unpack(row, count):
        return [
            jnp.sum(jnp.where(lane_id[:1] == i, row, 0.0), axis=1, keepdims=True)
            for i in range(count)
        ]

    def bulk_row(phase, band, count):
        rows = recv[phase, band, row_half(phase), pl.ds(block, parts, stride=room), :]
        return unpack(jnp.sum(rows, axis=0, keepdims=True), count)

    def send_small(slot, values):
        row = pack(values)
        small_send[slot] = row
        small_recv[slot, me] = row

        def start(other):
            pltpu.make_async_remote_copy(
                src_ref=small_send.at[slot],
                dst_ref=small_recv.at[slot, me],
                send_sem=small_out.at[slot],
                recv_sem=small_in.at[slot],
                device_id={"fft": other},
                device_id_type=MESH,
            ).start()

        for_peers(start)

    def receive_small(slot, count):
        wait_bytes(small_recv.at[slot, pl.ds(0, parts - 1)], small_in.at[slot])
        return unpack(jnp.sum(small_recv[slot], axis=0), count)


    def along_z(real, imag, table):
        count = real.shape[1] // n
        rows = jnp.concatenate(
            [jnp.concatenate([lanes(real, m), lanes(imag, m)], axis=1) for m in range(count)],
            axis=0,
        )
        out = right_dot(rows, table)
        picked = [out[m * n : (m + 1) * n] for m in range(count)]
        return (
            jnp.concatenate([lanes(v, 0) for v in picked], axis=1),
            jnp.concatenate([lanes(v, 1) for v in picked], axis=1),
        )

    def half_of(value, half):
        return value[:, half * group * n : (half + 1) * group * n]

    def send_real(phase, band, real, imag, row=None):
        for half in range(HALVES):
            part = jnp.concatenate(
                along_z(half_of(real, half), half_of(imag, half), right[0]), axis=0
            )
            store_half(phase, band, half, left_dot(outgoing[0], part), row)
            if phase == 0 and band == 0 and half == 0:
                pl.semaphore_wait(barrier, devices - 1)
            start_half(phase, band, half)

    def receive_real(phase, band):
        out = receive_bulk(phase, band, incoming[0])
        return out[:n], out[n:]

    def send_reciprocal(phase, band, real, imag, row=None):
        for half in range(HALVES):
            part = jnp.concatenate([half_of(real, half), half_of(imag, half)], axis=0)
            store_half(phase, band, half, left_dot(outgoing[1], part), row)
            start_half(phase, band, half)

    def receive_reciprocal(phase, band):
        out = receive_bulk(phase, band, incoming[1])
        return along_z(out[:n], out[n:], right[1])


    loads[0].wait()
    for band in range(BANDS):
        for c in range(2):
            for m in range(local):
                wave[band, c, :, m * n : (m + 1) * n] = raw[
                    band, c, pl.ds(m, n, stride=local), :
                ]
        if band == 0:
            loads[1].wait()
            loads[2].wait()
        send_real(0, band, wave[band, 0], wave[band, 1])

    def wavenumber(index):
        signed = jnp.where(2 * index >= n, index - n, index)
        return signed.astype(f32) * unit

    def offset(axis_number):
        bit = lax.rem(pool // 2**axis_number, 2)
        return (0.5 * bit.astype(f32) - 0.25) * unit

    index_x = lax.broadcasted_iota(jnp.int32, (n, n), 0)
    index_z = lax.broadcasted_iota(jnp.int32, (n, n), 1)
    square_x = (wavenumber(index_x) + offset(0)) ** 2
    square_z = (wavenumber(index_z) + offset(2)) ** 2
    for m in range(local):
        square_y = (wavenumber(me * local + m) + offset(1)) ** 2
        value = 0.5 * (square_x + square_y + square_z)
        kin[:, m * n : (m + 1) * n] = value
        pre[:, m * n : (m + 1) * n] = 1.0 / (value + 1.0)

    def wide(ref):
        return jnp.concatenate([ref[m] for m in range(local)], axis=1)


    overlaps = []
    for i in range(3, len(order)):
        loads[i].wait()
    for band in range(BANDS):
        real, imag = receive_real(0, band)
        space_wave[band, 0] = real
        space_wave[band, 1] = imag
        change = wide(perturbation)
        changed_real = change * real
        changed_imag = change * imag
        overlaps.append(lane_sums(changed_real * real + changed_imag * imag))
        if band == BANDS - 1:
            first_real = space_wave[0, 0]
            first_imag = space_wave[0, 1]
            overlaps.append(lane_sums(first_real * changed_real + first_imag * changed_imag))
            overlaps.append(lane_sums(first_real * changed_imag - first_imag * changed_real))
            send_small(0, overlaps)
        send_reciprocal(1, band, changed_real, changed_imag)

    def products(band, real, imag):
        sums = []
        for m in range(BANDS):
            sums.append(lane_sums(wave[m, 0] * real + wave[m, 1] * imag))
            sums.append(lane_sums(wave[m, 0] * imag - wave[m, 1] * real))
        return [value * inverse_total for value in sums]

    def kinetic_sum(band, left_real, left_imag, right_real, right_imag):
        shifted = kin[...] - energy[0, band]
        return lane_sums(shifted * (left_real * right_real + left_imag * right_imag)) * inverse_total

    def send_step(phase, band, resid_real, resid_imag):
        real = pre[...] * resid_real
        imag = pre[...] * resid_imag
        row = pack([lane_sums(resid_real * real + resid_imag * imag) * inverse_total])
        resid[band, 0] = resid_real
        resid[band, 1] = resid_imag
        ahead[band, 0] = real
        ahead[band, 1] = imag
        send_real(phase, band, real, imag, row)


    partial = [None] * BANDS
    rho = [None] * BANDS
    for band in range(BANDS):
        real, imag = receive_reciprocal(1, band)
        if band == 0:
            same0, same1, cross_real, cross_imag = receive_small(0, 4)
        if band == 0:
            m0_real, m0_imag, m1_real, m1_imag = same0, 0.0 * same0, cross_real, -cross_imag
        else:
            m0_real, m0_imag, m1_real, m1_imag = cross_real, cross_imag, same1, 0.0 * same1
        resid_real = (
            wave[0, 0] * m0_real
            - wave[0, 1] * m0_imag
            + wave[1, 0] * m1_real
            - wave[1, 1] * m1_imag
            - real
        )
        resid_imag = (
            wave[0, 0] * m0_imag
            + wave[0, 1] * m0_real
            + wave[1, 0] * m1_imag
            + wave[1, 1] * m1_real
            - imag
        )
        send_step(2, band, resid_real, resid_imag)


    step_size = [None] * BANDS

    def finish_curvature(band, values):
        curvature, c0_real, c0_imag, c1_real, c1_imag = values
        curvature = curvature + 2.0 * (
            c0_real * c0_real + c0_imag * c0_imag + c1_real * c1_real + c1_imag * c1_imag
        )
        return rho[band] / curvature

    for step in range(CG_STEPS):
        last = step + 1 == CG_STEPS
        for band in range(BANDS):
            real, imag = ahead[band, 0], ahead[band, 1]
            sums = [kinetic_sum(band, real, imag, real, imag)] + products(band, real, imag)
            if step > 0:
                cross = kinetic_sum(band, real, imag, search[band, 0], search[band, 1])
            real, imag = receive_real(2 + 2 * step, band)
            (rho_new,) = bulk_row(2 + 2 * step, band, 1)
            if step > 0:
                beta = rho_new / rho[band]
                before = partial[band]
                sums[0] = sums[0] + beta * (2.0 * cross + beta * before[0])
                for i in range(1, 1 + 2 * BANDS):
                    sums[i] = sums[i] + beta * before[i]
                real = real + beta * space_search[band, 0]
                imag = imag + beta * space_search[band, 1]
            rho[band] = rho_new
            partial[band] = list(sums)
            if not last:
                space_search[band, 0] = real
                space_search[band, 1] = imag
            level = wide(potential)
            image_real = level * real
            image_imag = level * imag
            sums[0] = sums[0] + lane_sums(image_real * real + image_imag * imag)
            if last:
                send_small(1 + band, sums)
            else:
                send_reciprocal(3 + 2 * step, band, image_real, image_imag, pack(sums))
            overlap[band] = space_wave[band, 0] * real + space_wave[band, 1] * imag
            for c in range(2):
                if step == 0:
                    search[band, c] = ahead[band, c]
                else:
                    search[band, c] = ahead[band, c] + beta * search[band, c]
        if last:
            break
        for band in range(BANDS):
            pot_real, pot_imag = receive_reciprocal(3 + 2 * step, band)
            values = bulk_row(3 + 2 * step, band, 5)
            _, c0_real, c0_imag, c1_real, c1_imag = values
            size = finish_curvature(band, values)
            shifted = kin[...] - energy[0, band]
            real = search[band, 0]
            imag = search[band, 1]
            image_real = (
                shifted * real
                + pot_real
                + 2.0
                * (
                    wave[0, 0] * c0_real
                    - wave[0, 1] * c0_imag
                    + wave[1, 0] * c1_real
                    - wave[1, 1] * c1_imag
                )
            )
            image_imag = (
                shifted * imag
                + pot_imag
                + 2.0
                * (
                    wave[0, 0] * c0_imag
                    + wave[0, 1] * c0_real
                    + wave[1, 0] * c1_imag
                    + wave[1, 1] * c1_real
                )
            )
            send_step(
                4 + 2 * step,
                band,
                resid[band, 0] - size * image_real,
                resid[band, 1] - size * image_imag,
            )
            added = size * overlap[band]
            total[...] = added if step == 0 and band == 0 else total[...] + added
            for c in range(2):
                moved = size * search[band, c]
                answer[band, c] = moved if step == 0 else answer[band, c] + moved


    columns = left_dot(basis_y[0], total[...])
    moved = [left_dot(basis_y[0], overlap[band]) for band in range(BANDS)]
    for band in range(BANDS):
        step_size[band] = finish_curvature(band, receive_small(1 + band, 5))
        columns = columns + step_size[band] * moved[band]

    slot = 2 * local

    def turn(which, source, target, all_columns):
        here = pl.multiple_of((pool * parts + me) * slot, slot)
        own = here if all_columns else pl.multiple_of(me * slot, slot)
        target[pl.ds(here, local), :] = source[pl.ds(own, local), :]

        def start(other, other_pool):
            there = other_pool * parts + other if all_columns else other
            there = pl.multiple_of(there * slot, slot)
            pltpu.make_async_remote_copy(
                src_ref=source.at[pl.ds(there, local)],
                dst_ref=target.at[pl.ds(here, local)],
                send_sem=turn_out.at[which],
                recv_sem=turn_in.at[which],
                device_id={"pool": other_pool, "fft": other},
                device_id_type=MESH,
            ).start()

        for_devices(start)

    def wait_turn(which, target):
        wait_bytes(target.at[pl.ds(0, local * (devices - 1))], turn_in.at[which])

    for m in range(local):
        go_send[pl.ds(m, devices, stride=slot), :] = lanes(columns, m)
    turn(0, go_send, go_recv, True)
    for band in range(BANDS):
        for c in range(2):
            value = answer[band, c] + step_size[band] * search[band, c]
            for m in range(local):
                coeff[band, c, pl.ds(m, n, stride=local), :] = lanes(value, m)

    even = 2 * me
    frequency = jnp.where(
        pool == 0, even, jnp.where(pool == 1, jnp.where(me == 0, n // 2, even), even + 1)
    )

    def plain_square(index):
        k = jnp.where(index > n // 2, index - n // 2, index)
        return (k.astype(f32) * unit) ** 2

    squared = (
        plain_square(index_x) + (frequency.astype(f32) * unit) ** 2 + plain_square(index_z)
    )
    nonzero = (squared > 0).astype(f32)
    coulomb = 4.0 * math.pi * nonzero / (squared + (1.0 - nonzero))

    wait_turn(0, go_recv)
    pieces = []
    for m in range(local):
        piece = go_recv[pl.ds(m, parts, stride=slot), :]
        for other in range(1, pools):
            piece = piece + go_recv[pl.ds(other * parts * slot + m, parts, stride=slot), :]
        back_send[0, pl.ds(m, parts, stride=slot), :] = piece
        pieces.append(piece)
    turn(1, back_send.at[0], back_recv.at[0], False)


    field = left_dot(basis_x[...], jnp.concatenate(pieces, axis=0))
    field = coulomb * right_dot(field, basis_z[0])
    field = left_dot(spread_x[...], right_dot(field, basis_z[1]))
    back_send[1] = field
    turn(2, back_send.at[1], back_recv.at[1], False)

    for i, result in enumerate((density, hxc)):
        wait_turn(1 + i, back_recv.at[i])
        columns = [back_recv[i, pl.ds(m, devices, stride=slot), :] for m in range(local)]
        whole = left_dot(basis_y[1], jnp.concatenate(columns, axis=1))
        for m in range(local):
            if i == 0:
                result[m] = lanes(whole, m)
            else:
                result[m] = lanes(whole, m) + xc[m] * density[m]


    for phase in range(2 * CG_STEPS + 1):
        for band in range(BANDS):
            for half in range(HALVES):
                wait_bytes(half_bytes(phase, band, half), bulk_out.at[phase, band, half])
    for slot in range(1 + BANDS):
        wait_bytes(small_recv.at[slot, pl.ds(0, parts - 1)], small_out.at[slot])
    for which in range(3):
        wait_bytes(go_recv.at[pl.ds(0, local * (devices - 1))], turn_out.at[which])


def hand_over(coeff, density, hxc, coeff_out, density_out, hxc_out, *scratch):
    held, held_density, held_hxc, came, gone = scratch
    moves = [(density, held_density, density_out), (hxc, held_hxc, hxc_out)]
    for b in range(BANDS):
        for c in range(2):
            moves.append((coeff.at[b, c], held.at[b, c], coeff_out.at[b, c]))
    first = [pltpu.make_async_copy(a, h, came.at[i]) for i, (a, h, _) in enumerate(moves)]
    second = [pltpu.make_async_copy(h, o, gone.at[i]) for i, (_, h, o) in enumerate(moves)]
    for copy in first:
        copy.start()
    for copy, onward in zip(first, second):
        copy.wait()
        onward.start()
    for copy in second:
        copy.wait()


def body(wave_coeff, band_energy, local_potential, perturbation, xc_kernel, parts, pools):
    n = wave_coeff.shape[-1]
    local = n // parts
    block = 2 * local * (local // HALVES)
    wide = local * n
    phases = 2 * CG_STEPS + 1
    room = block + 8
    slots = 1 + BANDS
    slot_rows = 2 * local * parts
    operands = [
        wave_coeff.reshape(BANDS, 2, n * local, n),
        local_potential,
        perturbation,
        xc_kernel,
    ] + [jnp.asarray(t) for t in make_tables(n, parts)]
    anywhere = pl.BlockSpec(memory_space=pl.ANY)
    vmem = pl.BlockSpec(memory_space=pltpu.VMEM)
    field = pltpu.VMEM((BANDS, 2, n, wide), f32)
    dma = pltpu.SemaphoreType.DMA
    coeff, density, hxc = pl.pallas_call(
        functools.partial(kernel, n, parts, pools),
        out_shape=(
            jax.ShapeDtypeStruct(operands[0].shape, f32),
            jax.ShapeDtypeStruct((local, n, n), f32),
            jax.ShapeDtypeStruct((local, n, n), f32),
        ),
        in_specs=[anywhere, pl.BlockSpec(memory_space=pltpu.SMEM)] + [anywhere] * 10,
        out_specs=(vmem, vmem, vmem),
        scratch_shapes=[pltpu.VMEM(t.shape, t.dtype) for t in operands]
        + [
            field,
            pltpu.VMEM((n, wide), f32),
            pltpu.VMEM((n, wide), f32),
            field,
            field,
            field,
            field,
            field,
            field,
            pltpu.VMEM((BANDS, n, wide), f32),
            pltpu.VMEM((n, wide), f32),
            pltpu.VMEM((phases, BANDS, HALVES, parts, room, n), f32),
            pltpu.VMEM((phases, BANDS, HALVES, parts * room, n), f32),
            pltpu.VMEM((slots, 1, n), f32),
            pltpu.VMEM((slots, parts, 1, n), f32),
            pltpu.VMEM((pools * slot_rows, n), f32),
            pltpu.VMEM((pools * slot_rows, n), f32),
            pltpu.VMEM((2, slot_rows, n), f32),
            pltpu.VMEM((2, pools * slot_rows, n), f32),
            dma((11,)),
            dma((phases, BANDS, HALVES)),
            dma((phases, BANDS, HALVES)),
            dma((slots,)),
            dma((slots,)),
            dma((3,)),
            dma((3,)),
        ],
        compiler_params=pltpu.CompilerParams(
            collective_id=0, has_side_effects=True, vmem_limit_bytes=56 * 1024 * 1024
        ),
    )(operands[0], band_energy, *operands[1:])
    results = [coeff, density, hxc]
    coeff, density, hxc = pl.pallas_call(
        hand_over,
        out_shape=[jax.ShapeDtypeStruct(t.shape, f32) for t in results],
        in_specs=[anywhere] * 3,
        out_specs=[anywhere] * 3,
        scratch_shapes=[pltpu.VMEM(t.shape, f32) for t in results]
        + [dma((2 * BANDS + 2,)), dma((2 * BANDS + 2,))],
    )(*results)
    return coeff.reshape(wave_coeff.shape), density, hxc


def solution(mesh):
    return jax.shard_map(
        functools.partial(body, parts=mesh.shape["fft"], pools=mesh.shape["pool"]),
        mesh=mesh,
        in_specs=(
            P("pool", None, None, None, "fft", None),
            P("pool", None),
            P("fft", None, None),
            P("fft", None, None),
            P("fft", None, None),
        ),
        out_specs=(
            P("pool", None, None, None, "fft", None),
            P("fft", None, None),
            P("fft", None, None),
        ),
        check_vma=False,
    )
```

```python
import functools
import math

import jax
import jax.numpy as jnp
import ml_dtypes
import numpy as np
from jax import lax
from jax.experimental import pallas as pl
from jax.experimental.pallas import tpu as pltpu
from jax.sharding import PartitionSpec as P

CG_STEPS = 3
BANDS = 2
HALVES = 2
cell_length = 51.3
unit = 2.0 * math.pi / cell_length
MESH = pl.DeviceIdType.MESH
f32 = jnp.float32
bf16 = jnp.bfloat16


def left_table(rows, cols, n, sign, scale=1.0):
    rows, cols = np.array(rows), np.array(cols)
    phase = 2.0 * np.pi * ((rows[:, None, 1] * cols[None, :, 1]) % n) / n
    out_part, in_part = rows[:, None, 0], cols[None, :, 0]
    value = np.where(
        out_part == in_part,
        np.cos(phase),
        np.where(out_part == 1, sign, -sign) * np.sin(phase),
    )
    return value * scale


def split_table(table, axis):
    high = table.astype(ml_dtypes.bfloat16)
    low = (table - high.astype(np.float64)).astype(ml_dtypes.bfloat16)
    return np.concatenate([high, high, low], axis=axis)


def real_basis(n, order):
    k = np.array([f for f, _ in order])
    phase = 2.0 * np.pi * ((k[:, None] * np.arange(n)[None, :]) % n) / n
    is_sin = np.array([s for _, s in order])[:, None]
    rows = np.where(is_sin == 1, np.sin(phase), np.cos(phase))
    weight = np.where((k == 0) | (2 * k == n), 1.0, 2.0)[:, None] / n
    return rows, rows * weight


def make_tables(n, parts):
    local = n // parts
    natural = [(c, j) for c in range(2) for j in range(n)]
    by_owner = [(c, q * local + m) for q in range(parts) for c in range(2) for m in range(local)]
    split = np.array_split(np.arange(local), HALVES)
    by_local = [
        [(c, q * local + m) for c in range(2) for m in ms for q in range(parts)] for ms in split
    ]
    outgoing = np.stack(
        [split_table(left_table(by_owner, natural, n, sign), 1) for sign in (1.0, -1.0)]
    )
    incoming = np.stack(
        [
            np.stack([split_table(left_table(natural, cols, n, sign, size), 1) for cols in by_local])
            for sign, size in ((1.0, 1.0 / n**3), (-1.0, 1.0))
        ]
    )
    right = np.stack(
        [
            split_table(left_table(natural, natural, n, 1.0).T, 0),
            split_table(left_table(natural, natural, n, -1.0).T, 0),
        ]
    )
    half = n // 2
    plain = [(k, 0) for k in range(half + 1)] + [(k, 1) for k in range(1, half)]
    columns = [
        [(2 * p, 0) for p in range(parts)],
        [(half, 0)] + [(2 * p, 1) for p in range(1, parts)],
        [(2 * p + 1, 0) for p in range(parts)],
        [(2 * p + 1, 1) for p in range(parts)],
    ]
    y_rows, y_back = real_basis(n, sum(columns, []))
    rows, back = real_basis(n, plain)
    by_local_x = [q * local + m for m in range(local) for q in range(parts)]
    x_rows = rows[:, by_local_x]
    x_back = np.zeros((parts, 2 * local, n))
    x_back[:, :local] = back.T.reshape(parts, local, n)
    basis_y = np.stack([split_table(y_rows * 2.0 * n**3, 1), split_table(y_back.T, 1)])
    basis_z = np.stack([split_table(rows.T, 0), split_table(back, 0)])
    basis_x = split_table(x_rows, 1)
    spread_x = split_table(x_back.reshape(2 * n, n), 1)
    return [outgoing, right, incoming, basis_y, basis_x, spread_x, basis_z]


def halves(value):
    high = value.astype(bf16)
    low = (value - high.astype(f32)).astype(bf16)
    return high, low


def left_dot(table, data):
    high, low = halves(data)
    return jnp.dot(table, jnp.concatenate([high, low, high], axis=0), preferred_element_type=f32)


def right_dot(data, table):
    high, low = halves(data)
    return jnp.dot(jnp.concatenate([high, low, high], axis=1), table, preferred_element_type=f32)


def kernel(
    n,
    parts,
    pools,
    raw_hbm,
    energy,
    potential_hbm,
    perturbation_hbm,
    xc_hbm,
    outgoing_hbm,
    right_hbm,
    incoming_hbm,
    basis_y_hbm,
    basis_x_hbm,
    spread_x_hbm,
    basis_z_hbm,
    coeff,
    density,
    hxc,
    raw,
    potential,
    perturbation,
    xc,
    outgoing,
    right,
    incoming,
    basis_y,
    basis_x,
    spread_x,
    basis_z,
    wave,
    kin,
    pre,
    resid,
    search,
    answer,
    ahead,
    space_wave,
    space_search,
    overlap,
    total,
    send,
    recv,
    small_send,
    small_recv,
    go_send,
    go_recv,
    back_send,
    back_recv,
    loaded,
    bulk_out,
    bulk_in,
    small_out,
    small_in,
    turn_out,
    turn_in,
    met,
):
    local = n // parts
    group = local // HALVES
    block = 2 * local * group
    room = block + 8
    devices = parts * pools
    inverse_total = 1.0 / n**3
    me = lax.axis_index("fft")
    pool = lax.axis_index("pool")
    def lanes(value, index):
        return value[:, index * n : (index + 1) * n]

    def turned(start, shift, size):
        index = start + shift
        return jnp.where(index >= size, index - size, index)

    def for_peers(act):
        def step(shift, _):
            act(turned(me, shift, parts))
            return 0

        lax.fori_loop(parts // 2, parts, step, 0)
        lax.fori_loop(1, parts // 2, step, 0)

    def for_devices(act):
        for pool_shift in (2, 1, 3):
            other_pool = turned(pool, pool_shift, pools)

            def step(shift, _, other_pool=other_pool):
                act(turned(me, shift, parts), other_pool)
                return 0

            lax.fori_loop(parts // 2, parts, step, 0)
            lax.fori_loop(0, parts // 2, step, 0)
        for_peers(lambda other: act(other, pool))

    barrier = pltpu.get_barrier_semaphore()

    def greet(other, other_pool):
        pl.semaphore_signal(
            barrier, inc=1, device_id={"pool": other_pool, "fft": other}, device_id_type=MESH
        )

    for_peers(lambda other: greet(other, pool))
    for pool_shift in range(1, pools):
        greet(me, turned(pool, pool_shift, pools))
    loads = {}
    order = [
        (raw_hbm, raw),
        (right_hbm, right),
        (outgoing_hbm, outgoing),
        (incoming_hbm, incoming),
        (perturbation_hbm, perturbation),
        (potential_hbm, potential),
        (basis_y_hbm, basis_y),
        (basis_x_hbm, basis_x),
        (basis_z_hbm, basis_z),
        (spread_x_hbm, spread_x),
        (xc_hbm, xc),
    ]
    for i, (source, target) in enumerate(order):
        loads[i] = pltpu.make_async_copy(source, target, loaded.at[i])
        loads[i].start()


    def row_half(phase):
        return phase % 2 if phase >= 2 else None

    def used_rows(phase, half):
        return block + 1 if half == row_half(phase) else block

    def store_half(phase, band, half, value, row=None):
        for m in range(group):
            send[phase, band, half, :, 2 * local * m : 2 * local * (m + 1), :] = lanes(
                value, m
            ).reshape(parts, 2 * local, n)
        if half == row_half(phase):
            send[phase, band, half, :, block:room, :] = jnp.broadcast_to(row, (parts, 8, n))

    def start_half(phase, band, half):
        here = pl.multiple_of(me * room, room)
        used = used_rows(phase, half)

        def start(other):
            pltpu.make_async_remote_copy(
                src_ref=send.at[phase, band, half, other, pl.ds(0, used)],
                dst_ref=recv.at[phase, band, half, pl.ds(here, used)],
                send_sem=bulk_out.at[phase, band, half],
                recv_sem=bulk_in.at[phase, band, half],
                device_id={"fft": other},
                device_id_type=MESH,
            ).start()

        for_peers(start)
        recv[phase, band, half, pl.ds(here, room), :] = send[phase, band, half, me]

    def half_bytes(phase, band, half):
        return recv.at[phase, band, half, pl.ds(0, (parts - 1) * used_rows(phase, half))]

    def wait_bytes(ref, sem):
        pltpu.make_async_copy(ref, ref, sem).wait()

    def receive_bulk(phase, band, tables):
        out = None
        for half in range(HALVES):
            wait_bytes(half_bytes(phase, band, half), bulk_in.at[phase, band, half])
            rows = []
            for c in range(2):
                for m in range(group):
                    pieces = []
                    for other in range(local):
                        first = 2 * local * m + local * c + other
                        pieces.append(
                            recv[phase, band, half, pl.ds(first, parts, stride=room), :]
                        )
                    rows.append(jnp.concatenate(pieces, axis=1))
            part = left_dot(tables[half], jnp.concatenate(rows, axis=0))
            out = part if out is None else out + part
        return out

    row_id = lax.broadcasted_iota(jnp.int32, (8, n), 0)
    lane_id = lax.broadcasted_iota(jnp.int32, (8, n), 1)

    def lane_sums(value):
        column = jnp.sum(value, axis=0, keepdims=True)
        result = lanes(column, 0)
        for m in range(1, local):
            result = result + lanes(column, m)
        return result

    def pack(values):
        stacked = jnp.zeros((8, n), f32)
        for i, value in enumerate(values):
            stacked = jnp.where(row_id == i, value, stacked)
        sums = jnp.sum(stacked, axis=1, keepdims=True)
        return jnp.sum(jnp.where(row_id == lane_id, sums, 0.0), axis=0, keepdims=True)

    def unpack(row, count):
        return [
            jnp.sum(jnp.where(lane_id[:1] == i, row, 0.0), axis=1, keepdims=True)
            for i in range(count)
        ]

    def bulk_row(phase, band, count):
        rows = recv[phase, band, row_half(phase), pl.ds(block, parts, stride=room), :]
        return unpack(jnp.sum(rows, axis=0, keepdims=True), count)

    def send_small(slot, values):
        row = pack(values)
        small_send[slot] = row
        small_recv[slot, me] = row

        def start(other):
            pltpu.make_async_remote_copy(
                src_ref=small_send.at[slot],
                dst_ref=small_recv.at[slot, me],
                send_sem=small_out.at[slot],
                recv_sem=small_in.at[slot],
                device_id={"fft": other},
                device_id_type=MESH,
            ).start()

        for_peers(start)

    def receive_small(slot, count):
        wait_bytes(small_recv.at[slot, pl.ds(0, parts - 1)], small_in.at[slot])
        return unpack(jnp.sum(small_recv[slot], axis=0), count)


    def along_z(real, imag, table):
        count = real.shape[1] // n
        rows = jnp.concatenate(
            [jnp.concatenate([lanes(real, m), lanes(imag, m)], axis=1) for m in range(count)],
            axis=0,
        )
        out = right_dot(rows, table)
        picked = [out[m * n : (m + 1) * n] for m in range(count)]
        return (
            jnp.concatenate([lanes(v, 0) for v in picked], axis=1),
            jnp.concatenate([lanes(v, 1) for v in picked], axis=1),
        )

    def half_of(value, half):
        return value[:, half * group * n : (half + 1) * group * n]

    def send_real(phase, band, real, imag, row=None):
        for half in range(HALVES):
            part = jnp.concatenate(
                along_z(half_of(real, half), half_of(imag, half), right[0]), axis=0
            )
            store_half(phase, band, half, left_dot(outgoing[0], part), row)
            if phase == 0 and band == 0 and half == 0:
                pl.semaphore_wait(barrier, parts + pools - 2)
            start_half(phase, band, half)

    def receive_real(phase, band):
        out = receive_bulk(phase, band, incoming[0])
        return out[:n], out[n:]

    def send_reciprocal(phase, band, real, imag, row=None):
        for half in range(HALVES):
            part = jnp.concatenate([half_of(real, half), half_of(imag, half)], axis=0)
            store_half(phase, band, half, left_dot(outgoing[1], part), row)
            start_half(phase, band, half)

    def receive_reciprocal(phase, band):
        out = receive_bulk(phase, band, incoming[1])
        return along_z(out[:n], out[n:], right[1])


    loads[0].wait()
    for band in range(BANDS):
        for c in range(2):
            for m in range(local):
                wave[band, c, :, m * n : (m + 1) * n] = raw[
                    band, c, pl.ds(m, n, stride=local), :
                ]
        if band == 0:
            loads[1].wait()
            loads[2].wait()
        send_real(0, band, wave[band, 0], wave[band, 1])

    for pool_shift in range(1, pools):
        pl.semaphore_signal(
            met,
            inc=1,
            device_id={"pool": turned(pool, pool_shift, pools), "fft": me},
            device_id_type=MESH,
        )

    def wavenumber(index):
        signed = jnp.where(2 * index >= n, index - n, index)
        return signed.astype(f32) * unit

    def offset(axis_number):
        bit = lax.rem(pool // 2**axis_number, 2)
        return (0.5 * bit.astype(f32) - 0.25) * unit

    index_x = lax.broadcasted_iota(jnp.int32, (n, n), 0)
    index_z = lax.broadcasted_iota(jnp.int32, (n, n), 1)
    square_x = (wavenumber(index_x) + offset(0)) ** 2
    square_z = (wavenumber(index_z) + offset(2)) ** 2
    for m in range(local):
        square_y = (wavenumber(me * local + m) + offset(1)) ** 2
        value = 0.5 * (square_x + square_y + square_z)
        kin[:, m * n : (m + 1) * n] = value
        pre[:, m * n : (m + 1) * n] = 1.0 / (value + 1.0)

    def wide(ref):
        return jnp.concatenate([ref[m] for m in range(local)], axis=1)


    overlaps = []
    for i in range(3, len(order)):
        loads[i].wait()
    for band in range(BANDS):
        real, imag = receive_real(0, band)
        space_wave[band, 0] = real
        space_wave[band, 1] = imag
        change = wide(perturbation)
        changed_real = change * real
        changed_imag = change * imag
        overlaps.append(lane_sums(changed_real * real + changed_imag * imag))
        if band == BANDS - 1:
            first_real = space_wave[0, 0]
            first_imag = space_wave[0, 1]
            overlaps.append(lane_sums(first_real * changed_real + first_imag * changed_imag))
            overlaps.append(lane_sums(first_real * changed_imag - first_imag * changed_real))
            send_small(0, overlaps)
        send_reciprocal(1, band, changed_real, changed_imag)

    def products(band, real, imag):
        sums = []
        for m in range(BANDS):
            sums.append(lane_sums(wave[m, 0] * real + wave[m, 1] * imag))
            sums.append(lane_sums(wave[m, 0] * imag - wave[m, 1] * real))
        return [value * inverse_total for value in sums]

    def kinetic_sum(band, left_real, left_imag, right_real, right_imag):
        shifted = kin[...] - energy[0, band]
        return lane_sums(shifted * (left_real * right_real + left_imag * right_imag)) * inverse_total

    def send_step(phase, band, resid_real, resid_imag):
        real = pre[...] * resid_real
        imag = pre[...] * resid_imag
        row = pack([lane_sums(resid_real * real + resid_imag * imag) * inverse_total])
        resid[band, 0] = resid_real
        resid[band, 1] = resid_imag
        ahead[band, 0] = real
        ahead[band, 1] = imag
        send_real(phase, band, real, imag, row)


    partial = [None] * BANDS
    rho = [None] * BANDS
    for band in range(BANDS):
        real, imag = receive_reciprocal(1, band)
        if band == 0:
            same0, same1, cross_real, cross_imag = receive_small(0, 4)
        if band == 0:
            m0_real, m0_imag, m1_real, m1_imag = same0, 0.0 * same0, cross_real, -cross_imag
        else:
            m0_real, m0_imag, m1_real, m1_imag = cross_real, cross_imag, same1, 0.0 * same1
        resid_real = (
            wave[0, 0] * m0_real
            - wave[0, 1] * m0_imag
            + wave[1, 0] * m1_real
            - wave[1, 1] * m1_imag
            - real
        )
        resid_imag = (
            wave[0, 0] * m0_imag
            + wave[0, 1] * m0_real
            + wave[1, 0] * m1_imag
            + wave[1, 1] * m1_real
            - imag
        )
        send_step(2, band, resid_real, resid_imag)


    step_size = [None] * BANDS

    def finish_curvature(product, values):
        curvature, c0_real, c0_imag, c1_real, c1_imag = values
        curvature = curvature + 2.0 * (
            c0_real * c0_real + c0_imag * c0_imag + c1_real * c1_real + c1_imag * c1_imag
        )
        return product / curvature

    for step in range(CG_STEPS):
        last = step + 1 == CG_STEPS
        for band in range(BANDS):
            real, imag = ahead[band, 0], ahead[band, 1]
            sums = [kinetic_sum(band, real, imag, real, imag)] + products(band, real, imag)
            if step > 0:
                cross = kinetic_sum(band, real, imag, search[band, 0], search[band, 1])
            real, imag = receive_real(2 + 2 * step, band)
            (rho_new,) = bulk_row(2 + 2 * step, band, 1)
            if step > 0:
                beta = rho_new / rho[band]
                before = partial[band]
                sums[0] = sums[0] + beta * (2.0 * cross + beta * before[0])
                for i in range(1, 1 + 2 * BANDS):
                    sums[i] = sums[i] + beta * before[i]
                real = real + beta * space_search[band, 0]
                imag = imag + beta * space_search[band, 1]
            rho[band] = rho_new
            partial[band] = list(sums)
            if not last:
                space_search[band, 0] = real
                space_search[band, 1] = imag
            level = wide(potential)
            image_real = level * real
            image_imag = level * imag
            sums[0] = sums[0] + lane_sums(image_real * real + image_imag * imag)
            if last and band + 1 < BANDS:
                send_small(1 + band, sums)
            if not last:
                send_reciprocal(3 + 2 * step, band, image_real, image_imag, pack(sums))
            overlap[band] = space_wave[band, 0] * real + space_wave[band, 1] * imag
            for c in range(2):
                if step == 0:
                    search[band, c] = ahead[band, c]
                else:
                    search[band, c] = ahead[band, c] + beta * search[band, c]
            if last and band == 0:
                base = left_dot(basis_y[0], total[...])
                moved = left_dot(basis_y[0], overlap[band])
        if last:
            break
        for band in range(BANDS):
            pot_real, pot_imag = receive_reciprocal(3 + 2 * step, band)
            values = bulk_row(3 + 2 * step, band, 5)
            _, c0_real, c0_imag, c1_real, c1_imag = values
            size = finish_curvature(rho[band], values)
            shifted = kin[...] - energy[0, band]
            real = search[band, 0]
            imag = search[band, 1]
            image_real = (
                shifted * real
                + pot_real
                + 2.0
                * (
                    wave[0, 0] * c0_real
                    - wave[0, 1] * c0_imag
                    + wave[1, 0] * c1_real
                    - wave[1, 1] * c1_imag
                )
            )
            image_imag = (
                shifted * imag
                + pot_imag
                + 2.0
                * (
                    wave[0, 0] * c0_imag
                    + wave[0, 1] * c0_real
                    + wave[1, 0] * c1_imag
                    + wave[1, 1] * c1_real
                )
            )
            send_step(
                4 + 2 * step,
                band,
                resid[band, 0] - size * image_real,
                resid[band, 1] - size * image_imag,
            )
            added = size * overlap[band]
            total[...] = added if step == 0 and band == 0 else total[...] + added
            for c in range(2):
                moved = size * search[band, c]
                answer[band, c] = moved if step == 0 else answer[band, c] + moved


    slot = 2 * local

    def turn(which, source, target, all_columns, rows=local):
        here = pl.multiple_of((pool * parts + me) * slot, slot)
        own = here if all_columns else pl.multiple_of(me * slot, slot)
        target[pl.ds(here, rows), :] = source[pl.ds(own, rows), :]

        def start(other, other_pool):
            there = other_pool * parts + other if all_columns else other
            there = pl.multiple_of(there * slot, slot)
            pltpu.make_async_remote_copy(
                src_ref=source.at[pl.ds(there, rows)],
                dst_ref=target.at[pl.ds(here, rows)],
                send_sem=turn_out.at[which],
                recv_sem=turn_in.at[which],
                device_id={"pool": other_pool, "fft": other},
                device_id_type=MESH,
            ).start()

        for_devices(start)

    def wait_turn(which, target, rows=local):
        wait_bytes(target.at[pl.ds(0, rows * (devices - 1))], turn_in.at[which])

    pl.semaphore_wait(met, pools - 1)
    step_size[0] = finish_curvature(rho[0], receive_small(1, 5))
    columns = base + step_size[0] * moved
    for m in range(local):
        go_send[0, pl.ds(m, devices, stride=slot), :] = lanes(columns, m)
    turn(0, go_send.at[0], go_recv.at[0], True)
    columns = left_dot(basis_y[0], overlap[1])
    for m in range(local):
        go_send[1, pl.ds(m, devices, stride=slot), :] = lanes(columns, m)
    share = jnp.where(lane_id[:1] == 0, rho[1] * (1.0 / parts), 0.0)
    go_send[1, pl.ds(local, devices, stride=slot), :] = jnp.broadcast_to(
        pack(sums + [share]), (devices, n)
    )
    turn(1, go_send.at[1], go_recv.at[1], True, local + 1)

    even = 2 * me
    frequency = jnp.where(
        pool == 0, even, jnp.where(pool == 1, jnp.where(me == 0, n // 2, even), even + 1)
    )

    def plain_square(index):
        k = jnp.where(index > n // 2, index - n // 2, index)
        return (k.astype(f32) * unit) ** 2

    squared = (
        plain_square(index_x) + (frequency.astype(f32) * unit) ** 2 + plain_square(index_z)
    )
    nonzero = (squared > 0).astype(f32)
    coulomb = 4.0 * math.pi * nonzero / (squared + (1.0 - nonzero))

    wait_turn(0, go_recv.at[0])
    wait_turn(1, go_recv.at[1], local + 1)
    sizes = []
    for other in range(pools):
        first = other * parts * slot + local
        rows = go_recv[1, pl.ds(first, parts, stride=slot), :]
        values = unpack(jnp.sum(rows, axis=0, keepdims=True), 6)
        sizes.append(finish_curvature(values[5], values[:5]))
    pieces = []
    for m in range(local):
        piece = None
        for other in range(pools):
            rows = pl.ds(other * parts * slot + m, parts, stride=slot)
            term = go_recv[0, rows, :] + sizes[other] * go_recv[1, rows, :]
            piece = term if piece is None else piece + term
        back_send[0, pl.ds(m, parts, stride=slot), :] = piece
        pieces.append(piece)
    turn(2, back_send.at[0], back_recv.at[0], False)


    field = left_dot(basis_x[...], jnp.concatenate(pieces, axis=0))
    field = coulomb * right_dot(field, basis_z[0])
    field = left_dot(spread_x[...], right_dot(field, basis_z[1]))
    back_send[1] = field
    turn(3, back_send.at[1], back_recv.at[1], False)

    step_size[1] = sum(jnp.where(pool == i, sizes[i], 0.0) for i in range(pools))
    for band in range(BANDS):
        for c in range(2):
            value = answer[band, c] + step_size[band] * search[band, c]
            for m in range(local):
                coeff[band, c, pl.ds(m, n, stride=local), :] = lanes(value, m)

    for i, result in enumerate((density, hxc)):
        wait_turn(2 + i, back_recv.at[i])
        columns = [back_recv[i, pl.ds(m, devices, stride=slot), :] for m in range(local)]
        whole = left_dot(basis_y[1], jnp.concatenate(columns, axis=1))
        for m in range(local):
            if i == 0:
                result[m] = lanes(whole, m)
            else:
                result[m] = lanes(whole, m) + xc[m] * density[m]


    for phase in range(2 * CG_STEPS + 1):
        for band in range(BANDS):
            for half in range(HALVES):
                wait_bytes(half_bytes(phase, band, half), bulk_out.at[phase, band, half])
    for slot in range(BANDS):
        wait_bytes(small_recv.at[slot, pl.ds(0, parts - 1)], small_out.at[slot])
    for which in range(4):
        rows = local + 1 if which == 1 else local
        wait_bytes(go_recv.at[0, pl.ds(0, rows * (devices - 1))], turn_out.at[which])


def hand_over(coeff, density, hxc, coeff_out, density_out, hxc_out, gone):
    moves = [(density, density_out), (hxc, hxc_out)]
    moves += [(coeff.at[b, c], coeff_out.at[b, c]) for b in range(BANDS) for c in range(2)]
    copies = [pltpu.make_async_copy(a, b, gone.at[i]) for i, (a, b) in enumerate(moves)]
    for copy in copies:
        copy.start()
    for copy in copies:
        copy.wait()


def body(wave_coeff, band_energy, local_potential, perturbation, xc_kernel, parts, pools):
    n = wave_coeff.shape[-1]
    local = n // parts
    block = 2 * local * (local // HALVES)
    wide = local * n
    phases = 2 * CG_STEPS + 1
    room = block + 8
    slots = BANDS
    slot_rows = 2 * local * parts
    operands = [
        wave_coeff.reshape(BANDS, 2, n * local, n),
        local_potential,
        perturbation,
        xc_kernel,
    ] + [jnp.asarray(t) for t in make_tables(n, parts)]
    anywhere = pl.BlockSpec(memory_space=pl.ANY)
    vmem = pl.BlockSpec(memory_space=pltpu.VMEM)
    field = pltpu.VMEM((BANDS, 2, n, wide), f32)
    dma = pltpu.SemaphoreType.DMA
    coeff, density, hxc = pl.pallas_call(
        functools.partial(kernel, n, parts, pools),
        out_shape=(
            pltpu.VMEM(operands[0].shape, f32),
            pltpu.VMEM((local, n, n), f32),
            pltpu.VMEM((local, n, n), f32),
        ),
        in_specs=[anywhere, pl.BlockSpec(memory_space=pltpu.SMEM)] + [anywhere] * 10,
        out_specs=(vmem, vmem, vmem),
        scratch_shapes=[pltpu.VMEM(t.shape, t.dtype) for t in operands]
        + [
            field,
            pltpu.VMEM((n, wide), f32),
            pltpu.VMEM((n, wide), f32),
            field,
            field,
            field,
            field,
            field,
            field,
            pltpu.VMEM((BANDS, n, wide), f32),
            pltpu.VMEM((n, wide), f32),
            pltpu.VMEM((phases, BANDS, HALVES, parts, room, n), f32),
            pltpu.VMEM((phases, BANDS, HALVES, parts * room, n), f32),
            pltpu.VMEM((slots, 1, n), f32),
            pltpu.VMEM((slots, parts, 1, n), f32),
            pltpu.VMEM((2, pools * slot_rows, n), f32),
            pltpu.VMEM((2, pools * slot_rows, n), f32),
            pltpu.VMEM((2, slot_rows, n), f32),
            pltpu.VMEM((2, pools * slot_rows, n), f32),
            dma((11,)),
            dma((phases, BANDS, HALVES)),
            dma((phases, BANDS, HALVES)),
            dma((slots,)),
            dma((slots,)),
            dma((4,)),
            dma((4,)),
            pltpu.SemaphoreType.REGULAR,
        ],
        compiler_params=pltpu.CompilerParams(
            collective_id=0, has_side_effects=True, vmem_limit_bytes=56 * 1024 * 1024
        ),
    )(operands[0], band_energy, *operands[1:])
    results = [coeff, density, hxc]
    coeff, density, hxc = pl.pallas_call(
        hand_over,
        out_shape=[jax.ShapeDtypeStruct(t.shape, f32) for t in results],
        in_specs=[vmem] * 3,
        out_specs=[anywhere] * 3,
        scratch_shapes=[dma((2 * BANDS + 2,))],
    )(*results)
    return coeff.reshape(wave_coeff.shape), density, hxc


def solution(mesh):
    return jax.shard_map(
        functools.partial(body, parts=mesh.shape["fft"], pools=mesh.shape["pool"]),
        mesh=mesh,
        in_specs=(
            P("pool", None, None, None, "fft", None),
            P("pool", None),
            P("fft", None, None),
            P("fft", None, None),
            P("fft", None, None),
        ),
        out_specs=(
            P("pool", None, None, None, "fft", None),
            P("fft", None, None),
            P("fft", None, None),
        ),
        check_vma=False,
    )
```

```python
import functools
import math

import jax
import jax.numpy as jnp
import ml_dtypes
import numpy as np
from jax import lax
from jax.experimental import pallas as pl
from jax.experimental.pallas import tpu as pltpu
from jax.sharding import PartitionSpec as P

CG_STEPS = 3
BANDS = 2
HALVES = 2
cell_length = 51.3
unit = 2.0 * math.pi / cell_length
MESH = pl.DeviceIdType.MESH
f32 = jnp.float32
bf16 = jnp.bfloat16


def left_table(rows, cols, n, sign, scale=1.0):
    rows, cols = np.array(rows), np.array(cols)
    phase = 2.0 * np.pi * ((rows[:, None, 1] * cols[None, :, 1]) % n) / n
    out_part, in_part = rows[:, None, 0], cols[None, :, 0]
    value = np.where(
        out_part == in_part,
        np.cos(phase),
        np.where(out_part == 1, sign, -sign) * np.sin(phase),
    )
    return value * scale


def split_table(table, axis):
    high = table.astype(ml_dtypes.bfloat16)
    low = (table - high.astype(np.float64)).astype(ml_dtypes.bfloat16)
    return np.concatenate([high, high, low], axis=axis)


def real_basis(n, order):
    k = np.array([f for f, _ in order])
    phase = 2.0 * np.pi * ((k[:, None] * np.arange(n)[None, :]) % n) / n
    is_sin = np.array([s for _, s in order])[:, None]
    rows = np.where(is_sin == 1, np.sin(phase), np.cos(phase))
    weight = np.where((k == 0) | (2 * k == n), 1.0, 2.0)[:, None] / n
    return rows, rows * weight


def make_tables(n, parts):
    local = n // parts
    natural = [(c, j) for c in range(2) for j in range(n)]
    by_owner = [(c, q * local + m) for q in range(parts) for c in range(2) for m in range(local)]
    split = np.array_split(np.arange(local), HALVES)
    by_local = [
        [(c, q * local + m) for c in range(2) for m in ms for q in range(parts)] for ms in split
    ]
    outgoing = np.stack(
        [split_table(left_table(by_owner, natural, n, sign), 1) for sign in (1.0, -1.0)]
    )
    incoming = np.stack(
        [
            np.stack([split_table(left_table(natural, cols, n, sign, size), 1) for cols in by_local])
            for sign, size in ((1.0, 1.0 / n**3), (-1.0, 1.0))
        ]
    )
    right = np.stack(
        [
            split_table(left_table(natural, natural, n, 1.0).T, 0),
            split_table(left_table(natural, natural, n, -1.0).T, 0),
        ]
    )
    half = n // 2
    plain = [(k, 0) for k in range(half + 1)] + [(k, 1) for k in range(1, half)]
    columns = [
        [(2 * p, 0) for p in range(parts)],
        [(half, 0)] + [(2 * p, 1) for p in range(1, parts)],
        [(2 * p + 1, 0) for p in range(parts)],
        [(2 * p + 1, 1) for p in range(parts)],
    ]
    y_rows, y_back = real_basis(n, sum(columns, []))
    rows, back = real_basis(n, plain)
    by_local_x = [q * local + m for m in range(local) for q in range(parts)]
    x_rows = rows[:, by_local_x]
    x_back = np.zeros((parts, 2 * local, n))
    x_back[:, :local] = back.T.reshape(parts, local, n)
    basis_y = np.stack([split_table(y_rows * 2.0 * n**3, 1), split_table(y_back.T, 1)])
    basis_z = np.stack([split_table(rows.T, 0), split_table(back, 0)])
    basis_x = split_table(x_rows, 1)
    spread_x = split_table(x_back.reshape(2 * n, n), 1)
    return [outgoing, right, incoming, basis_y, basis_x, spread_x, basis_z]


def halves(value):
    high = value.astype(bf16)
    low = (value - high.astype(f32)).astype(bf16)
    return high, low


def left_dot(table, data):
    high, low = halves(data)
    return jnp.dot(table, jnp.concatenate([high, low, high], axis=0), preferred_element_type=f32)


def right_dot(data, table):
    high, low = halves(data)
    return jnp.dot(jnp.concatenate([high, low, high], axis=1), table, preferred_element_type=f32)


def kernel(
    n,
    parts,
    pools,
    raw_hbm,
    energy,
    potential_hbm,
    perturbation_hbm,
    xc_hbm,
    outgoing_hbm,
    right_hbm,
    incoming_hbm,
    basis_y_hbm,
    basis_x_hbm,
    spread_x_hbm,
    basis_z_hbm,
    coeff_out,
    density_out,
    hxc_out,
    coeff,
    density,
    hxc,
    raw,
    potential,
    perturbation,
    xc,
    outgoing,
    right,
    incoming,
    basis_y,
    basis_x,
    spread_x,
    basis_z,
    wave,
    kin,
    pre,
    resid,
    search,
    answer,
    ahead,
    space_wave,
    space_search,
    overlap,
    total,
    send,
    recv,
    small_send,
    small_recv,
    go_send,
    go_recv,
    back_send,
    back_recv,
    loaded,
    bulk_out,
    bulk_in,
    small_out,
    small_in,
    turn_out,
    turn_in,
    met,
    stored,
):
    local = n // parts
    group = local // HALVES
    block = 2 * local * group
    room = block + 8
    devices = parts * pools
    inverse_total = 1.0 / n**3
    me = lax.axis_index("fft")
    pool = lax.axis_index("pool")
    def lanes(value, index):
        return value[:, index * n : (index + 1) * n]

    def turned(start, shift, size):
        index = start + shift
        return jnp.where(index >= size, index - size, index)

    def for_peers(act):
        def step(shift, _):
            act(turned(me, shift, parts))
            return 0

        lax.fori_loop(parts // 2, parts, step, 0)
        lax.fori_loop(1, parts // 2, step, 0)

    def for_devices(act):
        for pool_shift in (2, 1, 3):
            other_pool = turned(pool, pool_shift, pools)

            def step(shift, _, other_pool=other_pool):
                act(turned(me, shift, parts), other_pool)
                return 0

            lax.fori_loop(parts // 2, parts, step, 0)
            lax.fori_loop(0, parts // 2, step, 0)
        for_peers(lambda other: act(other, pool))

    barrier = pltpu.get_barrier_semaphore()

    def greet(other, other_pool):
        pl.semaphore_signal(
            barrier, inc=1, device_id={"pool": other_pool, "fft": other}, device_id_type=MESH
        )

    for_peers(lambda other: greet(other, pool))
    for pool_shift in range(1, pools):
        greet(me, turned(pool, pool_shift, pools))
    loads = {}
    order = [
        (raw_hbm, raw),
        (right_hbm, right),
        (outgoing_hbm, outgoing),
        (incoming_hbm, incoming),
        (perturbation_hbm, perturbation),
        (potential_hbm, potential),
        (basis_y_hbm, basis_y),
        (basis_x_hbm, basis_x),
        (basis_z_hbm, basis_z),
        (spread_x_hbm, spread_x),
        (xc_hbm, xc),
    ]
    for i, (source, target) in enumerate(order):
        loads[i] = pltpu.make_async_copy(source, target, loaded.at[i])
        loads[i].start()


    def row_half(phase):
        return HALVES - 1 if phase >= 2 else None

    def used_rows(phase, half):
        return block + 1 if half == row_half(phase) else block

    def store_half(phase, band, half, value, row=None):
        for m in range(group):
            send[phase, band, half, :, 2 * local * m : 2 * local * (m + 1), :] = lanes(
                value, m
            ).reshape(parts, 2 * local, n)
        if half == row_half(phase):
            send[phase, band, half, :, block:room, :] = jnp.broadcast_to(
                pack(row), (parts, 8, n)
            )

    def start_half(phase, band, half):
        here = pl.multiple_of(me * room, room)
        used = used_rows(phase, half)

        def start(other):
            pltpu.make_async_remote_copy(
                src_ref=send.at[phase, band, half, other, pl.ds(0, used)],
                dst_ref=recv.at[phase, band, half, pl.ds(here, used)],
                send_sem=bulk_out.at[phase, band, half],
                recv_sem=bulk_in.at[phase, band, half],
                device_id={"fft": other},
                device_id_type=MESH,
            ).start()

        for_peers(start)
        recv[phase, band, half, pl.ds(here, room), :] = send[phase, band, half, me]

    def half_bytes(phase, band, half):
        return recv.at[phase, band, half, pl.ds(0, (parts - 1) * used_rows(phase, half))]

    def wait_bytes(ref, sem):
        pltpu.make_async_copy(ref, ref, sem).wait()

    def receive_bulk(phase, band, tables):
        out = None
        for half in range(HALVES):
            wait_bytes(half_bytes(phase, band, half), bulk_in.at[phase, band, half])
            rows = []
            for c in range(2):
                for m in range(group):
                    pieces = []
                    for other in range(local):
                        first = 2 * local * m + local * c + other
                        pieces.append(
                            recv[phase, band, half, pl.ds(first, parts, stride=room), :]
                        )
                    rows.append(jnp.concatenate(pieces, axis=1))
            part = left_dot(tables[half], jnp.concatenate(rows, axis=0))
            out = part if out is None else out + part
        return out

    row_id = lax.broadcasted_iota(jnp.int32, (8, n), 0)
    lane_id = lax.broadcasted_iota(jnp.int32, (8, n), 1)

    def lane_sums(value):
        column = jnp.sum(value, axis=0, keepdims=True)
        result = lanes(column, 0)
        for m in range(1, local):
            result = result + lanes(column, m)
        return result

    def pack(values):
        stacked = jnp.zeros((8, n), f32)
        for i, value in enumerate(values):
            stacked = jnp.where(row_id == i, value, stacked)
        sums = jnp.sum(stacked, axis=1, keepdims=True)
        return jnp.sum(jnp.where(row_id == lane_id, sums, 0.0), axis=0, keepdims=True)

    def unpack(row, count):
        return [
            jnp.sum(jnp.where(lane_id[:1] == i, row, 0.0), axis=1, keepdims=True)
            for i in range(count)
        ]

    def bulk_row(phase, band, count):
        rows = recv[phase, band, row_half(phase), pl.ds(block, parts, stride=room), :]
        return unpack(jnp.sum(rows, axis=0, keepdims=True), count)

    def send_small(values):
        row = pack(values)
        small_send[...] = row
        small_recv[me] = row

        def start(other):
            pltpu.make_async_remote_copy(
                src_ref=small_send,
                dst_ref=small_recv.at[me],
                send_sem=small_out,
                recv_sem=small_in,
                device_id={"fft": other},
                device_id_type=MESH,
            ).start()

        for_peers(start)

    def receive_small(count):
        wait_bytes(small_recv.at[pl.ds(0, parts - 1)], small_in)
        return unpack(jnp.sum(small_recv[...], axis=0), count)


    def along_z(real, imag, table):
        count = real.shape[1] // n
        rows = jnp.concatenate(
            [jnp.concatenate([lanes(real, m), lanes(imag, m)], axis=1) for m in range(count)],
            axis=0,
        )
        out = right_dot(rows, table)
        picked = [out[m * n : (m + 1) * n] for m in range(count)]
        return (
            jnp.concatenate([lanes(v, 0) for v in picked], axis=1),
            jnp.concatenate([lanes(v, 1) for v in picked], axis=1),
        )

    def half_of(value, half):
        return value[:, half * group * n : (half + 1) * group * n]

    def send_real(phase, band, real, imag, row=None):
        for half in range(HALVES):
            part = jnp.concatenate(
                along_z(half_of(real, half), half_of(imag, half), right[0]), axis=0
            )
            store_half(phase, band, half, left_dot(outgoing[0], part), row)
            if phase == 0 and band == 0 and half == 0:
                pl.semaphore_wait(barrier, parts + pools - 2)
            start_half(phase, band, half)

    def receive_real(phase, band):
        out = receive_bulk(phase, band, incoming[0])
        return out[:n], out[n:]

    def send_reciprocal(phase, band, real, imag, row=None):
        for half in range(HALVES):
            part = jnp.concatenate([half_of(real, half), half_of(imag, half)], axis=0)
            store_half(phase, band, half, left_dot(outgoing[1], part), row)
            start_half(phase, band, half)

    def receive_reciprocal(phase, band):
        out = receive_bulk(phase, band, incoming[1])
        return along_z(out[:n], out[n:], right[1])


    loads[0].wait()
    for band in range(BANDS):
        for c in range(2):
            for m in range(local):
                wave[band, c, :, m * n : (m + 1) * n] = raw[
                    band, c, pl.ds(m, n, stride=local), :
                ]
        if band == 0:
            loads[1].wait()
            loads[2].wait()
        send_real(0, band, wave[band, 0], wave[band, 1])

    for pool_shift in range(1, pools):
        pl.semaphore_signal(
            met,
            inc=1,
            device_id={"pool": turned(pool, pool_shift, pools), "fft": me},
            device_id_type=MESH,
        )

    def wavenumber(index):
        signed = jnp.where(2 * index >= n, index - n, index)
        return signed.astype(f32) * unit

    def offset(axis_number):
        bit = lax.rem(pool // 2**axis_number, 2)
        return (0.5 * bit.astype(f32) - 0.25) * unit

    index_x = lax.broadcasted_iota(jnp.int32, (n, n), 0)
    index_z = lax.broadcasted_iota(jnp.int32, (n, n), 1)
    square_x = (wavenumber(index_x) + offset(0)) ** 2
    square_z = (wavenumber(index_z) + offset(2)) ** 2
    for m in range(local):
        square_y = (wavenumber(me * local + m) + offset(1)) ** 2
        value = 0.5 * (square_x + square_y + square_z)
        kin[:, m * n : (m + 1) * n] = value
        pre[:, m * n : (m + 1) * n] = 1.0 / (value + 1.0)

    def wide(ref):
        return jnp.concatenate([ref[m] for m in range(local)], axis=1)


    overlaps = []
    for i in range(3, len(order)):
        loads[i].wait()
    for band in range(BANDS):
        real, imag = receive_real(0, band)
        space_wave[band, 0] = real
        space_wave[band, 1] = imag
        change = wide(perturbation)
        changed_real = change * real
        changed_imag = change * imag
        overlaps.append(lane_sums(changed_real * real + changed_imag * imag))
        if band == BANDS - 1:
            first_real = space_wave[0, 0]
            first_imag = space_wave[0, 1]
            overlaps.append(lane_sums(first_real * changed_real + first_imag * changed_imag))
            overlaps.append(lane_sums(first_real * changed_imag - first_imag * changed_real))
            send_small(overlaps)
        send_reciprocal(1, band, changed_real, changed_imag)

    def products(band, real, imag):
        sums = []
        for m in range(BANDS):
            sums.append(lane_sums(wave[m, 0] * real + wave[m, 1] * imag))
            sums.append(lane_sums(wave[m, 0] * imag - wave[m, 1] * real))
        return [value * inverse_total for value in sums]

    def kinetic_sum(band, left_real, left_imag, right_real, right_imag):
        shifted = kin[...] - energy[0, band]
        return lane_sums(shifted * (left_real * right_real + left_imag * right_imag)) * inverse_total

    def send_step(phase, band, resid_real, resid_imag):
        real = pre[...] * resid_real
        imag = pre[...] * resid_imag
        row = [lane_sums(resid_real * real + resid_imag * imag) * inverse_total]
        resid[band, 0] = resid_real
        resid[band, 1] = resid_imag
        ahead[band, 0] = real
        ahead[band, 1] = imag
        send_real(phase, band, real, imag, row)


    partial = [None] * BANDS
    rho = [None] * BANDS
    for band in range(BANDS):
        real, imag = receive_reciprocal(1, band)
        if band == 0:
            same0, same1, cross_real, cross_imag = receive_small(4)
        if band == 0:
            m0_real, m0_imag, m1_real, m1_imag = same0, 0.0 * same0, cross_real, -cross_imag
        else:
            m0_real, m0_imag, m1_real, m1_imag = cross_real, cross_imag, same1, 0.0 * same1
        resid_real = (
            wave[0, 0] * m0_real
            - wave[0, 1] * m0_imag
            + wave[1, 0] * m1_real
            - wave[1, 1] * m1_imag
            - real
        )
        resid_imag = (
            wave[0, 0] * m0_imag
            + wave[0, 1] * m0_real
            + wave[1, 0] * m1_imag
            + wave[1, 1] * m1_real
            - imag
        )
        send_step(2, band, resid_real, resid_imag)


    def finish_curvature(product, values):
        curvature, c0_real, c0_imag, c1_real, c1_imag = values
        curvature = curvature + 2.0 * (
            c0_real * c0_real + c0_imag * c0_imag + c1_real * c1_real + c1_imag * c1_imag
        )
        return product / curvature


    slot = 2 * local

    def turn(which, source, target, all_columns, rows=local):
        here = pl.multiple_of((pool * parts + me) * slot, slot)
        own = here if all_columns else pl.multiple_of(me * slot, slot)
        target[pl.ds(here, rows), :] = source[pl.ds(own, rows), :]

        def start(other, other_pool):
            there = other_pool * parts + other if all_columns else other
            there = pl.multiple_of(there * slot, slot)
            pltpu.make_async_remote_copy(
                src_ref=source.at[pl.ds(there, rows)],
                dst_ref=target.at[pl.ds(here, rows)],
                send_sem=turn_out.at[which],
                recv_sem=turn_in.at[which],
                device_id={"pool": other_pool, "fft": other},
                device_id_type=MESH,
            ).start()

        for_devices(start)

    def wait_turn(which, target, rows=local):
        wait_bytes(target.at[pl.ds(0, rows * (devices - 1))], turn_in.at[which])

    def send_columns(which, value):
        columns = left_dot(basis_y[0], value)
        for m in range(local):
            go_send[which, pl.ds(m, devices, stride=slot), :] = lanes(columns, m)

    def send_term(band, sums):
        which = 1 + band
        send_columns(which, overlap[band])
        share = jnp.where(lane_id[:1] == 0, rho[band] * (1.0 / parts), 0.0)
        go_send[which, pl.ds(local, devices, stride=slot), :] = jnp.broadcast_to(
            pack(sums + [share]), (devices, n)
        )
        turn(which, go_send.at[which], go_recv.at[which], True, local + 1)

    for step in range(CG_STEPS):
        last = step + 1 == CG_STEPS
        if last:
            pl.semaphore_wait(met, pools - 1)
            send_columns(0, total[...])
            turn(0, go_send.at[0], go_recv.at[0], True)
        for band in range(BANDS):
            real, imag = ahead[band, 0], ahead[band, 1]
            sums = [kinetic_sum(band, real, imag, real, imag)] + products(band, real, imag)
            if step > 0:
                cross = kinetic_sum(band, real, imag, search[band, 0], search[band, 1])
            real, imag = receive_real(2 + 2 * step, band)
            (rho_new,) = bulk_row(2 + 2 * step, band, 1)
            if step > 0:
                beta = rho_new / rho[band]
                before = partial[band]
                sums[0] = sums[0] + beta * (2.0 * cross + beta * before[0])
                for i in range(1, 1 + 2 * BANDS):
                    sums[i] = sums[i] + beta * before[i]
                real = real + beta * space_search[band, 0]
                imag = imag + beta * space_search[band, 1]
            rho[band] = rho_new
            partial[band] = list(sums)
            if not last:
                space_search[band, 0] = real
                space_search[band, 1] = imag
            level = wide(potential)
            image_real = level * real
            image_imag = level * imag
            sums[0] = sums[0] + lane_sums(image_real * real + image_imag * imag)
            if not last:
                send_reciprocal(3 + 2 * step, band, image_real, image_imag, sums)
            overlap[band] = space_wave[band, 0] * real + space_wave[band, 1] * imag
            for c in range(2):
                if step == 0:
                    search[band, c] = ahead[band, c]
                else:
                    search[band, c] = ahead[band, c] + beta * search[band, c]
            if last:
                send_term(band, sums)
        if last:
            break
        for band in range(BANDS):
            pot_real, pot_imag = receive_reciprocal(3 + 2 * step, band)
            values = bulk_row(3 + 2 * step, band, 5)
            _, c0_real, c0_imag, c1_real, c1_imag = values
            size = finish_curvature(rho[band], values)
            shifted = kin[...] - energy[0, band]
            real = search[band, 0]
            imag = search[band, 1]
            image_real = (
                shifted * real
                + pot_real
                + 2.0
                * (
                    wave[0, 0] * c0_real
                    - wave[0, 1] * c0_imag
                    + wave[1, 0] * c1_real
                    - wave[1, 1] * c1_imag
                )
            )
            image_imag = (
                shifted * imag
                + pot_imag
                + 2.0
                * (
                    wave[0, 0] * c0_imag
                    + wave[0, 1] * c0_real
                    + wave[1, 0] * c1_imag
                    + wave[1, 1] * c1_real
                )
            )
            send_step(
                4 + 2 * step,
                band,
                resid[band, 0] - size * image_real,
                resid[band, 1] - size * image_imag,
            )
            added = size * overlap[band]
            total[...] = added if step == 0 and band == 0 else total[...] + added
            for c in range(2):
                moved = size * search[band, c]
                answer[band, c] = moved if step == 0 else answer[band, c] + moved

    even = 2 * me
    frequency = jnp.where(
        pool == 0, even, jnp.where(pool == 1, jnp.where(me == 0, n // 2, even), even + 1)
    )

    def plain_square(index):
        k = jnp.where(index > n // 2, index - n // 2, index)
        return (k.astype(f32) * unit) ** 2

    squared = (
        plain_square(index_x) + (frequency.astype(f32) * unit) ** 2 + plain_square(index_z)
    )
    nonzero = (squared > 0).astype(f32)
    coulomb = 4.0 * math.pi * nonzero / (squared + (1.0 - nonzero))

    wait_turn(0, go_recv.at[0])
    sizes = []
    for band in range(BANDS):
        wait_turn(1 + band, go_recv.at[1 + band], local + 1)
        sizes.append([])
        for other in range(pools):
            first = other * parts * slot + local
            rows = go_recv[1 + band, pl.ds(first, parts, stride=slot), :]
            values = unpack(jnp.sum(rows, axis=0, keepdims=True), 6)
            sizes[band].append(finish_curvature(values[5], values[:5]))
    pieces = []
    for m in range(local):
        piece = None
        for other in range(pools):
            rows = pl.ds(other * parts * slot + m, parts, stride=slot)
            term = go_recv[0, rows, :]
            for band in range(BANDS):
                term = term + sizes[band][other] * go_recv[1 + band, rows, :]
            piece = term if piece is None else piece + term
        back_send[0, pl.ds(m, parts, stride=slot), :] = piece
        pieces.append(piece)
    turn(3, back_send.at[0], back_recv.at[0], False)


    field = left_dot(basis_x[...], jnp.concatenate(pieces, axis=0))
    field = coulomb * right_dot(field, basis_z[0])
    field = left_dot(spread_x[...], right_dot(field, basis_z[1]))
    back_send[1] = field
    turn(4, back_send.at[1], back_recv.at[1], False)

    for band in range(BANDS):
        size = sum(jnp.where(pool == i, sizes[band][i], 0.0) for i in range(pools))
        for c in range(2):
            value = answer[band, c] + size * search[band, c]
            for m in range(local):
                coeff[band, c, pl.ds(m, n, stride=local), :] = lanes(value, m)
    results = [(coeff, coeff_out), (density, density_out), (hxc, hxc_out)]
    stores = [pltpu.make_async_copy(a, b, stored.at[i]) for i, (a, b) in enumerate(results)]
    stores[0].start()

    for i, result in enumerate((density, hxc)):
        wait_turn(3 + i, back_recv.at[i])
        columns = [back_recv[i, pl.ds(m, devices, stride=slot), :] for m in range(local)]
        whole = left_dot(basis_y[1], jnp.concatenate(columns, axis=1))
        for m in range(local):
            if i == 0:
                result[m] = lanes(whole, m)
            else:
                result[m] = lanes(whole, m) + xc[m] * density[m]
        stores[1 + i].start()


    for phase in range(2 * CG_STEPS + 1):
        for band in range(BANDS):
            for half in range(HALVES):
                wait_bytes(half_bytes(phase, band, half), bulk_out.at[phase, band, half])
    for store in stores:
        store.wait()
    wait_bytes(small_recv.at[pl.ds(0, parts - 1)], small_out)
    for which in range(5):
        rows = local + 1 if which in (1, 2) else local
        wait_bytes(go_recv.at[0, pl.ds(0, rows * (devices - 1))], turn_out.at[which])


def hand_over(coeff, density, hxc, coeff_out, density_out, hxc_out, *scratch):
    held, held_density, held_hxc, came, gone = scratch
    moves = [(density, held_density, density_out), (hxc, held_hxc, hxc_out)]
    for b in range(BANDS):
        for c in range(2):
            moves.append((coeff.at[b, c], held.at[b, c], coeff_out.at[b, c]))
    first = [pltpu.make_async_copy(a, h, came.at[i]) for i, (a, h, _) in enumerate(moves)]
    second = [pltpu.make_async_copy(h, o, gone.at[i]) for i, (_, h, o) in enumerate(moves)]
    for copy in first:
        copy.start()
    for copy, onward in zip(first, second):
        copy.wait()
        onward.start()
    for copy in second:
        copy.wait()


def body(wave_coeff, band_energy, local_potential, perturbation, xc_kernel, parts, pools):
    n = wave_coeff.shape[-1]
    local = n // parts
    block = 2 * local * (local // HALVES)
    wide = local * n
    phases = 2 * CG_STEPS + 1
    room = block + 8
    slot_rows = 2 * local * parts
    operands = [
        wave_coeff.reshape(BANDS, 2, n * local, n),
        local_potential,
        perturbation,
        xc_kernel,
    ] + [jnp.asarray(t) for t in make_tables(n, parts)]
    anywhere = pl.BlockSpec(memory_space=pl.ANY)
    vmem = pl.BlockSpec(memory_space=pltpu.VMEM)
    field = pltpu.VMEM((BANDS, 2, n, wide), f32)
    dma = pltpu.SemaphoreType.DMA
    coeff, density, hxc = pl.pallas_call(
        functools.partial(kernel, n, parts, pools),
        out_shape=(
            jax.ShapeDtypeStruct(operands[0].shape, f32),
            jax.ShapeDtypeStruct((local, n, n), f32),
            jax.ShapeDtypeStruct((local, n, n), f32),
        ),
        in_specs=[anywhere, pl.BlockSpec(memory_space=pltpu.SMEM)] + [anywhere] * 10,
        out_specs=(anywhere, anywhere, anywhere),
        scratch_shapes=[
            pltpu.VMEM(operands[0].shape, f32),
            pltpu.VMEM((local, n, n), f32),
            pltpu.VMEM((local, n, n), f32),
        ]
        + [pltpu.VMEM(t.shape, t.dtype) for t in operands]
        + [
            field,
            pltpu.VMEM((n, wide), f32),
            pltpu.VMEM((n, wide), f32),
            field,
            field,
            field,
            field,
            field,
            field,
            pltpu.VMEM((BANDS, n, wide), f32),
            pltpu.VMEM((n, wide), f32),
            pltpu.VMEM((phases, BANDS, HALVES, parts, room, n), f32),
            pltpu.VMEM((phases, BANDS, HALVES, parts * room, n), f32),
            pltpu.VMEM((1, n), f32),
            pltpu.VMEM((parts, 1, n), f32),
            pltpu.VMEM((1 + BANDS, pools * slot_rows, n), f32),
            pltpu.VMEM((1 + BANDS, pools * slot_rows, n), f32),
            pltpu.VMEM((2, slot_rows, n), f32),
            pltpu.VMEM((2, pools * slot_rows, n), f32),
            dma((11,)),
            dma((phases, BANDS, HALVES)),
            dma((phases, BANDS, HALVES)),
            dma(()),
            dma(()),
            dma((5,)),
            dma((5,)),
            pltpu.SemaphoreType.REGULAR,
            dma((3,)),
        ],
        compiler_params=pltpu.CompilerParams(
            collective_id=0, has_side_effects=True, vmem_limit_bytes=56 * 1024 * 1024
        ),
    )(operands[0], band_energy, *operands[1:])
    results = [coeff, density, hxc]
    coeff, density, hxc = pl.pallas_call(
        hand_over,
        out_shape=[jax.ShapeDtypeStruct(t.shape, f32) for t in results],
        in_specs=[anywhere] * 3,
        out_specs=[anywhere] * 3,
        scratch_shapes=[pltpu.VMEM(t.shape, f32) for t in results]
        + [dma((2 * BANDS + 2,)), dma((2 * BANDS + 2,))],
    )(*results)
    return coeff.reshape(wave_coeff.shape), density, hxc


def solution(mesh):
    return jax.shard_map(
        functools.partial(body, parts=mesh.shape["fft"], pools=mesh.shape["pool"]),
        mesh=mesh,
        in_specs=(
            P("pool", None, None, None, "fft", None),
            P("pool", None),
            P("fft", None, None),
            P("fft", None, None),
            P("fft", None, None),
        ),
        out_specs=(
            P("pool", None, None, None, "fft", None),
            P("fft", None, None),
            P("fft", None, None),
        ),
        check_vma=False,
    )
```

```python
import functools
import math

import jax
import jax.numpy as jnp
import ml_dtypes
import numpy as np
from jax import lax
from jax.experimental import pallas as pl
from jax.experimental.pallas import tpu as pltpu
from jax.sharding import PartitionSpec as P

CG_STEPS = 3
BANDS = 2
HALVES = 2
cell_length = 51.3
unit = 2.0 * math.pi / cell_length
MESH = pl.DeviceIdType.MESH
f32 = jnp.float32
bf16 = jnp.bfloat16


def left_table(rows, cols, n, sign, scale=1.0):
    rows, cols = np.array(rows), np.array(cols)
    phase = 2.0 * np.pi * ((rows[:, None, 1] * cols[None, :, 1]) % n) / n
    out_part, in_part = rows[:, None, 0], cols[None, :, 0]
    value = np.where(
        out_part == in_part,
        np.cos(phase),
        np.where(out_part == 1, sign, -sign) * np.sin(phase),
    )
    return value * scale


def split_table(table, axis):
    high = table.astype(ml_dtypes.bfloat16)
    low = (table - high.astype(np.float64)).astype(ml_dtypes.bfloat16)
    return np.concatenate([high, high, low], axis=axis)


def real_basis(n, order):
    k = np.array([f for f, _ in order])
    phase = 2.0 * np.pi * ((k[:, None] * np.arange(n)[None, :]) % n) / n
    is_sin = np.array([s for _, s in order])[:, None]
    rows = np.where(is_sin == 1, np.sin(phase), np.cos(phase))
    weight = np.where((k == 0) | (2 * k == n), 1.0, 2.0)[:, None] / n
    return rows, rows * weight


def make_tables(n, parts):
    local = n // parts
    natural = [(c, j) for c in range(2) for j in range(n)]
    by_owner = [(c, q * local + m) for q in range(parts) for c in range(2) for m in range(local)]
    split = np.array_split(np.arange(local), HALVES)
    by_local = [
        [(c, q * local + m) for c in range(2) for m in ms for q in range(parts)] for ms in split
    ]
    outgoing = np.stack(
        [split_table(left_table(by_owner, natural, n, sign), 1) for sign in (1.0, -1.0)]
    )
    incoming = np.stack(
        [
            np.stack([split_table(left_table(natural, cols, n, sign, size), 1) for cols in by_local])
            for sign, size in ((1.0, 1.0 / n**3), (-1.0, 1.0))
        ]
    )
    right = np.stack(
        [
            split_table(left_table(natural, natural, n, 1.0).T, 0),
            split_table(left_table(natural, natural, n, -1.0).T, 0),
        ]
    )
    half = n // 2
    plain = [(k, 0) for k in range(half + 1)] + [(k, 1) for k in range(1, half)]
    columns = [
        [(2 * p, 0) for p in range(parts)],
        [(half, 0)] + [(2 * p, 1) for p in range(1, parts)],
        [(2 * p + 1, 0) for p in range(parts)],
        [(2 * p + 1, 1) for p in range(parts)],
    ]
    y_rows, y_back = real_basis(n, sum(columns, []))
    rows, back = real_basis(n, plain)
    by_local_x = [q * local + m for m in range(local) for q in range(parts)]
    x_rows = rows[:, by_local_x]
    x_back = np.zeros((parts, 2 * local, n))
    x_back[:, :local] = back.T.reshape(parts, local, n)
    basis_y = np.stack([split_table(y_rows * 2.0 * n**3, 1), split_table(y_back.T, 1)])
    basis_z = np.stack([split_table(rows.T, 0), split_table(back, 0)])
    basis_x = split_table(x_rows, 1)
    spread_x = split_table(x_back.reshape(2 * n, n), 1)
    return [outgoing, right, incoming, basis_y, basis_x, spread_x, basis_z]


def halves(value):
    high = value.astype(bf16)
    low = (value - high.astype(f32)).astype(bf16)
    return high, low


def left_dot(table, data):
    high, low = halves(data)
    return jnp.dot(table, jnp.concatenate([high, low, high], axis=0), preferred_element_type=f32)


def right_dot(data, table):
    high, low = halves(data)
    return jnp.dot(jnp.concatenate([high, low, high], axis=1), table, preferred_element_type=f32)


def kernel(
    n,
    parts,
    pools,
    raw_hbm,
    energy,
    potential_hbm,
    perturbation_hbm,
    xc_hbm,
    outgoing_hbm,
    right_hbm,
    incoming_hbm,
    basis_y_hbm,
    basis_x_hbm,
    spread_x_hbm,
    basis_z_hbm,
    coeff_out,
    density_out,
    hxc_out,
    coeff,
    density,
    hxc,
    raw,
    potential,
    perturbation,
    xc,
    outgoing,
    right,
    incoming,
    basis_y,
    basis_x,
    spread_x,
    basis_z,
    wave,
    kin,
    pre,
    resid,
    search,
    answer,
    ahead,
    space_wave,
    space_search,
    overlap,
    total,
    send,
    recv,
    small_send,
    small_recv,
    go_send,
    go_recv,
    back_send,
    back_recv,
    loaded,
    bulk_out,
    bulk_in,
    small_out,
    small_in,
    turn_out,
    turn_in,
    met,
    stored,
):
    local = n // parts
    group = local // HALVES
    block = 2 * local * group
    room = block + 8
    devices = parts * pools
    inverse_total = 1.0 / n**3
    me = lax.axis_index("fft")
    pool = lax.axis_index("pool")
    def lanes(value, index):
        return value[:, index * n : (index + 1) * n]

    def turned(start, shift, size):
        index = start + shift
        return jnp.where(index >= size, index - size, index)

    def for_shifts(first, last, unroll, act):
        odd = (last - first) % unroll
        for shift in range(first, first + odd):
            act(turned(me, shift, parts))

        def step(index, _):
            shift = first + odd + index * unroll
            for more in range(unroll):
                act(turned(me, shift + more, parts))
            return 0

        lax.fori_loop(0, (last - first) // unroll, step, 0)

    def for_peers(act, unroll=4):
        for_shifts(parts // 2, parts, unroll, act)
        for_shifts(1, parts // 2, unroll, act)

    def for_devices(act):
        for pool_shift in (2, 1, 3):
            other_pool = turned(pool, pool_shift, pools)

            def at_pool(other, other_pool=other_pool):
                act(other, other_pool)

            for_shifts(parts // 2, parts, 8, at_pool)
            for_shifts(0, parts // 2, 8, at_pool)
        for_peers(lambda other: act(other, pool), 8)

    barrier = pltpu.get_barrier_semaphore()

    def greet(other, other_pool):
        pl.semaphore_signal(
            barrier, inc=1, device_id={"pool": other_pool, "fft": other}, device_id_type=MESH
        )

    for_peers(lambda other: greet(other, pool))
    for pool_shift in range(1, pools):
        greet(me, turned(pool, pool_shift, pools))
    loads = {}
    order = [
        (raw_hbm, raw),
        (right_hbm, right),
        (outgoing_hbm, outgoing),
        (incoming_hbm, incoming),
        (perturbation_hbm, perturbation),
        (potential_hbm, potential),
        (basis_y_hbm, basis_y),
        (basis_x_hbm, basis_x),
        (basis_z_hbm, basis_z),
        (spread_x_hbm, spread_x),
        (xc_hbm, xc),
    ]
    for i, (source, target) in enumerate(order):
        loads[i] = pltpu.make_async_copy(source, target, loaded.at[i])
        loads[i].start()


    def row_half(phase):
        return HALVES - 1 if phase >= 2 else None

    def used_rows(phase, half):
        return block + 1 if half == row_half(phase) else block

    def store_half(phase, band, half, value, row=None):
        for m in range(group):
            send[phase, band, half, :, 2 * local * m : 2 * local * (m + 1), :] = lanes(
                value, m
            ).reshape(parts, 2 * local, n)
        if half == row_half(phase):
            send[phase, band, half, :, block:room, :] = jnp.broadcast_to(
                pack(row), (parts, 8, n)
            )

    def start_half(phase, band, half):
        here = pl.multiple_of(me * room, room)
        used = used_rows(phase, half)

        def start(other):
            pltpu.make_async_remote_copy(
                src_ref=send.at[phase, band, half, other, pl.ds(0, used)],
                dst_ref=recv.at[phase, band, half, pl.ds(here, used)],
                send_sem=bulk_out.at[phase, band, half],
                recv_sem=bulk_in.at[phase, band, half],
                device_id={"fft": other},
                device_id_type=MESH,
            ).start()

        for_peers(start)
        recv[phase, band, half, pl.ds(here, room), :] = send[phase, band, half, me]

    def half_bytes(phase, band, half):
        return recv.at[phase, band, half, pl.ds(0, (parts - 1) * used_rows(phase, half))]

    def wait_bytes(ref, sem):
        pltpu.make_async_copy(ref, ref, sem).wait()

    def receive_bulk(phase, band, tables):
        out = None
        for half in range(HALVES):
            wait_bytes(half_bytes(phase, band, half), bulk_in.at[phase, band, half])
            rows = []
            for c in range(2):
                for m in range(group):
                    pieces = []
                    for other in range(local):
                        first = 2 * local * m + local * c + other
                        pieces.append(
                            recv[phase, band, half, pl.ds(first, parts, stride=room), :]
                        )
                    rows.append(jnp.concatenate(pieces, axis=1))
            part = left_dot(tables[half], jnp.concatenate(rows, axis=0))
            out = part if out is None else out + part
        return out

    row_id = lax.broadcasted_iota(jnp.int32, (8, n), 0)
    lane_id = lax.broadcasted_iota(jnp.int32, (8, n), 1)

    def lane_sums(value):
        column = jnp.sum(value, axis=0, keepdims=True)
        result = lanes(column, 0)
        for m in range(1, local):
            result = result + lanes(column, m)
        return result

    def pack(values):
        stacked = jnp.zeros((8, n), f32)
        for i, value in enumerate(values):
            stacked = jnp.where(row_id == i, value, stacked)
        sums = jnp.sum(stacked, axis=1, keepdims=True)
        return jnp.sum(jnp.where(row_id == lane_id, sums, 0.0), axis=0, keepdims=True)

    def unpack(row, count):
        return [
            jnp.sum(jnp.where(lane_id[:1] == i, row, 0.0), axis=1, keepdims=True)
            for i in range(count)
        ]

    def bulk_row(phase, band, count):
        rows = recv[phase, band, row_half(phase), pl.ds(block, parts, stride=room), :]
        return unpack(jnp.sum(rows, axis=0, keepdims=True), count)

    def send_small(which, values):
        row = pack(values)
        small_send[which] = row
        small_recv[which, me] = row

        def start(other):
            pltpu.make_async_remote_copy(
                src_ref=small_send.at[which],
                dst_ref=small_recv.at[which, me],
                send_sem=small_out.at[which],
                recv_sem=small_in.at[which],
                device_id={"fft": other},
                device_id_type=MESH,
            ).start()

        for_peers(start)

    def receive_small(which, count):
        wait_bytes(small_recv.at[which, pl.ds(0, parts - 1)], small_in.at[which])
        return unpack(jnp.sum(small_recv[which], axis=0), count)


    def along_z(real, imag, table):
        count = real.shape[1] // n
        rows = jnp.concatenate(
            [jnp.concatenate([lanes(real, m), lanes(imag, m)], axis=1) for m in range(count)],
            axis=0,
        )
        out = right_dot(rows, table)
        picked = [out[m * n : (m + 1) * n] for m in range(count)]
        return (
            jnp.concatenate([lanes(v, 0) for v in picked], axis=1),
            jnp.concatenate([lanes(v, 1) for v in picked], axis=1),
        )

    def half_of(value, half):
        return value[:, half * group * n : (half + 1) * group * n]

    def send_real(phase, band, real, imag, row=None):
        for half in range(HALVES):
            part = jnp.concatenate(
                along_z(half_of(real, half), half_of(imag, half), right[0]), axis=0
            )
            store_half(phase, band, half, left_dot(outgoing[0], part), row)
            if phase == 0 and band == 0 and half == 0:
                pl.semaphore_wait(barrier, parts + pools - 2)
            start_half(phase, band, half)

    def receive_real(phase, band):
        out = receive_bulk(phase, band, incoming[0])
        return out[:n], out[n:]

    def send_reciprocal(phase, band, real, imag, row=None):
        for half in range(HALVES):
            part = jnp.concatenate([half_of(real, half), half_of(imag, half)], axis=0)
            store_half(phase, band, half, left_dot(outgoing[1], part), row)
            start_half(phase, band, half)

    def receive_reciprocal(phase, band):
        out = receive_bulk(phase, band, incoming[1])
        return along_z(out[:n], out[n:], right[1])


    loads[0].wait()
    for band in range(BANDS):
        for c in range(2):
            for m in range(local):
                wave[band, c, :, m * n : (m + 1) * n] = raw[
                    band, c, pl.ds(m, n, stride=local), :
                ]
        if band == 0:
            loads[1].wait()
            loads[2].wait()
        send_real(0, band, wave[band, 0], wave[band, 1])

    for pool_shift in range(1, pools):
        pl.semaphore_signal(
            met,
            inc=1,
            device_id={"pool": turned(pool, pool_shift, pools), "fft": me},
            device_id_type=MESH,
        )

    def wavenumber(index):
        signed = jnp.where(2 * index >= n, index - n, index)
        return signed.astype(f32) * unit

    def offset(axis_number):
        bit = lax.rem(pool // 2**axis_number, 2)
        return (0.5 * bit.astype(f32) - 0.25) * unit

    index_x = lax.broadcasted_iota(jnp.int32, (n, n), 0)
    index_z = lax.broadcasted_iota(jnp.int32, (n, n), 1)
    square_x = (wavenumber(index_x) + offset(0)) ** 2
    square_z = (wavenumber(index_z) + offset(2)) ** 2
    for m in range(local):
        square_y = (wavenumber(me * local + m) + offset(1)) ** 2
        value = 0.5 * (square_x + square_y + square_z)
        kin[:, m * n : (m + 1) * n] = value
        pre[:, m * n : (m + 1) * n] = 1.0 / (value + 1.0)

    def wide(ref):
        return jnp.concatenate([ref[m] for m in range(local)], axis=1)


    overlaps = []
    for i in range(3, len(order)):
        loads[i].wait()
    for band in range(BANDS):
        real, imag = receive_real(0, band)
        space_wave[band, 0] = real
        space_wave[band, 1] = imag
        change = wide(perturbation)
        changed_real = change * real
        changed_imag = change * imag
        overlaps.append(lane_sums(changed_real * real + changed_imag * imag))
        if band == BANDS - 1:
            first_real = space_wave[0, 0]
            first_imag = space_wave[0, 1]
            overlaps.append(lane_sums(first_real * changed_real + first_imag * changed_imag))
            overlaps.append(lane_sums(first_real * changed_imag - first_imag * changed_real))
            send_small(0, overlaps)
        send_reciprocal(1, band, changed_real, changed_imag)

    def products(band, real, imag):
        sums = []
        for m in range(BANDS):
            sums.append(lane_sums(wave[m, 0] * real + wave[m, 1] * imag))
            sums.append(lane_sums(wave[m, 0] * imag - wave[m, 1] * real))
        return [value * inverse_total for value in sums]

    def kinetic_sum(band, left_real, left_imag, right_real, right_imag):
        shifted = kin[...] - energy[0, band]
        return lane_sums(shifted * (left_real * right_real + left_imag * right_imag)) * inverse_total

    def send_step(phase, band, resid_real, resid_imag):
        real = pre[...] * resid_real
        imag = pre[...] * resid_imag
        row = [lane_sums(resid_real * real + resid_imag * imag) * inverse_total]
        resid[band, 0] = resid_real
        resid[band, 1] = resid_imag
        ahead[band, 0] = real
        ahead[band, 1] = imag
        send_real(phase, band, real, imag, row)


    partial = [None] * BANDS
    rho = [None] * BANDS
    for band in range(BANDS):
        real, imag = receive_reciprocal(1, band)
        if band == 0:
            same0, same1, cross_real, cross_imag = receive_small(0, 4)
        if band == 0:
            m0_real, m0_imag, m1_real, m1_imag = same0, 0.0 * same0, cross_real, -cross_imag
        else:
            m0_real, m0_imag, m1_real, m1_imag = cross_real, cross_imag, same1, 0.0 * same1
        resid_real = (
            wave[0, 0] * m0_real
            - wave[0, 1] * m0_imag
            + wave[1, 0] * m1_real
            - wave[1, 1] * m1_imag
            - real
        )
        resid_imag = (
            wave[0, 0] * m0_imag
            + wave[0, 1] * m0_real
            + wave[1, 0] * m1_imag
            + wave[1, 1] * m1_real
            - imag
        )
        send_step(2, band, resid_real, resid_imag)


    def finish_curvature(product, values):
        curvature, c0_real, c0_imag, c1_real, c1_imag = values
        curvature = curvature + 2.0 * (
            c0_real * c0_real + c0_imag * c0_imag + c1_real * c1_real + c1_imag * c1_imag
        )
        return product / curvature


    slot = 2 * local

    def turn(which, source, target, all_columns, rows=local):
        here = pl.multiple_of((pool * parts + me) * slot, slot)
        own = here if all_columns else pl.multiple_of(me * slot, slot)
        target[pl.ds(here, rows), :] = source[pl.ds(own, rows), :]

        def start(other, other_pool):
            there = other_pool * parts + other if all_columns else other
            there = pl.multiple_of(there * slot, slot)
            pltpu.make_async_remote_copy(
                src_ref=source.at[pl.ds(there, rows)],
                dst_ref=target.at[pl.ds(here, rows)],
                send_sem=turn_out.at[which],
                recv_sem=turn_in.at[which],
                device_id={"pool": other_pool, "fft": other},
                device_id_type=MESH,
            ).start()

        for_devices(start)

    def wait_turn(which, target, rows=local):
        wait_bytes(target.at[pl.ds(0, rows * (devices - 1))], turn_in.at[which])

    def store_columns(which, columns):
        for m in range(local):
            go_send[which, pl.ds(m, devices, stride=slot), :] = lanes(columns, m)

    for step in range(CG_STEPS):
        last = step + 1 == CG_STEPS
        for band in range(BANDS):
            real, imag = ahead[band, 0], ahead[band, 1]
            sums = [kinetic_sum(band, real, imag, real, imag)] + products(band, real, imag)
            if step > 0:
                cross = kinetic_sum(band, real, imag, search[band, 0], search[band, 1])
            real, imag = receive_real(2 + 2 * step, band)
            (rho_new,) = bulk_row(2 + 2 * step, band, 1)
            if step > 0:
                beta = rho_new / rho[band]
                before = partial[band]
                sums[0] = sums[0] + beta * (2.0 * cross + beta * before[0])
                for i in range(1, 1 + 2 * BANDS):
                    sums[i] = sums[i] + beta * before[i]
                real = real + beta * space_search[band, 0]
                imag = imag + beta * space_search[band, 1]
            rho[band] = rho_new
            partial[band] = list(sums)
            if not last:
                space_search[band, 0] = real
                space_search[band, 1] = imag
            level = wide(potential)
            image_real = level * real
            image_imag = level * imag
            sums[0] = sums[0] + lane_sums(image_real * real + image_imag * imag)
            if not last:
                send_reciprocal(3 + 2 * step, band, image_real, image_imag, sums)
            overlap[band] = space_wave[band, 0] * real + space_wave[band, 1] * imag
            for c in range(2):
                if step == 0:
                    search[band, c] = ahead[band, c]
                else:
                    search[band, c] = ahead[band, c] + beta * search[band, c]
            if last and band == 0:
                send_small(1, sums)
                base = left_dot(basis_y[0], total[...])
                moved = left_dot(basis_y[0], overlap[band])
        if last:
            break
        for band in range(BANDS):
            pot_real, pot_imag = receive_reciprocal(3 + 2 * step, band)
            values = bulk_row(3 + 2 * step, band, 5)
            _, c0_real, c0_imag, c1_real, c1_imag = values
            size = finish_curvature(rho[band], values)
            shifted = kin[...] - energy[0, band]
            real = search[band, 0]
            imag = search[band, 1]
            image_real = (
                shifted * real
                + pot_real
                + 2.0
                * (
                    wave[0, 0] * c0_real
                    - wave[0, 1] * c0_imag
                    + wave[1, 0] * c1_real
                    - wave[1, 1] * c1_imag
                )
            )
            image_imag = (
                shifted * imag
                + pot_imag
                + 2.0
                * (
                    wave[0, 0] * c0_imag
                    + wave[0, 1] * c0_real
                    + wave[1, 0] * c1_imag
                    + wave[1, 1] * c1_real
                )
            )
            send_step(
                4 + 2 * step,
                band,
                resid[band, 0] - size * image_real,
                resid[band, 1] - size * image_imag,
            )
            added = size * overlap[band]
            total[...] = added if step == 0 and band == 0 else total[...] + added
            for c in range(2):
                moved = size * search[band, c]
                answer[band, c] = moved if step == 0 else answer[band, c] + moved

    pl.semaphore_wait(met, pools - 1)
    size_first = finish_curvature(rho[0], receive_small(1, 5))
    store_columns(0, base + size_first * moved)
    turn(0, go_send.at[0], go_recv.at[0], True)
    store_columns(1, left_dot(basis_y[0], overlap[1]))
    share = jnp.where(lane_id[:1] == 0, rho[1] * (1.0 / parts), 0.0)
    go_send[1, pl.ds(local, devices, stride=slot), :] = jnp.broadcast_to(
        pack(sums + [share]), (devices, n)
    )
    turn(1, go_send.at[1], go_recv.at[1], True, local + 1)

    even = 2 * me
    frequency = jnp.where(
        pool == 0, even, jnp.where(pool == 1, jnp.where(me == 0, n // 2, even), even + 1)
    )

    def plain_square(index):
        k = jnp.where(index > n // 2, index - n // 2, index)
        return (k.astype(f32) * unit) ** 2

    squared = (
        plain_square(index_x) + (frequency.astype(f32) * unit) ** 2 + plain_square(index_z)
    )
    nonzero = (squared > 0).astype(f32)
    coulomb = 4.0 * math.pi * nonzero / (squared + (1.0 - nonzero))

    wait_turn(0, go_recv.at[0])
    wait_turn(1, go_recv.at[1], local + 1)
    sizes = []
    for other in range(pools):
        first = other * parts * slot + local
        rows = go_recv[1, pl.ds(first, parts, stride=slot), :]
        values = unpack(jnp.sum(rows, axis=0, keepdims=True), 6)
        sizes.append(finish_curvature(values[5], values[:5]))
    pieces = []
    for m in range(local):
        piece = None
        for other in range(pools):
            rows = pl.ds(other * parts * slot + m, parts, stride=slot)
            term = go_recv[0, rows, :] + sizes[other] * go_recv[1, rows, :]
            piece = term if piece is None else piece + term
        back_send[0, pl.ds(m, parts, stride=slot), :] = piece
        pieces.append(piece)
    turn(2, back_send.at[0], back_recv.at[0], False)


    field = left_dot(basis_x[...], jnp.concatenate(pieces, axis=0))
    field = coulomb * right_dot(field, basis_z[0])
    field = left_dot(spread_x[...], right_dot(field, basis_z[1]))
    back_send[1] = field
    turn(3, back_send.at[1], back_recv.at[1], False)

    for band in range(BANDS):
        size = size_first
        if band == 1:
            size = sum(jnp.where(pool == i, sizes[i], 0.0) for i in range(pools))
        for c in range(2):
            value = answer[band, c] + size * search[band, c]
            for m in range(local):
                coeff[band, c, pl.ds(m, n, stride=local), :] = lanes(value, m)
    results = [(coeff, coeff_out), (density, density_out), (hxc, hxc_out)]
    stores = [pltpu.make_async_copy(a, b, stored.at[i]) for i, (a, b) in enumerate(results)]
    stores[0].start()
    for phase in range(2 * CG_STEPS + 1):
        for band in range(BANDS):
            for half in range(HALVES):
                wait_bytes(half_bytes(phase, band, half), bulk_out.at[phase, band, half])
    for slot_id in range(2):
        wait_bytes(small_recv.at[slot_id, pl.ds(0, parts - 1)], small_out.at[slot_id])

    for i, result in enumerate((density, hxc)):
        wait_turn(2 + i, back_recv.at[i])
        columns = [back_recv[i, pl.ds(m, devices, stride=slot), :] for m in range(local)]
        whole = left_dot(basis_y[1], jnp.concatenate(columns, axis=1))
        for m in range(local):
            if i == 0:
                result[m] = lanes(whole, m)
            else:
                result[m] = lanes(whole, m) + xc[m] * density[m]
        stores[1 + i].start()


    for store in stores:
        store.wait()
    for which in range(4):
        rows = local + 1 if which == 1 else local
        wait_bytes(go_recv.at[0, pl.ds(0, rows * (devices - 1))], turn_out.at[which])


def hand_over(coeff, density, hxc, coeff_out, density_out, hxc_out, *scratch):
    held, held_density, held_hxc, came, gone = scratch
    moves = [(density, held_density, density_out), (hxc, held_hxc, hxc_out)]
    for b in range(BANDS):
        for c in range(2):
            moves.append((coeff.at[b, c], held.at[b, c], coeff_out.at[b, c]))
    first = [pltpu.make_async_copy(a, h, came.at[i]) for i, (a, h, _) in enumerate(moves)]
    second = [pltpu.make_async_copy(h, o, gone.at[i]) for i, (_, h, o) in enumerate(moves)]
    for copy in first:
        copy.start()
    for copy, onward in zip(first, second):
        copy.wait()
        onward.start()
    for copy in second:
        copy.wait()


def body(wave_coeff, band_energy, local_potential, perturbation, xc_kernel, parts, pools):
    n = wave_coeff.shape[-1]
    local = n // parts
    block = 2 * local * (local // HALVES)
    wide = local * n
    phases = 2 * CG_STEPS + 1
    room = block + 8
    slot_rows = 2 * local * parts
    operands = [
        wave_coeff.reshape(BANDS, 2, n * local, n),
        local_potential,
        perturbation,
        xc_kernel,
    ] + [jnp.asarray(t) for t in make_tables(n, parts)]
    anywhere = pl.BlockSpec(memory_space=pl.ANY)
    vmem = pl.BlockSpec(memory_space=pltpu.VMEM)
    field = pltpu.VMEM((BANDS, 2, n, wide), f32)
    dma = pltpu.SemaphoreType.DMA
    coeff, density, hxc = pl.pallas_call(
        functools.partial(kernel, n, parts, pools),
        out_shape=(
            jax.ShapeDtypeStruct(operands[0].shape, f32),
            jax.ShapeDtypeStruct((local, n, n), f32),
            jax.ShapeDtypeStruct((local, n, n), f32),
        ),
        in_specs=[anywhere, pl.BlockSpec(memory_space=pltpu.SMEM)] + [anywhere] * 10,
        out_specs=(anywhere, anywhere, anywhere),
        scratch_shapes=[
            pltpu.VMEM(operands[0].shape, f32),
            pltpu.VMEM((local, n, n), f32),
            pltpu.VMEM((local, n, n), f32),
        ]
        + [pltpu.VMEM(t.shape, t.dtype) for t in operands]
        + [
            field,
            pltpu.VMEM((n, wide), f32),
            pltpu.VMEM((n, wide), f32),
            field,
            field,
            field,
            field,
            field,
            field,
            pltpu.VMEM((BANDS, n, wide), f32),
            pltpu.VMEM((n, wide), f32),
            pltpu.VMEM((phases, BANDS, HALVES, parts, room, n), f32),
            pltpu.VMEM((phases, BANDS, HALVES, parts * room, n), f32),
            pltpu.VMEM((2, 1, n), f32),
            pltpu.VMEM((2, parts, 1, n), f32),
            pltpu.VMEM((2, pools * slot_rows, n), f32),
            pltpu.VMEM((2, pools * slot_rows, n), f32),
            pltpu.VMEM((2, slot_rows, n), f32),
            pltpu.VMEM((2, pools * slot_rows, n), f32),
            dma((11,)),
            dma((phases, BANDS, HALVES)),
            dma((phases, BANDS, HALVES)),
            dma((2,)),
            dma((2,)),
            dma((4,)),
            dma((4,)),
            pltpu.SemaphoreType.REGULAR,
            dma((3,)),
        ],
        compiler_params=pltpu.CompilerParams(
            collective_id=0, has_side_effects=True, vmem_limit_bytes=56 * 1024 * 1024
        ),
    )(operands[0], band_energy, *operands[1:])
    results = [coeff, density, hxc]
    coeff, density, hxc = pl.pallas_call(
        hand_over,
        out_shape=[jax.ShapeDtypeStruct(t.shape, f32) for t in results],
        in_specs=[anywhere] * 3,
        out_specs=[anywhere] * 3,
        scratch_shapes=[pltpu.VMEM(t.shape, f32) for t in results]
        + [dma((2 * BANDS + 2,)), dma((2 * BANDS + 2,))],
    )(*results)
    return coeff.reshape(wave_coeff.shape), density, hxc


def solution(mesh):
    return jax.shard_map(
        functools.partial(body, parts=mesh.shape["fft"], pools=mesh.shape["pool"]),
        mesh=mesh,
        in_specs=(
            P("pool", None, None, None, "fft", None),
            P("pool", None),
            P("fft", None, None),
            P("fft", None, None),
            P("fft", None, None),
        ),
        out_specs=(
            P("pool", None, None, None, "fft", None),
            P("fft", None, None),
            P("fft", None, None),
        ),
        check_vma=False,
    )
```

```python
import functools
import math

import jax
import jax.numpy as jnp
import ml_dtypes
import numpy as np
from jax import lax
from jax.experimental import pallas as pl
from jax.experimental.pallas import tpu as pltpu
from jax.sharding import PartitionSpec as P

CG_STEPS = 3
BANDS = 2
HALVES = 2
cell_length = 51.3
unit = 2.0 * math.pi / cell_length
MESH = pl.DeviceIdType.MESH
f32 = jnp.float32
bf16 = jnp.bfloat16


def left_table(rows, cols, n, sign, scale=1.0):
    rows, cols = np.array(rows), np.array(cols)
    phase = 2.0 * np.pi * ((rows[:, None, 1] * cols[None, :, 1]) % n) / n
    out_part, in_part = rows[:, None, 0], cols[None, :, 0]
    value = np.where(
        out_part == in_part,
        np.cos(phase),
        np.where(out_part == 1, sign, -sign) * np.sin(phase),
    )
    return value * scale


def split_table(table, axis):
    high = table.astype(ml_dtypes.bfloat16)
    low = (table - high.astype(np.float64)).astype(ml_dtypes.bfloat16)
    return np.concatenate([high, high, low], axis=axis)


def real_basis(n, order):
    k = np.array([f for f, _ in order])
    phase = 2.0 * np.pi * ((k[:, None] * np.arange(n)[None, :]) % n) / n
    is_sin = np.array([s for _, s in order])[:, None]
    rows = np.where(is_sin == 1, np.sin(phase), np.cos(phase))
    weight = np.where((k == 0) | (2 * k == n), 1.0, 2.0)[:, None] / n
    return rows, rows * weight


def make_tables(n, parts):
    local = n // parts
    natural = [(c, j) for c in range(2) for j in range(n)]
    by_owner = [(c, q * local + m) for q in range(parts) for c in range(2) for m in range(local)]
    split = np.array_split(np.arange(local), HALVES)
    by_local = [
        [(c, q * local + m) for c in range(2) for m in ms for q in range(parts)] for ms in split
    ]
    outgoing = np.stack(
        [split_table(left_table(by_owner, natural, n, sign), 1) for sign in (1.0, -1.0)]
    )
    incoming = np.stack(
        [
            np.stack([split_table(left_table(natural, cols, n, sign, size), 1) for cols in by_local])
            for sign, size in ((1.0, 1.0 / n**3), (-1.0, 1.0))
        ]
    )
    right = np.stack(
        [
            split_table(left_table(natural, natural, n, 1.0).T, 0),
            split_table(left_table(natural, natural, n, -1.0).T, 0),
        ]
    )
    half = n // 2
    plain = [(k, 0) for k in range(half + 1)] + [(k, 1) for k in range(1, half)]
    columns = [
        [(2 * p, 0) for p in range(parts)],
        [(half, 0)] + [(2 * p, 1) for p in range(1, parts)],
        [(2 * p + 1, 0) for p in range(parts)],
        [(2 * p + 1, 1) for p in range(parts)],
    ]
    y_rows, y_back = real_basis(n, sum(columns, []))
    rows, back = real_basis(n, plain)
    by_local_x = [q * local + m for m in range(local) for q in range(parts)]
    x_rows = rows[:, by_local_x]
    x_back = np.zeros((parts, 2 * local, n))
    x_back[:, :local] = back.T.reshape(parts, local, n)
    basis_y = np.stack([split_table(y_rows * 2.0 * n**3, 1), split_table(y_back.T, 1)])
    basis_z = np.stack([split_table(rows.T, 0), split_table(back, 0)])
    basis_x = split_table(x_rows, 1)
    spread_x = split_table(x_back.reshape(2 * n, n), 1)
    return [outgoing, right, incoming, basis_y, basis_x, spread_x, basis_z]


def halves(value):
    high = value.astype(bf16)
    low = (value - high.astype(f32)).astype(bf16)
    return high, low


def left_dot(table, data):
    high, low = halves(data)
    return jnp.dot(table, jnp.concatenate([high, low, high], axis=0), preferred_element_type=f32)


def right_dot(data, table):
    high, low = halves(data)
    return jnp.dot(jnp.concatenate([high, low, high], axis=1), table, preferred_element_type=f32)


def kernel(
    n,
    parts,
    pools,
    raw_hbm,
    energy,
    potential_hbm,
    perturbation_hbm,
    xc_hbm,
    outgoing_hbm,
    right_hbm,
    incoming_hbm,
    basis_y_hbm,
    basis_x_hbm,
    spread_x_hbm,
    basis_z_hbm,
    coeff_out,
    density_out,
    hxc_out,
    coeff,
    density,
    hxc,
    raw,
    potential,
    perturbation,
    xc,
    outgoing,
    right,
    incoming,
    basis_y,
    basis_x,
    spread_x,
    basis_z,
    wave,
    kin,
    pre,
    resid,
    search,
    answer,
    ahead,
    space_wave,
    space_search,
    overlap,
    total,
    send,
    recv,
    small_send,
    small_recv,
    go_send,
    go_recv,
    back_send,
    back_recv,
    loaded,
    bulk_out,
    bulk_in,
    small_out,
    small_in,
    turn_out,
    turn_in,
    met,
    stored,
):
    local = n // parts
    group = local // HALVES
    block = 2 * local * group
    room = block + 8
    devices = parts * pools
    inverse_total = 1.0 / n**3
    me = lax.axis_index("fft")
    pool = lax.axis_index("pool")
    def lanes(value, index):
        return value[:, index * n : (index + 1) * n]

    def turned(start, shift, size):
        index = start + shift
        return jnp.where(index >= size, index - size, index)

    def for_shifts(first, last, unroll, act):
        odd = (last - first) % unroll
        for shift in range(first, first + odd):
            act(turned(me, shift, parts))

        def step(index, _):
            shift = first + odd + index * unroll
            for more in range(unroll):
                act(turned(me, shift + more, parts))
            return 0

        lax.fori_loop(0, (last - first) // unroll, step, 0)

    def for_peers(act, unroll=4):
        for_shifts(parts // 2, parts, unroll, act)
        for_shifts(1, parts // 2, unroll, act)

    def for_devices(act):
        for pool_shift in (2, 1, 3):
            other_pool = turned(pool, pool_shift, pools)

            def at_pool(other, other_pool=other_pool):
                act(other, other_pool)

            for_shifts(parts // 2, parts, 8, at_pool)
            for_shifts(0, parts // 2, 8, at_pool)
        for_peers(lambda other: act(other, pool), 8)

    barrier = pltpu.get_barrier_semaphore()

    def greet(other, other_pool):
        pl.semaphore_signal(
            barrier, inc=1, device_id={"pool": other_pool, "fft": other}, device_id_type=MESH
        )

    for_peers(lambda other: greet(other, pool))
    for pool_shift in range(1, pools):
        greet(me, turned(pool, pool_shift, pools))
    loads = {}
    order = [
        (raw_hbm, raw),
        (right_hbm, right),
        (outgoing_hbm, outgoing),
        (incoming_hbm, incoming),
        (perturbation_hbm, perturbation),
        (potential_hbm, potential),
        (basis_y_hbm, basis_y),
        (basis_x_hbm, basis_x),
        (basis_z_hbm, basis_z),
        (spread_x_hbm, spread_x),
        (xc_hbm, xc),
    ]
    for i, (source, target) in enumerate(order):
        loads[i] = pltpu.make_async_copy(source, target, loaded.at[i])
        loads[i].start()


    def row_half(phase):
        return HALVES - 1 if phase >= 2 else None

    def used_rows(phase, half):
        return block + 1 if half == row_half(phase) else block

    def store_half(phase, band, half, value, row=None):
        for m in range(group):
            send[phase, band, half, :, 2 * local * m : 2 * local * (m + 1), :] = lanes(
                value, m
            ).reshape(parts, 2 * local, n)
        if half == row_half(phase):
            send[phase, band, half, :, block:room, :] = jnp.broadcast_to(
                pack(row), (parts, 8, n)
            )

    def start_half(phase, band, half):
        here = pl.multiple_of(me * room, room)
        used = used_rows(phase, half)

        def start(other):
            pltpu.make_async_remote_copy(
                src_ref=send.at[phase, band, half, other, pl.ds(0, used)],
                dst_ref=recv.at[phase, band, half, pl.ds(here, used)],
                send_sem=bulk_out.at[phase, band, half],
                recv_sem=bulk_in.at[phase, band, half],
                device_id={"fft": other},
                device_id_type=MESH,
            ).start()

        for_peers(start)
        recv[phase, band, half, pl.ds(here, room), :] = send[phase, band, half, me]

    def half_bytes(phase, band, half):
        return recv.at[phase, band, half, pl.ds(0, (parts - 1) * used_rows(phase, half))]

    def wait_bytes(ref, sem):
        pltpu.make_async_copy(ref, ref, sem).wait()

    def receive_bulk(phase, band, tables):
        out = None
        for half in range(HALVES):
            wait_bytes(half_bytes(phase, band, half), bulk_in.at[phase, band, half])
            rows = []
            for c in range(2):
                for m in range(group):
                    pieces = []
                    for other in range(local):
                        first = 2 * local * m + local * c + other
                        pieces.append(
                            recv[phase, band, half, pl.ds(first, parts, stride=room), :]
                        )
                    rows.append(jnp.concatenate(pieces, axis=1))
            part = left_dot(tables[half], jnp.concatenate(rows, axis=0))
            out = part if out is None else out + part
        return out

    row_id = lax.broadcasted_iota(jnp.int32, (8, n), 0)
    lane_id = lax.broadcasted_iota(jnp.int32, (8, n), 1)

    def lane_sums(value):
        column = jnp.sum(value, axis=0, keepdims=True)
        result = lanes(column, 0)
        for m in range(1, local):
            result = result + lanes(column, m)
        return result

    def pack(values):
        stacked = jnp.zeros((8, n), f32)
        for i, value in enumerate(values):
            stacked = jnp.where(row_id == i, value, stacked)
        sums = jnp.sum(stacked, axis=1, keepdims=True)
        return jnp.sum(jnp.where(row_id == lane_id, sums, 0.0), axis=0, keepdims=True)

    def unpack(row, count):
        return [
            jnp.sum(jnp.where(lane_id[:1] == i, row, 0.0), axis=1, keepdims=True)
            for i in range(count)
        ]

    def bulk_row(phase, band, count):
        rows = recv[phase, band, row_half(phase), pl.ds(block, parts, stride=room), :]
        return unpack(jnp.sum(rows, axis=0, keepdims=True), count)

    def send_small(which, values):
        row = pack(values)
        small_send[which] = row
        small_recv[which, me] = row

        def start(other):
            pltpu.make_async_remote_copy(
                src_ref=small_send.at[which],
                dst_ref=small_recv.at[which, me],
                send_sem=small_out.at[which],
                recv_sem=small_in.at[which],
                device_id={"fft": other},
                device_id_type=MESH,
            ).start()

        for_peers(start)

    def receive_small(which, count):
        wait_bytes(small_recv.at[which, pl.ds(0, parts - 1)], small_in.at[which])
        return unpack(jnp.sum(small_recv[which], axis=0), count)


    def along_z(real, imag, table):
        count = real.shape[1] // n
        rows = jnp.concatenate(
            [jnp.concatenate([lanes(real, m), lanes(imag, m)], axis=1) for m in range(count)],
            axis=0,
        )
        out = right_dot(rows, table)
        picked = [out[m * n : (m + 1) * n] for m in range(count)]
        return (
            jnp.concatenate([lanes(v, 0) for v in picked], axis=1),
            jnp.concatenate([lanes(v, 1) for v in picked], axis=1),
        )

    def half_of(value, half):
        return value[:, half * group * n : (half + 1) * group * n]

    def send_real(phase, band, real, imag, row=None):
        for half in range(HALVES):
            part = jnp.concatenate(
                along_z(half_of(real, half), half_of(imag, half), right[0]), axis=0
            )
            store_half(phase, band, half, left_dot(outgoing[0], part), row)
            if phase == 0 and band == 0 and half == 0:
                pl.semaphore_wait(barrier, parts + pools - 2)
            start_half(phase, band, half)

    def receive_real(phase, band):
        out = receive_bulk(phase, band, incoming[0])
        return out[:n], out[n:]

    def send_reciprocal(phase, band, real, imag, row=None):
        for half in range(HALVES):
            part = jnp.concatenate([half_of(real, half), half_of(imag, half)], axis=0)
            store_half(phase, band, half, left_dot(outgoing[1], part), row)
            start_half(phase, band, half)

    def receive_reciprocal(phase, band):
        out = receive_bulk(phase, band, incoming[1])
        return along_z(out[:n], out[n:], right[1])


    loads[0].wait()
    for band in range(BANDS):
        for c in range(2):
            for m in range(local):
                wave[band, c, :, m * n : (m + 1) * n] = raw[
                    band, c, pl.ds(m, n, stride=local), :
                ]
        if band == 0:
            loads[1].wait()
            loads[2].wait()
        send_real(0, band, wave[band, 0], wave[band, 1])

    for pool_shift in range(1, pools):
        pl.semaphore_signal(
            met,
            inc=1,
            device_id={"pool": turned(pool, pool_shift, pools), "fft": me},
            device_id_type=MESH,
        )

    def wavenumber(index):
        signed = jnp.where(2 * index >= n, index - n, index)
        return signed.astype(f32) * unit

    def offset(axis_number):
        bit = lax.rem(pool // 2**axis_number, 2)
        return (0.5 * bit.astype(f32) - 0.25) * unit

    index_x = lax.broadcasted_iota(jnp.int32, (n, n), 0)
    index_z = lax.broadcasted_iota(jnp.int32, (n, n), 1)
    square_x = (wavenumber(index_x) + offset(0)) ** 2
    square_z = (wavenumber(index_z) + offset(2)) ** 2
    for m in range(local):
        square_y = (wavenumber(me * local + m) + offset(1)) ** 2
        value = 0.5 * (square_x + square_y + square_z)
        kin[:, m * n : (m + 1) * n] = value
        pre[:, m * n : (m + 1) * n] = 1.0 / (value + 1.0)

    def wide(ref):
        return jnp.concatenate([ref[m] for m in range(local)], axis=1)


    overlaps = []
    for i in range(3, len(order)):
        loads[i].wait()
    for band in range(BANDS):
        real, imag = receive_real(0, band)
        space_wave[band, 0] = real
        space_wave[band, 1] = imag
        change = wide(perturbation)
        changed_real = change * real
        changed_imag = change * imag
        overlaps.append(lane_sums(changed_real * real + changed_imag * imag))
        if band == BANDS - 1:
            first_real = space_wave[0, 0]
            first_imag = space_wave[0, 1]
            overlaps.append(lane_sums(first_real * changed_real + first_imag * changed_imag))
            overlaps.append(lane_sums(first_real * changed_imag - first_imag * changed_real))
            send_small(0, overlaps)
        send_reciprocal(1, band, changed_real, changed_imag)

    def products(band, real, imag):
        sums = []
        for m in range(BANDS):
            sums.append(lane_sums(wave[m, 0] * real + wave[m, 1] * imag))
            sums.append(lane_sums(wave[m, 0] * imag - wave[m, 1] * real))
        return [value * inverse_total for value in sums]

    def kinetic_sum(band, left_real, left_imag, right_real, right_imag):
        shifted = kin[...] - energy[0, band]
        return lane_sums(shifted * (left_real * right_real + left_imag * right_imag)) * inverse_total

    def send_step(phase, band, resid_real, resid_imag):
        real = pre[...] * resid_real
        imag = pre[...] * resid_imag
        row = [lane_sums(resid_real * real + resid_imag * imag) * inverse_total]
        resid[band, 0] = resid_real
        resid[band, 1] = resid_imag
        ahead[band, 0] = real
        ahead[band, 1] = imag
        send_real(phase, band, real, imag, row)


    partial = [None] * BANDS
    rho = [None] * BANDS
    for band in range(BANDS):
        real, imag = receive_reciprocal(1, band)
        if band == 0:
            same0, same1, cross_real, cross_imag = receive_small(0, 4)
        if band == 0:
            m0_real, m0_imag, m1_real, m1_imag = same0, 0.0 * same0, cross_real, -cross_imag
        else:
            m0_real, m0_imag, m1_real, m1_imag = cross_real, cross_imag, same1, 0.0 * same1
        resid_real = (
            wave[0, 0] * m0_real
            - wave[0, 1] * m0_imag
            + wave[1, 0] * m1_real
            - wave[1, 1] * m1_imag
            - real
        )
        resid_imag = (
            wave[0, 0] * m0_imag
            + wave[0, 1] * m0_real
            + wave[1, 0] * m1_imag
            + wave[1, 1] * m1_real
            - imag
        )
        send_step(2, band, resid_real, resid_imag)


    def finish_curvature(product, values):
        curvature, c0_real, c0_imag, c1_real, c1_imag = values
        curvature = curvature + 2.0 * (
            c0_real * c0_real + c0_imag * c0_imag + c1_real * c1_real + c1_imag * c1_imag
        )
        return product / curvature


    slot = 2 * local

    def turn(which, source, target, all_columns, rows=local):
        here = pl.multiple_of((pool * parts + me) * slot, slot)
        own = here if all_columns else pl.multiple_of(me * slot, slot)
        target[pl.ds(here, rows), :] = source[pl.ds(own, rows), :]

        def start(other, other_pool):
            there = other_pool * parts + other if all_columns else other
            there = pl.multiple_of(there * slot, slot)
            pltpu.make_async_remote_copy(
                src_ref=source.at[pl.ds(there, rows)],
                dst_ref=target.at[pl.ds(here, rows)],
                send_sem=turn_out.at[which],
                recv_sem=turn_in.at[which],
                device_id={"pool": other_pool, "fft": other},
                device_id_type=MESH,
            ).start()

        for_devices(start)

    def wait_turn(which, target, rows=local):
        wait_bytes(target.at[pl.ds(0, rows * (devices - 1))], turn_in.at[which])

    def store_columns(which, columns):
        for m in range(local):
            go_send[which, pl.ds(m, devices, stride=slot), :] = lanes(columns, m)

    for step in range(CG_STEPS):
        last = step + 1 == CG_STEPS
        for band in range(BANDS):
            real, imag = ahead[band, 0], ahead[band, 1]
            sums = [kinetic_sum(band, real, imag, real, imag)] + products(band, real, imag)
            if step > 0:
                cross = kinetic_sum(band, real, imag, search[band, 0], search[band, 1])
            if last and band == 1:
                pl.semaphore_wait(met, pools - 1)
                size_first = finish_curvature(rho[0], receive_small(1, 5))
                store_columns(0, base + size_first * moved)
                turn(0, go_send.at[0], go_recv.at[0], True)
            real, imag = receive_real(2 + 2 * step, band)
            (rho_new,) = bulk_row(2 + 2 * step, band, 1)
            if step > 0:
                beta = rho_new / rho[band]
                before = partial[band]
                sums[0] = sums[0] + beta * (2.0 * cross + beta * before[0])
                for i in range(1, 1 + 2 * BANDS):
                    sums[i] = sums[i] + beta * before[i]
                real = real + beta * space_search[band, 0]
                imag = imag + beta * space_search[band, 1]
            rho[band] = rho_new
            partial[band] = list(sums)
            if not last:
                space_search[band, 0] = real
                space_search[band, 1] = imag
            level = wide(potential)
            image_real = level * real
            image_imag = level * imag
            sums[0] = sums[0] + lane_sums(image_real * real + image_imag * imag)
            if not last:
                send_reciprocal(3 + 2 * step, band, image_real, image_imag, sums)
            overlap[band] = space_wave[band, 0] * real + space_wave[band, 1] * imag
            for c in range(2):
                if step == 0:
                    search[band, c] = ahead[band, c]
                else:
                    search[band, c] = ahead[band, c] + beta * search[band, c]
            if last and band == 0:
                send_small(1, sums)
                base = left_dot(basis_y[0], total[...])
                moved = left_dot(basis_y[0], overlap[band])
        if last:
            break
        for band in range(BANDS):
            pot_real, pot_imag = receive_reciprocal(3 + 2 * step, band)
            values = bulk_row(3 + 2 * step, band, 5)
            _, c0_real, c0_imag, c1_real, c1_imag = values
            size = finish_curvature(rho[band], values)
            shifted = kin[...] - energy[0, band]
            real = search[band, 0]
            imag = search[band, 1]
            image_real = (
                shifted * real
                + pot_real
                + 2.0
                * (
                    wave[0, 0] * c0_real
                    - wave[0, 1] * c0_imag
                    + wave[1, 0] * c1_real
                    - wave[1, 1] * c1_imag
                )
            )
            image_imag = (
                shifted * imag
                + pot_imag
                + 2.0
                * (
                    wave[0, 0] * c0_imag
                    + wave[0, 1] * c0_real
                    + wave[1, 0] * c1_imag
                    + wave[1, 1] * c1_real
                )
            )
            send_step(
                4 + 2 * step,
                band,
                resid[band, 0] - size * image_real,
                resid[band, 1] - size * image_imag,
            )
            added = size * overlap[band]
            total[...] = added if step == 0 and band == 0 else total[...] + added
            for c in range(2):
                moved = size * search[band, c]
                answer[band, c] = moved if step == 0 else answer[band, c] + moved

    store_columns(1, left_dot(basis_y[0], overlap[1]))
    share = jnp.where(lane_id[:1] == 0, rho[1] * (1.0 / parts), 0.0)
    go_send[1, pl.ds(local, devices, stride=slot), :] = jnp.broadcast_to(
        pack(sums + [share]), (devices, n)
    )
    turn(1, go_send.at[1], go_recv.at[1], True, local + 1)

    even = 2 * me
    frequency = jnp.where(
        pool == 0, even, jnp.where(pool == 1, jnp.where(me == 0, n // 2, even), even + 1)
    )

    def plain_square(index):
        k = jnp.where(index > n // 2, index - n // 2, index)
        return (k.astype(f32) * unit) ** 2

    squared = (
        plain_square(index_x) + (frequency.astype(f32) * unit) ** 2 + plain_square(index_z)
    )
    nonzero = (squared > 0).astype(f32)
    coulomb = 4.0 * math.pi * nonzero / (squared + (1.0 - nonzero))

    wait_turn(0, go_recv.at[0])
    wait_turn(1, go_recv.at[1], local + 1)
    gathered = []
    for other in range(pools):
        first = other * parts * slot + local
        rows = go_recv[1, pl.ds(first, parts, stride=slot), :]
        gathered.append(jnp.sum(rows, axis=0, keepdims=True))
    gathered = jnp.concatenate(gathered, axis=0)
    lane = lane_id[:pools]
    terms = jnp.where(lane == 0, gathered, 2.0 * gathered * gathered)
    curvature = jnp.sum(jnp.where(lane < 1 + 2 * BANDS, terms, 0.0), axis=1, keepdims=True)
    product = jnp.sum(jnp.where(lane == 1 + 2 * BANDS, gathered, 0.0), axis=1, keepdims=True)
    quotient = product / curvature
    sizes = [quotient[other : other + 1] for other in range(pools)]
    pieces = []
    for m in range(local):
        piece = None
        for other in range(pools):
            rows = pl.ds(other * parts * slot + m, parts, stride=slot)
            term = go_recv[0, rows, :] + sizes[other] * go_recv[1, rows, :]
            piece = term if piece is None else piece + term
        back_send[0, pl.ds(m, parts, stride=slot), :] = piece
        pieces.append(piece)
    turn(2, back_send.at[0], back_recv.at[0], False)


    field = left_dot(basis_x[...], jnp.concatenate(pieces, axis=0))
    field = coulomb * right_dot(field, basis_z[0])
    field = left_dot(spread_x[...], right_dot(field, basis_z[1]))
    back_send[1] = field
    turn(3, back_send.at[1], back_recv.at[1], False)

    for band in range(BANDS):
        size = size_first
        if band == 1:
            size = sum(jnp.where(pool == i, sizes[i], 0.0) for i in range(pools))
        for c in range(2):
            value = answer[band, c] + size * search[band, c]
            for m in range(local):
                coeff[band, c, pl.ds(m, n, stride=local), :] = lanes(value, m)
    results = [(coeff, coeff_out), (density, density_out), (hxc, hxc_out)]
    stores = [pltpu.make_async_copy(a, b, stored.at[i]) for i, (a, b) in enumerate(results)]
    stores[0].start()
    for phase in range(2 * CG_STEPS + 1):
        for band in range(BANDS):
            for half in range(HALVES):
                wait_bytes(half_bytes(phase, band, half), bulk_out.at[phase, band, half])
    for slot_id in range(2):
        wait_bytes(small_recv.at[slot_id, pl.ds(0, parts - 1)], small_out.at[slot_id])

    for i, result in enumerate((density, hxc)):
        wait_turn(2 + i, back_recv.at[i])
        columns = [back_recv[i, pl.ds(m, devices, stride=slot), :] for m in range(local)]
        whole = left_dot(basis_y[1], jnp.concatenate(columns, axis=1))
        for m in range(local):
            if i == 0:
                result[m] = lanes(whole, m)
            else:
                result[m] = lanes(whole, m) + xc[m] * density[m]
        stores[1 + i].start()


    for store in stores:
        store.wait()
    for which in range(4):
        rows = local + 1 if which == 1 else local
        wait_bytes(go_recv.at[0, pl.ds(0, rows * (devices - 1))], turn_out.at[which])


def hand_over(coeff, density, hxc, coeff_out, density_out, hxc_out, *scratch):
    held, held_density, held_hxc, came, gone = scratch
    moves = [(density, held_density, density_out), (hxc, held_hxc, hxc_out)]
    for b in range(BANDS):
        for c in range(2):
            moves.append((coeff.at[b, c], held.at[b, c], coeff_out.at[b, c]))
    first = [pltpu.make_async_copy(a, h, came.at[i]) for i, (a, h, _) in enumerate(moves)]
    second = [pltpu.make_async_copy(h, o, gone.at[i]) for i, (_, h, o) in enumerate(moves)]
    for copy in first:
        copy.start()
    for copy, onward in zip(first, second):
        copy.wait()
        onward.start()
    for copy in second:
        copy.wait()


def body(wave_coeff, band_energy, local_potential, perturbation, xc_kernel, parts, pools):
    n = wave_coeff.shape[-1]
    local = n // parts
    block = 2 * local * (local // HALVES)
    wide = local * n
    phases = 2 * CG_STEPS + 1
    room = block + 8
    slot_rows = 2 * local * parts
    operands = [
        wave_coeff.reshape(BANDS, 2, n * local, n),
        local_potential,
        perturbation,
        xc_kernel,
    ] + [jnp.asarray(t) for t in make_tables(n, parts)]
    anywhere = pl.BlockSpec(memory_space=pl.ANY)
    vmem = pl.BlockSpec(memory_space=pltpu.VMEM)
    field = pltpu.VMEM((BANDS, 2, n, wide), f32)
    dma = pltpu.SemaphoreType.DMA
    coeff, density, hxc = pl.pallas_call(
        functools.partial(kernel, n, parts, pools),
        out_shape=(
            jax.ShapeDtypeStruct(operands[0].shape, f32),
            jax.ShapeDtypeStruct((local, n, n), f32),
            jax.ShapeDtypeStruct((local, n, n), f32),
        ),
        in_specs=[anywhere, pl.BlockSpec(memory_space=pltpu.SMEM)] + [anywhere] * 10,
        out_specs=(anywhere, anywhere, anywhere),
        scratch_shapes=[
            pltpu.VMEM(operands[0].shape, f32),
            pltpu.VMEM((local, n, n), f32),
            pltpu.VMEM((local, n, n), f32),
        ]
        + [pltpu.VMEM(t.shape, t.dtype) for t in operands]
        + [
            field,
            pltpu.VMEM((n, wide), f32),
            pltpu.VMEM((n, wide), f32),
            field,
            field,
            field,
            field,
            field,
            field,
            pltpu.VMEM((BANDS, n, wide), f32),
            pltpu.VMEM((n, wide), f32),
            pltpu.VMEM((phases, BANDS, HALVES, parts, room, n), f32),
            pltpu.VMEM((phases, BANDS, HALVES, parts * room, n), f32),
            pltpu.VMEM((2, 1, n), f32),
            pltpu.VMEM((2, parts, 1, n), f32),
            pltpu.VMEM((2, pools * slot_rows, n), f32),
            pltpu.VMEM((2, pools * slot_rows, n), f32),
            pltpu.VMEM((2, slot_rows, n), f32),
            pltpu.VMEM((2, pools * slot_rows, n), f32),
            dma((11,)),
            dma((phases, BANDS, HALVES)),
            dma((phases, BANDS, HALVES)),
            dma((2,)),
            dma((2,)),
            dma((4,)),
            dma((4,)),
            pltpu.SemaphoreType.REGULAR,
            dma((3,)),
        ],
        compiler_params=pltpu.CompilerParams(
            collective_id=0, has_side_effects=True, vmem_limit_bytes=56 * 1024 * 1024
        ),
    )(operands[0], band_energy, *operands[1:])
    results = [coeff, density, hxc]
    coeff, density, hxc = pl.pallas_call(
        hand_over,
        out_shape=[jax.ShapeDtypeStruct(t.shape, f32) for t in results],
        in_specs=[anywhere] * 3,
        out_specs=[anywhere] * 3,
        scratch_shapes=[pltpu.VMEM(t.shape, f32) for t in results]
        + [dma((2 * BANDS + 2,)), dma((2 * BANDS + 2,))],
    )(*results)
    return coeff.reshape(wave_coeff.shape), density, hxc


def solution(mesh):
    return jax.shard_map(
        functools.partial(body, parts=mesh.shape["fft"], pools=mesh.shape["pool"]),
        mesh=mesh,
        in_specs=(
            P("pool", None, None, None, "fft", None),
            P("pool", None),
            P("fft", None, None),
            P("fft", None, None),
            P("fft", None, None),
        ),
        out_specs=(
            P("pool", None, None, None, "fft", None),
            P("fft", None, None),
            P("fft", None, None),
        ),
        check_vma=False,
    )
```

```python
import functools
import math

import jax
import jax.numpy as jnp
import ml_dtypes
import numpy as np
from jax import lax
from jax.experimental import pallas as pl
from jax.experimental.pallas import tpu as pltpu
from jax.sharding import PartitionSpec as P

CG_STEPS = 3
BANDS = 2
HALVES = 2
cell_length = 51.3
unit = 2.0 * math.pi / cell_length
MESH = pl.DeviceIdType.MESH
f32 = jnp.float32
bf16 = jnp.bfloat16


def left_table(rows, cols, n, sign, scale=1.0):
    rows, cols = np.array(rows), np.array(cols)
    phase = 2.0 * np.pi * ((rows[:, None, 1] * cols[None, :, 1]) % n) / n
    out_part, in_part = rows[:, None, 0], cols[None, :, 0]
    value = np.where(
        out_part == in_part,
        np.cos(phase),
        np.where(out_part == 1, sign, -sign) * np.sin(phase),
    )
    return value * scale


def split_table(table, axis):
    high = table.astype(ml_dtypes.bfloat16)
    low = (table - high.astype(np.float64)).astype(ml_dtypes.bfloat16)
    return np.concatenate([high, high, low], axis=axis)


def real_basis(n, order):
    k = np.array([f for f, _ in order])
    phase = 2.0 * np.pi * ((k[:, None] * np.arange(n)[None, :]) % n) / n
    is_sin = np.array([s for _, s in order])[:, None]
    rows = np.where(is_sin == 1, np.sin(phase), np.cos(phase))
    weight = np.where((k == 0) | (2 * k == n), 1.0, 2.0)[:, None] / n
    return rows, rows * weight


def make_tables(n, parts):
    local = n // parts
    natural = [(c, j) for c in range(2) for j in range(n)]
    by_owner = [(c, q * local + m) for q in range(parts) for c in range(2) for m in range(local)]
    split = np.array_split(np.arange(local), HALVES)
    by_local = [
        [(c, q * local + m) for c in range(2) for m in ms for q in range(parts)] for ms in split
    ]
    outgoing = np.stack(
        [split_table(left_table(by_owner, natural, n, sign), 1) for sign in (1.0, -1.0)]
    )
    incoming = np.stack(
        [
            np.stack([split_table(left_table(natural, cols, n, sign, size), 1) for cols in by_local])
            for sign, size in ((1.0, 1.0 / n**3), (-1.0, 1.0))
        ]
    )
    right = np.stack(
        [
            split_table(left_table(natural, natural, n, 1.0).T, 0),
            split_table(left_table(natural, natural, n, -1.0).T, 0),
        ]
    )
    half = n // 2
    plain = [(k, 0) for k in range(half + 1)] + [(k, 1) for k in range(1, half)]
    columns = [
        [(2 * p, 0) for p in range(parts)],
        [(half, 0)] + [(2 * p, 1) for p in range(1, parts)],
        [(2 * p + 1, 0) for p in range(parts)],
        [(2 * p + 1, 1) for p in range(parts)],
    ]
    y_rows, y_back = real_basis(n, sum(columns, []))
    rows, back = real_basis(n, plain)
    by_local_x = [q * local + m for m in range(local) for q in range(parts)]
    x_rows = rows[:, by_local_x]
    x_back = np.zeros((parts, 2 * local, n))
    x_back[:, :local] = back.T.reshape(parts, local, n)
    basis_y = np.stack([split_table(y_rows * 2.0 * n**3, 1), split_table(y_back.T, 1)])
    basis_z = np.stack([split_table(rows.T, 0), split_table(back, 0)])
    basis_x = split_table(x_rows, 1)
    spread_x = split_table(x_back.reshape(2 * n, n), 1)
    return [outgoing, right, incoming, basis_y, basis_x, spread_x, basis_z]


def halves(value):
    high = value.astype(bf16)
    low = (value - high.astype(f32)).astype(bf16)
    return high, low


def left_dot(table, data):
    high, low = halves(data)
    return jnp.dot(table, jnp.concatenate([high, low, high], axis=0), preferred_element_type=f32)


def right_dot(data, table):
    high, low = halves(data)
    return jnp.dot(jnp.concatenate([high, low, high], axis=1), table, preferred_element_type=f32)


def kernel(
    n,
    parts,
    pools,
    grid,
    raw_hbm,
    energy,
    potential_hbm,
    perturbation_hbm,
    xc_hbm,
    outgoing_hbm,
    right_hbm,
    incoming_hbm,
    basis_y_hbm,
    basis_x_hbm,
    spread_x_hbm,
    basis_z_hbm,
    coeff_out,
    density_out,
    hxc_out,
    coeff,
    density,
    hxc,
    raw,
    potential,
    perturbation,
    xc,
    outgoing,
    right,
    incoming,
    basis_y,
    basis_x,
    spread_x,
    basis_z,
    wave,
    kin,
    pre,
    resid,
    search,
    answer,
    ahead,
    space_wave,
    space_search,
    overlap,
    total,
    send,
    recv,
    small_send,
    small_recv,
    go_send,
    go_recv,
    back_send,
    back_recv,
    loaded,
    bulk_out,
    bulk_in,
    small_out,
    small_in,
    turn_out,
    turn_in,
    met,
    stored,
):
    local = n // parts
    group = local // HALVES
    block = 2 * local * group
    room = block + 8
    devices = parts * pools
    inverse_total = 1.0 / n**3
    me = lax.axis_index("fft")
    pool = lax.axis_index("pool")
    def lanes(value, index):
        return value[:, index * n : (index + 1) * n]

    def turned(start, shift, size):
        index = start + shift
        return jnp.where(index >= size, index - size, index)

    size_z, size_x, size_c = grid
    plane = size_x * size_c
    my_z, my_x, my_c = me // plane, lax.rem(me // size_c, size_x), lax.rem(me, size_c)
    in_plane = [
        turned(my_x, dx, size_x) * size_c + turned(my_c, dc, size_c)
        for dx in reversed(range(size_x))
        for dc in reversed(range(size_c))
    ]

    def for_planes(first, act):
        def step(index, _):
            base = turned(my_z, size_z - 1 - index, size_z) * plane
            for place in in_plane:
                act(base + place)
            return 0

        lax.fori_loop(0, size_z - first, step, 0)

    def for_peers(act):
        for_planes(1, act)
        for place in in_plane[:-1]:
            act(my_z * plane + place)

    def for_devices(act):
        for pool_shift in (2, 1, 3):
            other_pool = turned(pool, pool_shift, pools)

            def at_pool(other, other_pool=other_pool):
                act(other, other_pool)

            for_planes(0, at_pool)
        for_peers(lambda other: act(other, pool))

    barrier = pltpu.get_barrier_semaphore()

    def greet(other, other_pool):
        pl.semaphore_signal(
            barrier, inc=1, device_id={"pool": other_pool, "fft": other}, device_id_type=MESH
        )

    for_peers(lambda other: greet(other, pool))
    for pool_shift in range(1, pools):
        greet(me, turned(pool, pool_shift, pools))
    loads = {}
    order = [
        (raw_hbm, raw),
        (right_hbm, right),
        (outgoing_hbm, outgoing),
        (incoming_hbm, incoming),
        (perturbation_hbm, perturbation),
        (potential_hbm, potential),
        (basis_y_hbm, basis_y),
        (basis_x_hbm, basis_x),
        (basis_z_hbm, basis_z),
        (spread_x_hbm, spread_x),
        (xc_hbm, xc),
    ]
    for i, (source, target) in enumerate(order):
        loads[i] = pltpu.make_async_copy(source, target, loaded.at[i])
        loads[i].start()


    def row_half(phase):
        return HALVES - 1 if phase >= 2 else None

    def used_rows(phase, half):
        return block + 1 if half == row_half(phase) else block

    def store_half(phase, band, half, value, row=None):
        for m in range(group):
            send[phase, band, half, :, 2 * local * m : 2 * local * (m + 1), :] = lanes(
                value, m
            ).reshape(parts, 2 * local, n)
        if half == row_half(phase):
            send[phase, band, half, :, block:room, :] = jnp.broadcast_to(
                pack(row), (parts, 8, n)
            )

    def start_half(phase, band, half):
        here = pl.multiple_of(me * room, room)
        used = used_rows(phase, half)

        def start(other):
            pltpu.make_async_remote_copy(
                src_ref=send.at[phase, band, half, other, pl.ds(0, used)],
                dst_ref=recv.at[phase, band, half, pl.ds(here, used)],
                send_sem=bulk_out.at[phase, band, half],
                recv_sem=bulk_in.at[phase, band, half],
                device_id={"fft": other},
                device_id_type=MESH,
            ).start()

        for_peers(start)
        recv[phase, band, half, pl.ds(here, room), :] = send[phase, band, half, me]

    def half_bytes(phase, band, half):
        return recv.at[phase, band, half, pl.ds(0, (parts - 1) * used_rows(phase, half))]

    def wait_bytes(ref, sem):
        pltpu.make_async_copy(ref, ref, sem).wait()

    def receive_bulk(phase, band, tables):
        out = None
        for half in range(HALVES):
            wait_bytes(half_bytes(phase, band, half), bulk_in.at[phase, band, half])
            rows = []
            for c in range(2):
                for m in range(group):
                    pieces = []
                    for other in range(local):
                        first = 2 * local * m + local * c + other
                        pieces.append(
                            recv[phase, band, half, pl.ds(first, parts, stride=room), :]
                        )
                    rows.append(jnp.concatenate(pieces, axis=1))
            part = left_dot(tables[half], jnp.concatenate(rows, axis=0))
            out = part if out is None else out + part
        return out

    row_id = lax.broadcasted_iota(jnp.int32, (8, n), 0)
    lane_id = lax.broadcasted_iota(jnp.int32, (8, n), 1)

    def lane_sums(value):
        column = jnp.sum(value, axis=0, keepdims=True)
        result = lanes(column, 0)
        for m in range(1, local):
            result = result + lanes(column, m)
        return result

    def pack(values):
        stacked = jnp.zeros((8, n), f32)
        for i, value in enumerate(values):
            stacked = jnp.where(row_id == i, value, stacked)
        sums = jnp.sum(stacked, axis=1, keepdims=True)
        return jnp.sum(jnp.where(row_id == lane_id, sums, 0.0), axis=0, keepdims=True)

    def unpack(row, count):
        return [
            jnp.sum(jnp.where(lane_id[:1] == i, row, 0.0), axis=1, keepdims=True)
            for i in range(count)
        ]

    def bulk_row(phase, band, count):
        rows = recv[phase, band, row_half(phase), pl.ds(block, parts, stride=room), :]
        return unpack(jnp.sum(rows, axis=0, keepdims=True), count)

    def send_small(which, values):
        row = pack(values)
        small_send[which] = row
        small_recv[which, me] = row

        def start(other):
            pltpu.make_async_remote_copy(
                src_ref=small_send.at[which],
                dst_ref=small_recv.at[which, me],
                send_sem=small_out.at[which],
                recv_sem=small_in.at[which],
                device_id={"fft": other},
                device_id_type=MESH,
            ).start()

        for_peers(start)

    def receive_small(which, count):
        wait_bytes(small_recv.at[which, pl.ds(0, parts - 1)], small_in.at[which])
        return unpack(jnp.sum(small_recv[which], axis=0), count)


    def along_z(real, imag, table):
        count = real.shape[1] // n
        rows = jnp.concatenate(
            [jnp.concatenate([lanes(real, m), lanes(imag, m)], axis=1) for m in range(count)],
            axis=0,
        )
        out = right_dot(rows, table)
        picked = [out[m * n : (m + 1) * n] for m in range(count)]
        return (
            jnp.concatenate([lanes(v, 0) for v in picked], axis=1),
            jnp.concatenate([lanes(v, 1) for v in picked], axis=1),
        )

    def half_of(value, half):
        return value[:, half * group * n : (half + 1) * group * n]

    def send_real(phase, band, real, imag, row=None):
        for half in range(HALVES):
            part = jnp.concatenate(
                along_z(half_of(real, half), half_of(imag, half), right[0]), axis=0
            )
            store_half(phase, band, half, left_dot(outgoing[0], part), row)
            if phase == 0 and band == 0 and half == 0:
                pl.semaphore_wait(barrier, parts + pools - 2)
            start_half(phase, band, half)

    def receive_real(phase, band):
        out = receive_bulk(phase, band, incoming[0])
        return out[:n], out[n:]

    def send_reciprocal(phase, band, real, imag, row=None):
        for half in range(HALVES):
            part = jnp.concatenate([half_of(real, half), half_of(imag, half)], axis=0)
            store_half(phase, band, half, left_dot(outgoing[1], part), row)
            start_half(phase, band, half)

    def receive_reciprocal(phase, band):
        out = receive_bulk(phase, band, incoming[1])
        return along_z(out[:n], out[n:], right[1])


    loads[0].wait()
    for band in range(BANDS):
        for c in range(2):
            for m in range(local):
                wave[band, c, :, m * n : (m + 1) * n] = raw[
                    band, c, pl.ds(m, n, stride=local), :
                ]
        if band == 0:
            loads[1].wait()
            loads[2].wait()
        send_real(0, band, wave[band, 0], wave[band, 1])

    for pool_shift in range(1, pools):
        pl.semaphore_signal(
            met,
            inc=1,
            device_id={"pool": turned(pool, pool_shift, pools), "fft": me},
            device_id_type=MESH,
        )

    def wavenumber(index):
        signed = jnp.where(2 * index >= n, index - n, index)
        return signed.astype(f32) * unit

    def offset(axis_number):
        bit = lax.rem(pool // 2**axis_number, 2)
        return (0.5 * bit.astype(f32) - 0.25) * unit

    index_x = lax.broadcasted_iota(jnp.int32, (n, n), 0)
    index_z = lax.broadcasted_iota(jnp.int32, (n, n), 1)
    square_x = (wavenumber(index_x) + offset(0)) ** 2
    square_z = (wavenumber(index_z) + offset(2)) ** 2
    for m in range(local):
        square_y = (wavenumber(me * local + m) + offset(1)) ** 2
        value = 0.5 * (square_x + square_y + square_z)
        kin[:, m * n : (m + 1) * n] = value
        pre[:, m * n : (m + 1) * n] = 1.0 / (value + 1.0)

    def wide(ref):
        return jnp.concatenate([ref[m] for m in range(local)], axis=1)


    overlaps = []
    for i in range(3, len(order)):
        loads[i].wait()
    for band in range(BANDS):
        real, imag = receive_real(0, band)
        space_wave[band, 0] = real
        space_wave[band, 1] = imag
        change = wide(perturbation)
        changed_real = change * real
        changed_imag = change * imag
        overlaps.append(lane_sums(changed_real * real + changed_imag * imag))
        if band == BANDS - 1:
            first_real = space_wave[0, 0]
            first_imag = space_wave[0, 1]
            overlaps.append(lane_sums(first_real * changed_real + first_imag * changed_imag))
            overlaps.append(lane_sums(first_real * changed_imag - first_imag * changed_real))
            send_small(0, overlaps)
        send_reciprocal(1, band, changed_real, changed_imag)

    def products(band, real, imag):
        sums = []
        for m in range(BANDS):
            sums.append(lane_sums(wave[m, 0] * real + wave[m, 1] * imag))
            sums.append(lane_sums(wave[m, 0] * imag - wave[m, 1] * real))
        return [value * inverse_total for value in sums]

    def kinetic_sum(band, left_real, left_imag, right_real, right_imag):
        shifted = kin[...] - energy[0, band]
        return lane_sums(shifted * (left_real * right_real + left_imag * right_imag)) * inverse_total

    def send_step(phase, band, resid_real, resid_imag):
        real = pre[...] * resid_real
        imag = pre[...] * resid_imag
        row = [lane_sums(resid_real * real + resid_imag * imag) * inverse_total]
        resid[band, 0] = resid_real
        resid[band, 1] = resid_imag
        ahead[band, 0] = real
        ahead[band, 1] = imag
        send_real(phase, band, real, imag, row)


    partial = [None] * BANDS
    rho = [None] * BANDS
    for band in range(BANDS):
        real, imag = receive_reciprocal(1, band)
        if band == 0:
            same0, same1, cross_real, cross_imag = receive_small(0, 4)
        if band == 0:
            m0_real, m0_imag, m1_real, m1_imag = same0, 0.0 * same0, cross_real, -cross_imag
        else:
            m0_real, m0_imag, m1_real, m1_imag = cross_real, cross_imag, same1, 0.0 * same1
        resid_real = (
            wave[0, 0] * m0_real
            - wave[0, 1] * m0_imag
            + wave[1, 0] * m1_real
            - wave[1, 1] * m1_imag
            - real
        )
        resid_imag = (
            wave[0, 0] * m0_imag
            + wave[0, 1] * m0_real
            + wave[1, 0] * m1_imag
            + wave[1, 1] * m1_real
            - imag
        )
        send_step(2, band, resid_real, resid_imag)


    def finish_curvature(product, values):
        curvature, c0_real, c0_imag, c1_real, c1_imag = values
        curvature = curvature + 2.0 * (
            c0_real * c0_real + c0_imag * c0_imag + c1_real * c1_real + c1_imag * c1_imag
        )
        return product / curvature


    slot = 2 * local

    def turn(which, source, target, all_columns, rows=local):
        here = pl.multiple_of((pool * parts + me) * slot, slot)
        own = here if all_columns else pl.multiple_of(me * slot, slot)
        target[pl.ds(here, rows), :] = source[pl.ds(own, rows), :]

        def start(other, other_pool):
            there = other_pool * parts + other if all_columns else other
            there = pl.multiple_of(there * slot, slot)
            pltpu.make_async_remote_copy(
                src_ref=source.at[pl.ds(there, rows)],
                dst_ref=target.at[pl.ds(here, rows)],
                send_sem=turn_out.at[which],
                recv_sem=turn_in.at[which],
                device_id={"pool": other_pool, "fft": other},
                device_id_type=MESH,
            ).start()

        for_devices(start)

    def wait_turn(which, target, rows=local):
        wait_bytes(target.at[pl.ds(0, rows * (devices - 1))], turn_in.at[which])

    def store_columns(which, columns):
        for m in range(local):
            go_send[which, pl.ds(m, devices, stride=slot), :] = lanes(columns, m)

    for step in range(CG_STEPS):
        last = step + 1 == CG_STEPS
        for band in range(BANDS):
            real, imag = ahead[band, 0], ahead[band, 1]
            sums = [kinetic_sum(band, real, imag, real, imag)] + products(band, real, imag)
            if step > 0:
                cross = kinetic_sum(band, real, imag, search[band, 0], search[band, 1])
            if last and band == 1:
                pl.semaphore_wait(met, pools - 1)
                size_first = finish_curvature(rho[0], receive_small(1, 5))
                store_columns(0, base + size_first * moved)
                turn(0, go_send.at[0], go_recv.at[0], True)
            real, imag = receive_real(2 + 2 * step, band)
            (rho_new,) = bulk_row(2 + 2 * step, band, 1)
            if step > 0:
                beta = rho_new / rho[band]
                before = partial[band]
                sums[0] = sums[0] + beta * (2.0 * cross + beta * before[0])
                for i in range(1, 1 + 2 * BANDS):
                    sums[i] = sums[i] + beta * before[i]
                real = real + beta * space_search[band, 0]
                imag = imag + beta * space_search[band, 1]
            rho[band] = rho_new
            partial[band] = list(sums)
            if not last:
                space_search[band, 0] = real
                space_search[band, 1] = imag
            level = wide(potential)
            image_real = level * real
            image_imag = level * imag
            sums[0] = sums[0] + lane_sums(image_real * real + image_imag * imag)
            if not last:
                send_reciprocal(3 + 2 * step, band, image_real, image_imag, sums)
            overlap[band] = space_wave[band, 0] * real + space_wave[band, 1] * imag
            for c in range(2):
                if step == 0:
                    search[band, c] = ahead[band, c]
                else:
                    search[band, c] = ahead[band, c] + beta * search[band, c]
            if last and band == 0:
                send_small(1, sums)
                base = left_dot(basis_y[0], total[...])
                moved = left_dot(basis_y[0], overlap[band])
        if last:
            break
        for band in range(BANDS):
            pot_real, pot_imag = receive_reciprocal(3 + 2 * step, band)
            values = bulk_row(3 + 2 * step, band, 5)
            _, c0_real, c0_imag, c1_real, c1_imag = values
            size = finish_curvature(rho[band], values)
            shifted = kin[...] - energy[0, band]
            real = search[band, 0]
            imag = search[band, 1]
            image_real = (
                shifted * real
                + pot_real
                + 2.0
                * (
                    wave[0, 0] * c0_real
                    - wave[0, 1] * c0_imag
                    + wave[1, 0] * c1_real
                    - wave[1, 1] * c1_imag
                )
            )
            image_imag = (
                shifted * imag
                + pot_imag
                + 2.0
                * (
                    wave[0, 0] * c0_imag
                    + wave[0, 1] * c0_real
                    + wave[1, 0] * c1_imag
                    + wave[1, 1] * c1_real
                )
            )
            send_step(
                4 + 2 * step,
                band,
                resid[band, 0] - size * image_real,
                resid[band, 1] - size * image_imag,
            )
            added = size * overlap[band]
            total[...] = added if step == 0 and band == 0 else total[...] + added
            for c in range(2):
                moved = size * search[band, c]
                answer[band, c] = moved if step == 0 else answer[band, c] + moved

    store_columns(1, left_dot(basis_y[0], overlap[1]))
    share = jnp.where(lane_id[:1] == 0, rho[1] * (1.0 / parts), 0.0)
    go_send[1, pl.ds(local, devices, stride=slot), :] = jnp.broadcast_to(
        pack(sums + [share]), (devices, n)
    )
    turn(1, go_send.at[1], go_recv.at[1], True, local + 1)

    even = 2 * me
    frequency = jnp.where(
        pool == 0, even, jnp.where(pool == 1, jnp.where(me == 0, n // 2, even), even + 1)
    )

    def plain_square(index):
        k = jnp.where(index > n // 2, index - n // 2, index)
        return (k.astype(f32) * unit) ** 2

    squared = (
        plain_square(index_x) + (frequency.astype(f32) * unit) ** 2 + plain_square(index_z)
    )
    nonzero = (squared > 0).astype(f32)
    coulomb = 4.0 * math.pi * nonzero / (squared + (1.0 - nonzero))

    wait_turn(0, go_recv.at[0])
    wait_turn(1, go_recv.at[1], local + 1)
    gathered = []
    for other in range(pools):
        first = other * parts * slot + local
        rows = go_recv[1, pl.ds(first, parts, stride=slot), :]
        gathered.append(jnp.sum(rows, axis=0, keepdims=True))
    gathered = jnp.concatenate(gathered, axis=0)
    lane = lane_id[:pools]
    terms = jnp.where(lane == 0, gathered, 2.0 * gathered * gathered)
    curvature = jnp.sum(jnp.where(lane < 1 + 2 * BANDS, terms, 0.0), axis=1, keepdims=True)
    product = jnp.sum(jnp.where(lane == 1 + 2 * BANDS, gathered, 0.0), axis=1, keepdims=True)
    quotient = product / curvature
    sizes = [quotient[other : other + 1] for other in range(pools)]
    pieces = []
    for m in range(local):
        piece = None
        for other in range(pools):
            rows = pl.ds(other * parts * slot + m, parts, stride=slot)
            term = go_recv[0, rows, :] + sizes[other] * go_recv[1, rows, :]
            piece = term if piece is None else piece + term
        back_send[0, pl.ds(m, parts, stride=slot), :] = piece
        pieces.append(piece)
    turn(2, back_send.at[0], back_recv.at[0], False)


    field = left_dot(basis_x[...], jnp.concatenate(pieces, axis=0))
    field = coulomb * right_dot(field, basis_z[0])
    field = left_dot(spread_x[...], right_dot(field, basis_z[1]))
    back_send[1] = field
    turn(3, back_send.at[1], back_recv.at[1], False)

    for band in range(BANDS):
        size = size_first
        if band == 1:
            size = sum(jnp.where(pool == i, sizes[i], 0.0) for i in range(pools))
        for c in range(2):
            value = answer[band, c] + size * search[band, c]
            for m in range(local):
                coeff[band, c, pl.ds(m, n, stride=local), :] = lanes(value, m)
    results = [(coeff, coeff_out), (density, density_out), (hxc, hxc_out)]
    stores = [pltpu.make_async_copy(a, b, stored.at[i]) for i, (a, b) in enumerate(results)]
    stores[0].start()
    for phase in range(2 * CG_STEPS + 1):
        for band in range(BANDS):
            for half in range(HALVES):
                wait_bytes(half_bytes(phase, band, half), bulk_out.at[phase, band, half])
    for slot_id in range(2):
        wait_bytes(small_recv.at[slot_id, pl.ds(0, parts - 1)], small_out.at[slot_id])

    for i, result in enumerate((density, hxc)):
        wait_turn(2 + i, back_recv.at[i])
        columns = [back_recv[i, pl.ds(m, devices, stride=slot), :] for m in range(local)]
        whole = left_dot(basis_y[1], jnp.concatenate(columns, axis=1))
        for m in range(local):
            if i == 0:
                result[m] = lanes(whole, m)
            else:
                result[m] = lanes(whole, m) + xc[m] * density[m]
        stores[1 + i].start()


    for store in stores:
        store.wait()
    for which in range(4):
        rows = local + 1 if which == 1 else local
        wait_bytes(go_recv.at[0, pl.ds(0, rows * (devices - 1))], turn_out.at[which])


def hand_over(coeff, density, hxc, coeff_out, density_out, hxc_out, *scratch):
    held, held_density, held_hxc, came, gone = scratch
    moves = [(density, held_density, density_out), (hxc, held_hxc, hxc_out)]
    for b in range(BANDS):
        for c in range(2):
            moves.append((coeff.at[b, c], held.at[b, c], coeff_out.at[b, c]))
    first = [pltpu.make_async_copy(a, h, came.at[i]) for i, (a, h, _) in enumerate(moves)]
    second = [pltpu.make_async_copy(h, o, gone.at[i]) for i, (_, h, o) in enumerate(moves)]
    for copy in first:
        copy.start()
    for copy, onward in zip(first, second):
        copy.wait()
        onward.start()
    for copy in second:
        copy.wait()


def body(wave_coeff, band_energy, local_potential, perturbation, xc_kernel, parts, pools):
    n = wave_coeff.shape[-1]
    local = n // parts
    block = 2 * local * (local // HALVES)
    wide = local * n
    phases = 2 * CG_STEPS + 1
    room = block + 8
    slot_rows = 2 * local * parts
    grid = (4, 4, 2) if parts == 32 else (1, parts // 2, 2)
    operands = [
        wave_coeff.reshape(BANDS, 2, n * local, n),
        local_potential,
        perturbation,
        xc_kernel,
    ] + [jnp.asarray(t) for t in make_tables(n, parts)]
    anywhere = pl.BlockSpec(memory_space=pl.ANY)
    vmem = pl.BlockSpec(memory_space=pltpu.VMEM)
    field = pltpu.VMEM((BANDS, 2, n, wide), f32)
    dma = pltpu.SemaphoreType.DMA
    coeff, density, hxc = pl.pallas_call(
        functools.partial(kernel, n, parts, pools, grid),
        out_shape=(
            jax.ShapeDtypeStruct(operands[0].shape, f32),
            jax.ShapeDtypeStruct((local, n, n), f32),
            jax.ShapeDtypeStruct((local, n, n), f32),
        ),
        in_specs=[anywhere, pl.BlockSpec(memory_space=pltpu.SMEM)] + [anywhere] * 10,
        out_specs=(anywhere, anywhere, anywhere),
        scratch_shapes=[
            pltpu.VMEM(operands[0].shape, f32),
            pltpu.VMEM((local, n, n), f32),
            pltpu.VMEM((local, n, n), f32),
        ]
        + [pltpu.VMEM(t.shape, t.dtype) for t in operands]
        + [
            field,
            pltpu.VMEM((n, wide), f32),
            pltpu.VMEM((n, wide), f32),
            field,
            field,
            field,
            field,
            field,
            field,
            pltpu.VMEM((BANDS, n, wide), f32),
            pltpu.VMEM((n, wide), f32),
            pltpu.VMEM((phases, BANDS, HALVES, parts, room, n), f32),
            pltpu.VMEM((phases, BANDS, HALVES, parts * room, n), f32),
            pltpu.VMEM((2, 1, n), f32),
            pltpu.VMEM((2, parts, 1, n), f32),
            pltpu.VMEM((2, pools * slot_rows, n), f32),
            pltpu.VMEM((2, pools * slot_rows, n), f32),
            pltpu.VMEM((2, slot_rows, n), f32),
            pltpu.VMEM((2, pools * slot_rows, n), f32),
            dma((11,)),
            dma((phases, BANDS, HALVES)),
            dma((phases, BANDS, HALVES)),
            dma((2,)),
            dma((2,)),
            dma((4,)),
            dma((4,)),
            pltpu.SemaphoreType.REGULAR,
            dma((3,)),
        ],
        compiler_params=pltpu.CompilerParams(
            collective_id=0, has_side_effects=True, vmem_limit_bytes=56 * 1024 * 1024
        ),
    )(operands[0], band_energy, *operands[1:])
    results = [coeff, density, hxc]
    coeff, density, hxc = pl.pallas_call(
        hand_over,
        out_shape=[jax.ShapeDtypeStruct(t.shape, f32) for t in results],
        in_specs=[anywhere] * 3,
        out_specs=[anywhere] * 3,
        scratch_shapes=[pltpu.VMEM(t.shape, f32) for t in results]
        + [dma((2 * BANDS + 2,)), dma((2 * BANDS + 2,))],
    )(*results)
    return coeff.reshape(wave_coeff.shape), density, hxc


def solution(mesh):
    return jax.shard_map(
        functools.partial(body, parts=mesh.shape["fft"], pools=mesh.shape["pool"]),
        mesh=mesh,
        in_specs=(
            P("pool", None, None, None, "fft", None),
            P("pool", None),
            P("fft", None, None),
            P("fft", None, None),
            P("fft", None, None),
        ),
        out_specs=(
            P("pool", None, None, None, "fft", None),
            P("fft", None, None),
            P("fft", None, None),
        ),
        check_vma=False,
    )
```
